128 devices in a mesh: ctx: 16 (over x, z_hi, core), fsdp: 8 (over y, z_lo).
Axes of the slice: x: 4, y: 4, z: 4 (z_hi: 2, z_lo: 2; z = z_hi * 2 + z_lo), core: 2. Of those that a mesh axis runs over, the one named last changes fastest.
Arguments:
- tokens: bfloat16 [8, 2048, 960], P('fsdp', 'ctx'), may hold values from -6 to 6
- norm_attn: bfloat16 [960], P('fsdp'), may hold values from 0.099609375 to 1.8984375
- w_query: bfloat16 [960, 960], P('fsdp'), may hold values from -0.1875 to 0.1875
- w_key: bfloat16 [960, 320], P('fsdp'), may hold values from -0.1875 to 0.1875
- w_value: bfloat16 [960, 320], P('fsdp'), may hold values from -0.1875 to 0.1875
- w_out: bfloat16 [960, 960], P('fsdp'), may hold values from -1.5 to 1.5
- norm_ffn: bfloat16 [960], P('fsdp'), may hold values from 0.099609375 to 1.8984375
- w_gate: bfloat16 [960, 2560], P('fsdp'), may hold values from -0.1875 to 0.1875
- w_up: bfloat16 [960, 2560], P('fsdp'), may hold values from -0.1875 to 0.1875
- w_down: bfloat16 [2560, 960], P('fsdp'), may hold values from -0.125 to 0.125
- cotangent: bfloat16 [8, 2048, 960], P('fsdp', 'ctx'), may hold values from -6 to 6
Outputs:
- output: bfloat16 [8, 2048, 960], P('fsdp', 'ctx')
- input_grad: bfloat16 [8, 2048, 960], P('fsdp', 'ctx')
- grad_norm_attn: float32 [960], P('fsdp')
- grad_query: float32 [960, 960], P('fsdp')
- grad_key: float32 [960, 320], P('fsdp')
- grad_value: float32 [960, 320], P('fsdp')
- grad_out: float32 [960, 960], P('fsdp')
- grad_norm_ffn: float32 [960], P('fsdp')
- grad_gate: float32 [960, 2560], P('fsdp')
- grad_up: float32 [960, 2560], P('fsdp')
- grad_down: float32 [2560, 960], P('fsdp')
The draws below stay inside these ranges and needn't reach their ends.
All inputs are finite; a program needn't handle non-finite values.
Results may differ from the reference program's by a relative error of at most 0.03.
Values may be sent and summed in bfloat16 or wider, within the bound.
No kernel may reach another device: no remote copies, remote signals or barrier semaphores. Data moves between devices by JAX's collectives and lax.ppermute only.
A program may use at most 128 MiB of HBM per device.

```python
import jax
import jax.numpy as jnp
from jax import lax

D = 960
HEADS = 15
KV_HEADS = 5
HEAD = 64
FF = 2560
BATCH = 8
LENGTH = 2048
QWIDTH = 960
KVWIDTH = 320


def level_of(key, shape, split, least, top_value):
    def one(position, parts):
        steps = jax.random.uniform(jax.random.fold_in(jax.random.fold_in(key, 6), position), (parts,), jnp.float32, least / len(split), top_value / len(split))
        return jnp.repeat(jnp.exp(steps), shape[position] // parts).reshape((-1,) + (1,) * (len(shape) - position - 1))

    factor_of = one(*split[0])
    for cut in split[1:]:
        factor_of = factor_of * one(*cut)
    return factor_of


def bell_draw(key, extent, deviation, reach, split=(), kind=jnp.bfloat16):
    result = jax.random.normal(key, extent, jnp.float32) * deviation
    if len(split) > 0:
        result = level_of(key, extent, split, -0.22, 0.18) * result
    return jnp.clip(result, min=-reach, max=reach).astype(kind)


def setup_inputs(seed: int = 0) -> dict:
    seeds = jax.random.split(jax.random.key(seed), 12)
    return {
        "tokens": bell_draw(seeds[0], (BATCH, LENGTH, D), 1.0, 6.0, ((0, 8), (1, 16))),
        "norm_attn": jnp.clip(1.0 + 0.18 * jax.random.normal(seeds[1], (D,), jnp.float32), 0.099609375, 1.8984375).astype(jnp.bfloat16),
        "w_query": bell_draw(seeds[2], (D, QWIDTH), D ** -0.5, 0.1875, ((0, 8),)),
        "w_key": bell_draw(seeds[3], (D, KVWIDTH), D ** -0.5, 0.1875, ((0, 8),)),
        "w_value": bell_draw(seeds[4], (D, KVWIDTH), D ** -0.5, 0.1875, ((0, 8),)),
        "w_out": bell_draw(seeds[5], (QWIDTH, D), (max(D // 64, 1)) ** -0.5, 1.5, ((0, 8),)),
        "norm_ffn": jnp.clip(1.0 + 0.18 * jax.random.normal(seeds[6], (D,), jnp.float32), 0.099609375, 1.8984375).astype(jnp.bfloat16),
        "w_gate": bell_draw(seeds[7], (D, FF), D ** -0.5, 0.1875, ((0, 8),)),
        "w_up": bell_draw(seeds[8], (D, FF), D ** -0.5, 0.1875, ((0, 8),)),
        "w_down": bell_draw(seeds[9], (FF, D), FF ** -0.5, 0.125, ((0, 8),)),
        "cotangent": bell_draw(seeds[10], (BATCH, LENGTH, D), 1.0, 6.0, ((0, 8), (1, 16))),
    }


EPSILON = 1e-05
ROPE_BASE = 10000.0
MASK_VALUE = -1e+30
HIGHEST = lax.Precision.HIGHEST

@jax.custom_vjp
def low(v):
    return lax.optimization_barrier(v.astype(jnp.bfloat16)).astype(jnp.float32)

@jax.custom_vjp
def low_back(v):
    return v

def low_keep(v):
    return (low(v), None)

def low_pass(kept, grad):
    return (grad,)

def back_keep(v):
    return (v, None)

def back_low(kept, grad):
    return (low(grad),)
low.defvjp(low_keep, low_pass)
low_back.defvjp(back_keep, back_low)

def rope_tables(positions):
    half_size = HEAD // 2
    inverse = ROPE_BASE ** (-(jnp.arange(half_size, dtype=jnp.float32) * 2.0 / HEAD))
    angles = positions[:, None] * inverse[None, :]
    return (jnp.cos(angles), jnp.sin(angles))

def rotate(values, cosine, sine_table):
    half_size = values.shape[-1] // 2
    first_half = values[..., :half_size]
    second_half = values[..., half_size:]
    cos_rows = cosine[:, None, :]
    sin_rows = sine_table[:, None, :]
    return jnp.concatenate([first_half * cos_rows - second_half * sin_rows, second_half * cos_rows + first_half * sin_rows], axis=-1)

def rms_norm(values, gain_vec):
    inverse = lax.rsqrt(lax.optimization_barrier(jnp.mean(values * values, axis=-1, keepdims=True)) + EPSILON)
    return values * inverse * gain_vec

def matmul(left_side, right_side):
    return jnp.dot(left_side, right_side, precision=HIGHEST, preferred_element_type=jnp.float32)

def attend(queries, keys, values):
    block_size = min(512, LENGTH)
    group_size = HEADS // KV_HEADS
    grouped = queries.reshape(LENGTH // block_size, block_size, KV_HEADS, group_size, HEAD)
    starts = jnp.arange(LENGTH // block_size, dtype=jnp.int32) * block_size
    key_pos = jnp.arange(LENGTH, dtype=jnp.int32)

    def one_block(inputs_pair):
        query_part, first_row = inputs_pair
        scores = jnp.einsum('rkgd,jkd->kgrj', query_part, keys, precision=HIGHEST) * HEAD ** (-0.5)
        scores = low_back(scores)
        query_pos = first_row + jnp.arange(block_size, dtype=jnp.int32)
        allowed = key_pos[None, :] <= query_pos[:, None]
        scores = jnp.where(allowed, scores, MASK_VALUE)
        probs = low(jax.nn.softmax(scores, axis=-1))
        return jnp.einsum('kgrj,jkd->rkgd', probs, values, precision=HIGHEST)
    blocks = lax.map(jax.checkpoint(one_block), (grouped, starts))
    return blocks.reshape(LENGTH, HEADS * HEAD)

def block_layer(inputs, gain_one, w_query, w_key, w_value, w_out, gain_two, w_gate, w_up, w_down):
    positions = jnp.arange(LENGTH, dtype=jnp.float32)
    cosine, sine_table = rope_tables(positions)

    def one_sequence(sequence):
        act_one = low(rms_norm(sequence, gain_one))
        queries = low(rotate(low_back(matmul(act_one, w_query)).reshape(LENGTH, HEADS, HEAD), cosine, sine_table))
        keys = low(rotate(low_back(matmul(act_one, w_key)).reshape(LENGTH, KV_HEADS, HEAD), cosine, sine_table))
        values = low(low_back(matmul(act_one, w_value))).reshape(LENGTH, KV_HEADS, HEAD)
        attn = low(low_back(attend(queries, keys, values)))
        hidden = sequence + low_back(matmul(attn, w_out))
        act_two = low(rms_norm(hidden, gain_two))
        gate = low_back(matmul(act_two, w_gate))
        upward = low_back(matmul(act_two, w_up))
        inner = low(jax.nn.silu(gate) * upward)
        return hidden + low_back(matmul(inner, w_down))
    return lax.map(one_sequence, inputs)

def reference(tokens, norm_attn, w_query, w_key, w_value, w_out, norm_ffn, w_gate, w_up, w_down, cotangent):
    output, pullback = jax.vjp(block_layer, tokens.astype(jnp.float32), norm_attn.astype(jnp.float32), w_query.astype(jnp.float32), w_key.astype(jnp.float32), w_value.astype(jnp.float32), w_out.astype(jnp.float32), norm_ffn.astype(jnp.float32), w_gate.astype(jnp.float32), w_up.astype(jnp.float32), w_down.astype(jnp.float32))
    grads = pullback(cotangent.astype(jnp.float32))
    return (output.astype(jnp.bfloat16), grads[0].astype(jnp.bfloat16), grads[1], grads[2], grads[3], grads[4], grads[5], grads[6], grads[7], grads[8], grads[9])
```

```python
import functools

import jax
import jax.numpy as jnp
from jax import lax
from jax.experimental import pallas as pl
from jax.experimental.pallas import tpu as pltpu
from jax.sharding import PartitionSpec as P

HEADS = 15
KV_HEADS = 5
GROUP = HEADS // KV_HEADS
HEAD = 64
QWIDTH = HEADS * HEAD
KVWIDTH = KV_HEADS * HEAD

EPSILON = 1e-05
ROPE_BASE = 10000.0
MASK_VALUE = -1e30
SCALE = HEAD ** (-0.5)

BF16 = jnp.bfloat16
F32 = jnp.float32
VMEM_LIMIT = 48 * 1024 * 1024

FSDP_STEPS = [(dy, dz) for dy in range(4) for dz in range(2)]
CTX_STEPS = [(dx, dz) for dx in range(4) for dz in range(2)]


def fsdp_move(index, dy, dz):
    return ((index // 2 + dy) % 4) * 2 + (index % 2 + dz) % 2


def fsdp_from(value, step):
    pairs = [(i, fsdp_move(i, -step[0], step[1])) for i in range(8)]
    return lax.ppermute(value, "fsdp", pairs)


def ctx_move(index, dx, dz):
    return ((index // 4 + dx) % 4) * 4 + ((index // 2 + dz) % 2) * 2 + index % 2


def earlier_pairs(step):
    pairs = [(i, ctx_move(i, *step)) for i in range(16) if i // 4 + step[0] < 4]
    return [(i, j) for i, j in pairs if i // 2 < j // 2]


def core_swap(value):
    return lax.ppermute(value, "ctx", [(i, i ^ 1) for i in range(16)])


def gather_blocks(value):
    return [value] + [fsdp_from(value, step) for step in FSDP_STEPS[1:]]


def exchange_blocks(blocks, me):
    received = []
    for dy, dz in FSDP_STEPS:
        part = lax.dynamic_index_in_dim(blocks, fsdp_move(me, -dy, dz), 0, keepdims=False)
        received.append(part if (dy, dz) == (0, 0) else fsdp_from(part, (dy, dz)))
    return received


def place_kernel(where_ref, *refs):
    blocks, out_ref = refs[:-1], refs[-1]
    for r, block in enumerate(blocks):
        out_ref[where_ref[r]] = block[...]


def place(blocks, where):
    shape = blocks[0].shape
    return pl.pallas_call(
        place_kernel,
        out_shape=jax.ShapeDtypeStruct((len(blocks),) + shape, blocks[0].dtype),
        in_specs=[pl.BlockSpec(memory_space=pltpu.SMEM)]
        + [pl.BlockSpec(memory_space=pltpu.VMEM)] * len(blocks),
        out_specs=pl.BlockSpec(memory_space=pltpu.VMEM),
        compiler_params=pltpu.CompilerParams(vmem_limit_bytes=VMEM_LIMIT),
        name="place",
    )(where, *blocks)


def place_pair_kernel(where_ref, *refs):
    ours, theirs, out_ref = refs[:8], refs[8:16], refs[16]
    core = where_ref[8]
    rows = out_ref.shape[2]
    for r in range(8):
        out_ref[core, where_ref[r]] = ours[r][:rows]
        out_ref[1 - core, where_ref[r]] = theirs[r][:rows]
    if len(refs) > 17:
        for r in range(8):
            refs[17][where_ref[r]] = ours[r][112:128, :128].astype(F32)[8:]


def place_pair(ours, theirs, where, rows, gains):
    columns = ours[0].shape[1]
    out_shape = [jax.ShapeDtypeStruct((2, 8, rows, columns), BF16)]
    if gains:
        out_shape.append(jax.ShapeDtypeStruct((8, 8, 128), F32))
    return pl.pallas_call(
        place_pair_kernel,
        out_shape=out_shape,
        in_specs=[pl.BlockSpec(memory_space=pltpu.SMEM)]
        + [pl.BlockSpec(memory_space=pltpu.VMEM)] * 16,
        out_specs=[pl.BlockSpec(memory_space=pltpu.VMEM)] * len(out_shape),
        compiler_params=pltpu.CompilerParams(vmem_limit_bytes=VMEM_LIMIT),
        name="place_pair",
    )(where, *ours, *theirs)


def contract(left, right, left_dim, right_dim):
    return lax.dot_general(
        left, right, (((left_dim,), (right_dim,)), ((), ())), preferred_element_type=F32
    )


def lanes_of_group(ref, h):
    return jnp.concatenate(
        [ref[(GROUP * h + g) * HEAD : (GROUP * h + g + 1) * HEAD, :] for g in range(GROUP)], axis=1
    )


def causal(rows):
    key = lax.broadcasted_iota(jnp.int32, (rows, GROUP * rows), 0)
    query = lax.broadcasted_iota(jnp.int32, (rows, GROUP * rows), 1) % rows
    return key <= query


def attend_kernel(order_ref, q_ref, *refs):
    blocks = refs[:16]
    out_ref, log_ref, kv_s, q_s, acc_s, max_s, sum_s = refs[16:]
    rows = q_ref.shape[1]
    for j in range(16):
        kv_s[j] = blocks[j][...]
    for h in range(KV_HEADS):
        q_s[h] = lanes_of_group(q_ref, h) * BF16(SCALE)

    def scores_of(j, h):
        keys = kv_s[j, h * HEAD : (h + 1) * HEAD, :]
        return contract(keys, q_s[h], 0, 0)

    def values_of(j, h):
        return kv_s[j, KVWIDTH + h * HEAD : KVWIDTH + (h + 1) * HEAD, :]

    allowed = causal(rows)
    for h in range(KV_HEADS):
        scores = jnp.where(allowed, scores_of(0, h), MASK_VALUE)
        top = jnp.max(scores, axis=0, keepdims=True)
        weights = jnp.exp(scores - top)
        max_s[h] = top
        sum_s[h] = jnp.sum(weights, axis=0, keepdims=True)
        acc_s[h] = contract(values_of(0, h), weights.astype(BF16), 1, 0)

    def step(i, carry):
        j = order_ref[i]
        for h in range(KV_HEADS):
            scores = scores_of(j, h)
            old = max_s[h]
            top = jnp.maximum(old, jnp.max(scores, axis=0, keepdims=True))
            weights = jnp.exp(scores - top)
            factor = jnp.exp(old - top)
            max_s[h] = top
            sum_s[h] = sum_s[h] * factor + jnp.sum(weights, axis=0, keepdims=True)
            acc_s[h] = acc_s[h] * factor + contract(values_of(j, h), weights.astype(BF16), 1, 0)
        return carry

    lax.fori_loop(1, order_ref[16], step, 0)
    for h in range(KV_HEADS):
        result = acc_s[h] / sum_s[h]
        logs = max_s[h] + jnp.log(sum_s[h])
        for g in range(GROUP):
            head = GROUP * h + g
            out_ref[head * HEAD : (head + 1) * HEAD, :] = result[:, g * rows : (g + 1) * rows]
            log_ref[head : head + 1, :] = logs[:, g * rows : (g + 1) * rows]


def attend(order, queries, blocks):
    rows = queries.shape[1]
    return pl.pallas_call(
        attend_kernel,
        out_shape=[
            jax.ShapeDtypeStruct((QWIDTH, rows), F32),
            jax.ShapeDtypeStruct((HEADS, rows), F32),
        ],
        in_specs=[pl.BlockSpec(memory_space=pltpu.SMEM)]
        + [pl.BlockSpec(memory_space=pltpu.VMEM)] * 17,
        out_specs=[pl.BlockSpec(memory_space=pltpu.VMEM)] * 2,
        scratch_shapes=[
            pltpu.VMEM((16, 2 * KVWIDTH, rows), BF16),
            pltpu.VMEM((KV_HEADS, HEAD, GROUP * rows), BF16),
            pltpu.VMEM((KV_HEADS, HEAD, GROUP * rows), F32),
            pltpu.VMEM((KV_HEADS, 1, GROUP * rows), F32),
            pltpu.VMEM((KV_HEADS, 1, GROUP * rows), F32),
        ],
        compiler_params=pltpu.CompilerParams(vmem_limit_bytes=VMEM_LIMIT),
        name="attend",
    )(order, queries, *blocks)


def attend_back_kernel(order_ref, q_ref, g_ref, out_ref, log_ref, *refs):
    blocks = refs[:16]
    gq_ref, ours_ref, theirs_ref, kv_s, q_s, g_s, gq_s, log_s, delta_s, gkv_s = refs[16:]
    rows = q_ref.shape[1]
    for j in range(16):
        kv_s[j] = blocks[j][...]
        gkv_s[j] = jnp.zeros(gkv_s.shape[1:], BF16)
    for h in range(KV_HEADS):
        q_s[h] = lanes_of_group(q_ref, h) * BF16(SCALE)
        grads = lanes_of_group(g_ref, h)
        g_s[h] = grads
        delta_s[h] = jnp.sum(
            grads.astype(F32) * lanes_of_group(out_ref, h), axis=0, keepdims=True
        )
        log_s[h] = jnp.concatenate(
            [log_ref[GROUP * h + g : GROUP * h + g + 1, :] for g in range(GROUP)], axis=1
        )

    def absorb(j, h, allowed):
        keys = kv_s[j, h * HEAD : (h + 1) * HEAD, :]
        values = kv_s[j, KVWIDTH + h * HEAD : KVWIDTH + (h + 1) * HEAD, :]
        probs = jnp.exp(contract(keys, q_s[h], 0, 0) - log_s[h])
        if allowed is not None:
            probs = jnp.where(allowed, probs, 0.0)
        g_probs = contract(values, g_s[h], 0, 0)
        g_scores = (probs * (g_probs - delta_s[h])).astype(BF16)
        gkv_s[j, h * HEAD : (h + 1) * HEAD, :] = contract(q_s[h], g_scores, 1, 1).astype(BF16)
        gkv_s[j, KVWIDTH + h * HEAD : KVWIDTH + (h + 1) * HEAD, :] = contract(
            g_s[h], probs.astype(BF16), 1, 1
        ).astype(BF16)
        return contract(keys, g_scores, 1, 0)

    allowed = causal(rows)
    for h in range(KV_HEADS):
        gq_s[h] = absorb(0, h, allowed)

    def step(i, carry):
        j = order_ref[i]
        for h in range(KV_HEADS):
            gq_s[h] += absorb(j, h, None)
        return carry

    lax.fori_loop(1, order_ref[16], step, 0)
    for h in range(KV_HEADS):
        result = gq_s[h] * SCALE
        for g in range(GROUP):
            head = GROUP * h + g
            gq_ref[head * HEAD : (head + 1) * HEAD, :] = result[:, g * rows : (g + 1) * rows]
    for k in range(8):
        ours_ref[k] = gkv_s[2 * k]
        theirs_ref[k] = gkv_s[2 * k + 1]


def attend_back(order, queries, grads, result, logs, blocks):
    rows = queries.shape[1]
    half = jax.ShapeDtypeStruct((8, 2 * KVWIDTH, rows), BF16)
    wide = (KV_HEADS, HEAD, GROUP * rows)
    return pl.pallas_call(
        attend_back_kernel,
        out_shape=[jax.ShapeDtypeStruct((QWIDTH, rows), F32), half, half],
        in_specs=[pl.BlockSpec(memory_space=pltpu.SMEM)]
        + [pl.BlockSpec(memory_space=pltpu.VMEM)] * 20,
        out_specs=[pl.BlockSpec(memory_space=pltpu.VMEM)] * 3,
        scratch_shapes=[
            pltpu.VMEM((16, 2 * KVWIDTH, rows), BF16),
            pltpu.VMEM(wide, BF16),
            pltpu.VMEM(wide, BF16),
            pltpu.VMEM(wide, F32),
            pltpu.VMEM((KV_HEADS, 1, GROUP * rows), F32),
            pltpu.VMEM((KV_HEADS, 1, GROUP * rows), F32),
            pltpu.VMEM((16, 2 * KVWIDTH, rows), BF16),
        ],
        compiler_params=pltpu.CompilerParams(vmem_limit_bytes=VMEM_LIMIT),
        name="attend_back",
    )(order, queries, grads, result, logs, *blocks)


def turn(heads, cosine, sine, sign):
    parts = heads.reshape(-1, 2, HEAD // 2, heads.shape[-1])
    first, second = parts[:, 0], parts[:, 1]
    sine = sign * sine
    return jnp.stack(
        [first * cosine - second * sine, second * cosine + first * sine], axis=1
    ).reshape(heads.shape)


def norm_back(grad, normed, inverse, gain):
    scaled = grad * gain
    mean = jnp.mean(scaled * normed, axis=-1, keepdims=True)
    return inverse * (scaled - normed * mean), jnp.sum(grad * normed, axis=0)


def body(
    tokens, norm_attn, w_query, w_key, w_value, w_out, norm_ffn, w_gate, w_up, w_down, cotangent
):
    rows, width = tokens.shape[1:]
    part = norm_attn.shape[0]
    ff_part = w_down.shape[0]
    ctx = lax.axis_index("ctx")
    me = lax.axis_index("fsdp")
    core = ctx % 2
    chip = ctx // 2
    first = core == 0
    inputs = tokens.reshape(rows, width).astype(F32)
    cot = cotangent.reshape(rows, width)
    ahead = [fsdp_move(me, dy, dz) for dy, dz in FSDP_STEPS]
    where = jnp.stack(ahead + [core]).astype(jnp.int32)

    half = jnp.where(
        first,
        jnp.concatenate([w_query, w_key], axis=1),
        jnp.concatenate([w_out, w_value], axis=1),
    )
    gain_rows = jnp.zeros((8, half.shape[1]), BF16)
    gain_rows = gain_rows.at[0, :part].set(norm_attn).at[1, :part].set(norm_ffn)
    ours = gather_blocks(jnp.concatenate([half, gain_rows], axis=0))
    theirs = [core_swap(block) for block in ours]
    attn_weights, gains = place_pair(ours, theirs, where, part, True)
    full_qk = attn_weights[0].reshape(width, QWIDTH + KVWIDTH)
    full_ov = attn_weights[1].reshape(width, width + KVWIDTH)
    gain_one = gains[:, 0, :part].reshape(1, width)
    gain_two = gains[:, 1, :part].reshape(1, width)

    ff_half = jnp.where(first, w_gate, w_up).reshape(part, 8, ff_part).transpose(1, 0, 2)
    ours = exchange_blocks(ff_half, me)
    theirs = [core_swap(block) for block in ours]
    ff_weights = place_pair(ours, theirs, where, part, False)[0]
    gate_cols = ff_weights[0].reshape(width, ff_part)
    up_cols = ff_weights[1].reshape(width, ff_part)

    inverse_one = lax.rsqrt(jnp.mean(inputs * inputs, axis=-1, keepdims=True) + EPSILON)
    normed_one = inputs * inverse_one
    act_one = (normed_one * gain_one).astype(BF16)
    inverse_freq = ROPE_BASE ** (-(jnp.arange(HEAD // 2, dtype=F32) * 2.0 / HEAD))
    positions = (ctx * rows + jnp.arange(rows, dtype=jnp.int32)).astype(F32)
    angles = inverse_freq[:, None] * positions[None, :]
    cosine, sine = jnp.cos(angles), jnp.sin(angles)
    rotated = turn(contract(full_qk, act_one, 0, 1), cosine, sine, 1.0).astype(BF16)
    values = contract(full_ov, act_one, 0, 1)[width:].astype(BF16)
    queries = rotated[:QWIDTH]
    local_kv = jnp.concatenate([rotated[QWIDTH:], values], axis=0)
    same = [local_kv]
    for step in CTX_STEPS[1:]:
        same.append(lax.ppermute(local_kv, "ctx", earlier_pairs(step)))
    blocks = []
    for block in same:
        blocks += [block, core_swap(block)]
    x, z_hi = chip // 2, chip % 2
    valid = [jnp.bool_(True), core == 1]
    for dx, dz in CTX_STEPS[1:]:
        z_from = (z_hi + dz) % 2
        here = jnp.logical_and(x >= dx, (x - dx) * 2 + z_from < chip)
        valid += [here, here]
    valid = jnp.stack(valid)
    order = jnp.argsort(jnp.logical_not(valid), stable=True).astype(jnp.int32)
    order = jnp.concatenate([order, jnp.sum(valid.astype(jnp.int32))[None]])
    result, logs = attend(order, queries, blocks)
    attn = result.astype(BF16)
    hidden = inputs + contract(attn, full_ov[:, :width], 0, 0)

    inverse_two = lax.rsqrt(jnp.mean(hidden * hidden, axis=-1, keepdims=True) + EPSILON)
    normed_two = hidden * inverse_two
    act_two = (normed_two * gain_two).astype(BF16)
    every = 8 * rows
    act_all = place(gather_blocks(act_two), where).reshape(every, width)
    cot_all = lax.all_gather(cot, "fsdp", axis=0, tiled=True)
    g_inner = contract(cot_all, w_down, 1, 1)
    gate = contract(act_all, gate_cols, 1, 0)
    up = contract(act_all, up_cols, 1, 0)
    sigmoid = jax.nn.sigmoid(gate)
    silu = gate * sigmoid
    inner = (silu * up).astype(BF16)
    g_gate = (g_inner * up * sigmoid * (1.0 + gate * (1.0 - sigmoid))).astype(BF16)
    g_up = (g_inner * silu).astype(BF16)
    g_act_part = contract(g_gate, gate_cols, 1, 1) + contract(g_up, up_cols, 1, 1)
    g_act_parts = exchange_blocks(g_act_part.astype(BF16).reshape(8, rows, width), me)
    g_act_two = sum(block.astype(F32) for block in g_act_parts)
    down_part = contract(inner, w_down, 1, 0).astype(BF16)
    down = lax.psum_scatter(down_part, "fsdp", scatter_dimension=0, tiled=True)
    output = (hidden + down.astype(F32)).astype(BF16)
    grad_gate_cols = contract(act_all, g_gate, 0, 0)
    grad_up_cols = contract(act_all, g_up, 0, 0)
    grad_ff_cols = jnp.concatenate([grad_gate_cols, grad_up_cols], axis=1).astype(BF16)
    grad_ff_rows = place(exchange_blocks(grad_ff_cols.reshape(8, part, 2 * ff_part), me), where)
    grad_down = contract(inner, cot_all, 0, 0).astype(BF16)
    grad_ff_rows = lax.psum(grad_ff_rows, "ctx")
    grad_down = lax.psum(grad_down, "ctx").astype(F32)
    grad_gate = grad_ff_rows[..., :ff_part].transpose(1, 0, 2).reshape(part, -1).astype(F32)
    grad_up = grad_ff_rows[..., ff_part:].transpose(1, 0, 2).reshape(part, -1).astype(F32)

    g_normed, gain_two_term = norm_back(g_act_two, normed_two, inverse_two, gain_two)
    g_hidden = cot.astype(F32) + g_normed
    g_hid = g_hidden.astype(BF16)
    g_attn = contract(full_ov[:, :width], g_hid, 1, 1).astype(BF16)
    attn_rows = place(exchange_blocks(attn.reshape(8, part, rows), me), where)
    attn_rows = attn_rows.transpose(1, 0, 2).reshape(part, every)
    g_hid_all = lax.all_gather(g_hid, "fsdp", axis=0, tiled=True)
    grad_out = lax.psum(contract(attn_rows, g_hid_all, 1, 0).astype(BF16), "ctx").astype(F32)

    g_query_rot, g_ours, g_theirs = attend_back(order, queries, g_attn, result, logs, blocks)
    g_pairs = g_ours.astype(F32) + core_swap(g_theirs).astype(F32)
    g_kv = g_pairs[0]
    for k in range(1, 8):
        back = [(j, i) for i, j in earlier_pairs(CTX_STEPS[k])]
        g_kv = g_kv + lax.ppermute(g_pairs[k].astype(BF16), "ctx", back).astype(F32)
    g_qkv = jnp.concatenate(
        [
            turn(g_query_rot, cosine, sine, -1.0),
            turn(g_kv[:KVWIDTH], cosine, sine, -1.0),
            g_kv[KVWIDTH:],
        ],
        axis=0,
    ).astype(BF16)
    g_act_one = contract(g_qkv[: QWIDTH + KVWIDTH], full_qk, 0, 1) + contract(
        g_qkv[QWIDTH + KVWIDTH :], full_ov[:, width:], 0, 1
    )
    g_inputs, gain_one_term = norm_back(g_act_one, normed_one, inverse_one, gain_one)
    input_grad = (g_hidden + g_inputs).astype(BF16)

    columns = g_qkv.shape[0] // 8
    act_one_all = lax.all_gather(act_one, "fsdp", axis=0, tiled=True)
    g_cols = place(exchange_blocks(g_qkv.reshape(8, columns, rows), me), where)
    g_cols = g_cols.transpose(1, 0, 2).reshape(columns, every)
    grad_cols = contract(act_one_all, g_cols, 0, 1)
    gain_terms = jnp.stack([gain_one_term, gain_two_term], axis=1)
    grad_cols = jnp.concatenate([grad_cols, gain_terms], axis=1).astype(BF16)
    grad_rows = place(exchange_blocks(grad_cols.reshape(8, part, columns + 2), me), where)
    grad_gains = jnp.sum(grad_rows[..., columns:].astype(F32), axis=0).astype(BF16)
    grad_rows = grad_rows[..., :columns].transpose(1, 0, 2).reshape(part, -1)
    grad_rows = jnp.concatenate([grad_rows, grad_gains], axis=1)
    grad_rows = lax.psum(grad_rows, "ctx").astype(F32)
    return (
        output[None],
        input_grad[None],
        grad_rows[:, 8 * columns],
        grad_rows[:, :QWIDTH],
        grad_rows[:, QWIDTH : QWIDTH + KVWIDTH],
        grad_rows[:, QWIDTH + KVWIDTH : 8 * columns],
        grad_out,
        grad_rows[:, 8 * columns + 1],
        grad_gate,
        grad_up,
        grad_down,
    )


def solution(mesh):
    rows = P("fsdp", None)
    tokens = P("fsdp", "ctx", None)
    in_specs = (
        tokens,
        P("fsdp"),
        rows,
        rows,
        rows,
        rows,
        P("fsdp"),
        rows,
        rows,
        rows,
        tokens,
    )
    out_specs = (
        tokens,
        tokens,
        P("fsdp"),
        rows,
        rows,
        rows,
        rows,
        P("fsdp"),
        rows,
        rows,
        rows,
    )
    return jax.shard_map(body, mesh=mesh, in_specs=in_specs, out_specs=out_specs, check_vma=False)
```

```python
import functools

import jax
import jax.numpy as jnp
from jax import lax
from jax.experimental import pallas as pl
from jax.experimental.pallas import tpu as pltpu
from jax.sharding import PartitionSpec as P

HEADS = 15
KV_HEADS = 5
GROUP = HEADS // KV_HEADS
HEAD = 64
QWIDTH = HEADS * HEAD
KVWIDTH = KV_HEADS * HEAD

EPSILON = 1e-05
ROPE_BASE = 10000.0
MASK_VALUE = -1e30
SCALE = HEAD ** (-0.5)

BF16 = jnp.bfloat16
F32 = jnp.float32
VMEM_LIMIT = 48 * 1024 * 1024

STEPS = [(ring, pair) for ring in range(4) for pair in range(2)]


def moved(index, axis, ring, pair):
    low = 1 if axis == "fsdp" else 2
    core = index % low
    place = index // low
    place = ((place // 2 + ring) % 4) * 2 + (place % 2 + pair) % 2
    return place * low + core


def take(value, axis, ring, pair):
    size = 8 if axis == "fsdp" else 16
    return lax.ppermute(
        value, axis, [(i, moved(i, axis, -ring, pair)) for i in range(size)]
    )


def core_swap(value):
    return lax.ppermute(value, "ctx", [(i, i ^ 1) for i in range(16)])


def gather_blocks(value, axis):
    found = {(0, 0): value, (0, 1): take(value, axis, 0, 1)}
    found[1, 0] = take(value, axis, 1, 0)
    found[3, 0] = take(value, axis, 3, 0)
    found[1, 1] = take(found[0, 1], axis, 1, 0)
    found[3, 1] = take(found[0, 1], axis, 3, 0)
    found[2, 0] = take(found[1, 0], axis, 1, 0)
    found[2, 1] = take(found[3, 1], axis, 3, 0)
    return [found[step] for step in STEPS]


def reduce_blocks(blocks, axis, me):
    term = {
        step: lax.dynamic_index_in_dim(blocks, moved(me, "fsdp", *step), 0, keepdims=False)
        for step in STEPS
    }

    def plus(first, *others):
        return sum((other.astype(F32) for other in others), first.astype(F32))

    one = plus(term[1, 0], take(term[2, 0], axis, 3, 0)).astype(BF16)
    three = plus(term[3, 1], take(term[2, 1], axis, 1, 0)).astype(BF16)
    pair = plus(term[0, 1], take(term[1, 1], axis, 3, 0), take(three, axis, 1, 0)).astype(BF16)
    return plus(
        term[0, 0], take(term[3, 0], axis, 1, 0), take(one, axis, 3, 0), take(pair, axis, 0, 1)
    )


def exchange_blocks(blocks, me):
    received = []
    for step in STEPS:
        goal = moved(me, "fsdp", -step[0], step[1])
        part = lax.dynamic_index_in_dim(blocks, goal, 0, keepdims=False)
        received.append(part if step == (0, 0) else take(part, "fsdp", *step))
    return received


def later(value, ring):
    pairs = [(i, i + 4 * ring) for i in range(16 - 4 * ring)]
    return lax.ppermute(value, "ctx", pairs)


def sooner(value, ring):
    pairs = [(i, i - 4 * ring) for i in range(4 * ring, 16)]
    return lax.ppermute(value, "ctx", pairs)


def gather_earlier(value):
    found = {(0, 0): value, (1, 0): later(value, 1)}
    found[0, 1] = take(value, "ctx", 0, 1)
    found[1, 1] = later(found[0, 1], 1)
    for p in range(2):
        found[3, p] = later(found[0, p], 3)
        found[2, p] = later(found[1, p], 1)
    return [found[step] for step in STEPS]


def reduce_earlier(terms):
    term = dict(zip(STEPS, terms))
    home = []
    for p in (1, 0):
        one = term[1, p] + sooner(term[2, p].astype(BF16), 1).astype(F32)
        total = term[0, p] + sooner(term[3, p].astype(BF16), 3).astype(F32)
        home.append(total + sooner(one.astype(BF16), 1).astype(F32))
    return home[1] + take(home[0].astype(BF16), "ctx", 0, 1).astype(F32)


def place_kernel(where_ref, *refs):
    blocks, out_ref = refs[:-1], refs[-1]
    for r, block in enumerate(blocks):
        out_ref[where_ref[r]] = block[...]


def place(blocks, where):
    shape = blocks[0].shape
    return pl.pallas_call(
        place_kernel,
        out_shape=jax.ShapeDtypeStruct((len(blocks),) + shape, blocks[0].dtype),
        in_specs=[pl.BlockSpec(memory_space=pltpu.SMEM)]
        + [pl.BlockSpec(memory_space=pltpu.VMEM)] * len(blocks),
        out_specs=pl.BlockSpec(memory_space=pltpu.VMEM),
        compiler_params=pltpu.CompilerParams(vmem_limit_bytes=VMEM_LIMIT),
        name="place",
    )(where, *blocks)


def place_pair_kernel(where_ref, *refs):
    ours, theirs, zero_ref, one_ref = refs[:8], refs[8:16], refs[16], refs[17]

    @pl.when(where_ref[8] == 0)
    def _():
        for r in range(8):
            zero_ref[where_ref[r]] = ours[r][...]
            one_ref[where_ref[r]] = theirs[r][...]

    @pl.when(where_ref[8] == 1)
    def _():
        for r in range(8):
            zero_ref[where_ref[r]] = theirs[r][...]
            one_ref[where_ref[r]] = ours[r][...]


def place_pair(ours, theirs, where):
    shape = (8,) + ours[0].shape
    return pl.pallas_call(
        place_pair_kernel,
        out_shape=[jax.ShapeDtypeStruct(shape, BF16)] * 2,
        in_specs=[pl.BlockSpec(memory_space=pltpu.SMEM)]
        + [pl.BlockSpec(memory_space=pltpu.VMEM)] * 16,
        out_specs=[pl.BlockSpec(memory_space=pltpu.VMEM)] * 2,
        compiler_params=pltpu.CompilerParams(vmem_limit_bytes=VMEM_LIMIT),
        name="place_pair",
    )(where, *ours, *theirs)


def spread(value):
    rows = value.shape[0]
    groups = value.reshape(rows, 8, -1)
    return jnp.pad(groups, ((0, 0), (0, 0), (0, 128 - groups.shape[2]))).reshape(rows, 1024)


def unspread(value, part):
    rows = value.shape[0]
    return value.reshape(rows, 8, 128)[:, :, :part].reshape(rows, 8 * part)


def spread_rows(value, part):
    groups = value.reshape(8, part, -1)
    return jnp.pad(groups, ((0, 0), (0, 128 - part), (0, 0))).reshape(1024, -1)


def unspread_rows(value, part):
    return value.reshape(8, 128, -1)[:, :part].reshape(8 * part, -1)


def contract(left, right, left_dim, right_dim):
    return lax.dot_general(
        left, right, (((left_dim,), (right_dim,)), ((), ())), preferred_element_type=F32
    )


def lanes_of_group(ref, h):
    return jnp.concatenate(
        [ref[(GROUP * h + g) * HEAD : (GROUP * h + g + 1) * HEAD, :] for g in range(GROUP)], axis=1
    )


def causal(rows):
    key = lax.broadcasted_iota(jnp.int32, (rows, GROUP * rows), 0)
    query = lax.broadcasted_iota(jnp.int32, (rows, GROUP * rows), 1) % rows
    return key <= query


def present(ctx, j):
    x, z_hi, core = ctx // 4, (ctx // 2) % 2, ctx % 2
    ring, pair = j // 4, (j // 2) % 2
    z_from = (z_hi + pair) % 2
    earlier = jnp.logical_or(ring > 0, z_from < z_hi)
    sibling = jnp.logical_and(j == 1, core == 1)
    return jnp.logical_or(jnp.logical_and(x >= ring, earlier), sibling)


def attend_kernel(ctx_ref, q_ref, *refs):
    blocks = refs[:16]
    out_ref, log_ref, kv_s, q_s, acc_s, max_s, sum_s = refs[16:]
    rows = q_ref.shape[1]
    for j in range(16):
        kv_s[j] = blocks[j][...]
    for h in range(KV_HEADS):
        q_s[h] = lanes_of_group(q_ref, h) * BF16(SCALE)

    def scores_of(j, h):
        keys = kv_s[j, h * HEAD : (h + 1) * HEAD, :]
        return contract(keys, q_s[h], 0, 0)

    def values_of(j, h):
        return kv_s[j, KVWIDTH + h * HEAD : KVWIDTH + (h + 1) * HEAD, :]

    allowed = causal(rows)
    for h in range(KV_HEADS):
        scores = jnp.where(allowed, scores_of(0, h), MASK_VALUE)
        top = jnp.max(scores, axis=0, keepdims=True)
        weights = jnp.exp(scores - top)
        max_s[h] = top
        sum_s[h] = jnp.sum(weights, axis=0, keepdims=True)
        acc_s[h] = contract(values_of(0, h), weights.astype(BF16), 1, 0)

    def step(j, carry):
        pl.when(present(ctx_ref[0], j))(functools.partial(absorb, j))
        return carry

    def absorb(j):
        for h in range(KV_HEADS):
            scores = scores_of(j, h)
            old = max_s[h]
            top = jnp.maximum(old, jnp.max(scores, axis=0, keepdims=True))
            weights = jnp.exp(scores - top)
            factor = jnp.exp(old - top)
            max_s[h] = top
            sum_s[h] = sum_s[h] * factor + jnp.sum(weights, axis=0, keepdims=True)
            acc_s[h] = acc_s[h] * factor + contract(values_of(j, h), weights.astype(BF16), 1, 0)

    lax.fori_loop(1, 16, step, 0)
    for h in range(KV_HEADS):
        result = acc_s[h] / sum_s[h]
        logs = max_s[h] + jnp.log(sum_s[h])
        for g in range(GROUP):
            head = GROUP * h + g
            out_ref[head * HEAD : (head + 1) * HEAD, :] = result[:, g * rows : (g + 1) * rows]
            log_ref[head : head + 1, :] = logs[:, g * rows : (g + 1) * rows]


def attend(ctx, queries, blocks):
    rows = queries.shape[1]
    return pl.pallas_call(
        attend_kernel,
        out_shape=[
            jax.ShapeDtypeStruct((QWIDTH, rows), F32),
            jax.ShapeDtypeStruct((HEADS, rows), F32),
        ],
        in_specs=[pl.BlockSpec(memory_space=pltpu.SMEM)]
        + [pl.BlockSpec(memory_space=pltpu.VMEM)] * 17,
        out_specs=[pl.BlockSpec(memory_space=pltpu.VMEM)] * 2,
        scratch_shapes=[
            pltpu.VMEM((16, 2 * KVWIDTH, rows), BF16),
            pltpu.VMEM((KV_HEADS, HEAD, GROUP * rows), BF16),
            pltpu.VMEM((KV_HEADS, HEAD, GROUP * rows), F32),
            pltpu.VMEM((KV_HEADS, 1, GROUP * rows), F32),
            pltpu.VMEM((KV_HEADS, 1, GROUP * rows), F32),
        ],
        compiler_params=pltpu.CompilerParams(vmem_limit_bytes=VMEM_LIMIT),
        name="attend",
    )(ctx, queries, *blocks)


def attend_back_kernel(ctx_ref, q_ref, g_ref, out_ref, log_ref, *refs):
    blocks = refs[:16]
    gq_ref, ours_ref, theirs_ref, kv_s, q_s, g_s, gq_s, log_s, delta_s, gkv_s = refs[16:]
    rows = q_ref.shape[1]
    for j in range(16):
        kv_s[j] = blocks[j][...]
        gkv_s[j] = jnp.zeros(gkv_s.shape[1:], BF16)
    for h in range(KV_HEADS):
        q_s[h] = lanes_of_group(q_ref, h) * BF16(SCALE)
        grads = lanes_of_group(g_ref, h)
        g_s[h] = grads
        delta_s[h] = jnp.sum(
            grads.astype(F32) * lanes_of_group(out_ref, h), axis=0, keepdims=True
        )
        log_s[h] = jnp.concatenate(
            [log_ref[GROUP * h + g : GROUP * h + g + 1, :] for g in range(GROUP)], axis=1
        )

    def absorb(j, h, allowed):
        keys = kv_s[j, h * HEAD : (h + 1) * HEAD, :]
        values = kv_s[j, KVWIDTH + h * HEAD : KVWIDTH + (h + 1) * HEAD, :]
        probs = jnp.exp(contract(keys, q_s[h], 0, 0) - log_s[h])
        if allowed is not None:
            probs = jnp.where(allowed, probs, 0.0)
        g_probs = contract(values, g_s[h], 0, 0)
        g_scores = (probs * (g_probs - delta_s[h])).astype(BF16)
        gkv_s[j, h * HEAD : (h + 1) * HEAD, :] = contract(q_s[h], g_scores, 1, 1).astype(BF16)
        gkv_s[j, KVWIDTH + h * HEAD : KVWIDTH + (h + 1) * HEAD, :] = contract(
            g_s[h], probs.astype(BF16), 1, 1
        ).astype(BF16)
        return contract(keys, g_scores, 1, 0)

    allowed = causal(rows)
    for h in range(KV_HEADS):
        gq_s[h] = absorb(0, h, allowed)

    def step(j, carry):
        @pl.when(present(ctx_ref[0], j))
        def _():
            for h in range(KV_HEADS):
                gq_s[h] += absorb(j, h, None)

        return carry

    lax.fori_loop(1, 16, step, 0)
    for h in range(KV_HEADS):
        result = gq_s[h] * SCALE
        for g in range(GROUP):
            head = GROUP * h + g
            gq_ref[head * HEAD : (head + 1) * HEAD, :] = result[:, g * rows : (g + 1) * rows]
    for k in range(8):
        ours_ref[k] = gkv_s[2 * k]
        theirs_ref[k] = gkv_s[2 * k + 1]


def attend_back(ctx, queries, grads, result, logs, blocks):
    rows = queries.shape[1]
    half = jax.ShapeDtypeStruct((8, 2 * KVWIDTH, rows), BF16)
    wide = (KV_HEADS, HEAD, GROUP * rows)
    return pl.pallas_call(
        attend_back_kernel,
        out_shape=[jax.ShapeDtypeStruct((QWIDTH, rows), F32), half, half],
        in_specs=[pl.BlockSpec(memory_space=pltpu.SMEM)]
        + [pl.BlockSpec(memory_space=pltpu.VMEM)] * 20,
        out_specs=[pl.BlockSpec(memory_space=pltpu.VMEM)] * 3,
        scratch_shapes=[
            pltpu.VMEM((16, 2 * KVWIDTH, rows), BF16),
            pltpu.VMEM(wide, BF16),
            pltpu.VMEM(wide, BF16),
            pltpu.VMEM(wide, F32),
            pltpu.VMEM((KV_HEADS, 1, GROUP * rows), F32),
            pltpu.VMEM((KV_HEADS, 1, GROUP * rows), F32),
            pltpu.VMEM((16, 2 * KVWIDTH, rows), BF16),
        ],
        compiler_params=pltpu.CompilerParams(vmem_limit_bytes=VMEM_LIMIT),
        name="attend_back",
    )(ctx, queries, grads, result, logs, *blocks)


def turn(heads, cosine, sine, sign):
    parts = heads.reshape(-1, 2, HEAD // 2, heads.shape[-1])
    first, second = parts[:, 0], parts[:, 1]
    sine = sign * sine
    return jnp.stack(
        [first * cosine - second * sine, second * cosine + first * sine], axis=1
    ).reshape(heads.shape)


def norm_back(grad, normed, inverse, gain):
    scaled = grad * gain
    mean = jnp.mean(scaled * normed, axis=-1, keepdims=True)
    return inverse * (scaled - normed * mean), jnp.sum(grad * normed, axis=0)


def body(
    tokens, norm_attn, w_query, w_key, w_value, w_out, norm_ffn, w_gate, w_up, w_down, cotangent
):
    rows, width = tokens.shape[1:]
    part = norm_attn.shape[0]
    ff_part = w_down.shape[0]
    ctx = lax.axis_index("ctx")
    me = lax.axis_index("fsdp")
    chip = ctx // 2
    first = ctx % 2 == 0
    inputs = tokens.reshape(rows, width).astype(F32)
    cot = cotangent.reshape(rows, width)
    ahead = [moved(me, "fsdp", *step) for step in STEPS]
    where = jnp.stack(ahead + [ctx % 2]).astype(jnp.int32)
    chips_ahead = [moved(chip, "fsdp", *step) for step in STEPS]
    chip_where = jnp.stack(chips_ahead).astype(jnp.int32)

    half = jnp.where(
        first,
        jnp.concatenate([w_query, w_key], axis=1),
        jnp.concatenate([w_out, w_value], axis=1),
    )
    columns = half.shape[1]
    gain_rows = jnp.zeros((128 - part, columns), BF16)
    gain_rows = gain_rows.at[0, :part].set(norm_attn).at[1, :part].set(norm_ffn)
    ours = gather_blocks(jnp.concatenate([half, gain_rows], axis=0), "fsdp")
    theirs = [core_swap(block) for block in ours]
    full_qk, full_ov = place_pair(ours, theirs, where)
    gains = full_qk[:, part : part + 2, :part].astype(F32)
    gain_one = gains[:, 0].reshape(1, width)
    gain_two = gains[:, 1].reshape(1, width)
    full_qk = full_qk.reshape(1024, columns)
    full_ov = full_ov.reshape(1024, columns)

    w_gate, w_up, cot_late, _ = lax.optimization_barrier((w_gate, w_up, cot, ours[7]))
    ff_half = jnp.where(first, w_gate, w_up).reshape(part, 8, ff_part).transpose(1, 0, 2)
    ff_half = jnp.pad(ff_half, ((0, 0), (0, 128 - part), (0, 0)))
    ff_ours = exchange_blocks(ff_half, me)
    gate_cols, up_cols = place_pair(ff_ours, [core_swap(block) for block in ff_ours], where)
    gate_cols = gate_cols.reshape(1024, ff_part)
    up_cols = up_cols.reshape(1024, ff_part)

    inverse_one = lax.rsqrt(jnp.mean(inputs * inputs, axis=-1, keepdims=True) + EPSILON)
    normed_one = inputs * inverse_one
    act_one = spread((normed_one * gain_one).astype(BF16))
    inverse_freq = ROPE_BASE ** (-(jnp.arange(HEAD // 2, dtype=F32) * 2.0 / HEAD))
    positions = (ctx * rows + jnp.arange(rows, dtype=jnp.int32)).astype(F32)
    angles = inverse_freq[:, None] * positions[None, :]
    cosine, sine = jnp.cos(angles), jnp.sin(angles)
    rotated = turn(contract(full_qk, act_one, 0, 1), cosine, sine, 1.0).astype(BF16)
    values = contract(full_ov, act_one, 0, 1)[width:].astype(BF16)
    queries = rotated[:QWIDTH]
    blocks = []
    for block in gather_earlier(jnp.concatenate([rotated[QWIDTH:], values], axis=0)):
        blocks += [block, core_swap(block)]
    position = ctx.astype(jnp.int32).reshape(1)
    result, logs = attend(position, queries, blocks)
    attn = spread_rows(result.astype(BF16), part)
    hidden = inputs + contract(attn, full_ov, 0, 0)[:, :width]

    inverse_two = lax.rsqrt(jnp.mean(hidden * hidden, axis=-1, keepdims=True) + EPSILON)
    normed_two = hidden * inverse_two
    act_two = spread((normed_two * gain_two).astype(BF16))
    every = 8 * rows
    cot_all = lax.all_gather(spread(cot_late), "fsdp", axis=0, tiled=True)
    g_inner = contract(cot_all, spread(w_down), 1, 1)
    act_all = place(gather_blocks(act_two, "fsdp"), where).reshape(every, 1024)
    gate = contract(act_all, gate_cols, 1, 0)
    up = contract(act_all, up_cols, 1, 0)
    sigmoid = jax.nn.sigmoid(gate)
    silu = gate * sigmoid
    inner = (silu * up).astype(BF16)
    g_gate = (g_inner * up * sigmoid * (1.0 + gate * (1.0 - sigmoid))).astype(BF16)
    g_up = (g_inner * silu).astype(BF16)
    g_act_part = contract(g_gate, gate_cols, 1, 1) + contract(g_up, up_cols, 1, 1)
    g_act_two = reduce_blocks(g_act_part.astype(BF16).reshape(8, rows, 1024), "fsdp", me)
    down_part = contract(inner, w_down, 1, 0).astype(BF16)
    down = lax.psum_scatter(down_part, "fsdp", scatter_dimension=0, tiled=True)
    output = (hidden + down.astype(F32)).astype(BF16)

    grad_gate = contract(act_all, g_gate, 0, 0)
    grad_up = contract(act_all, g_up, 0, 0)
    grad_down = contract(cot_all, inner, 0, 0)
    low_down, high_down = grad_down[:, : ff_part // 2], grad_down[:, ff_part // 2 :]
    mine = jnp.concatenate(
        [jnp.where(first, grad_gate, grad_up), jnp.where(first, low_down, high_down)], axis=1
    )
    other = jnp.concatenate(
        [jnp.where(first, grad_up, grad_gate), jnp.where(first, high_down, low_down)], axis=1
    )
    ff_sum = mine + core_swap(other.astype(BF16)).astype(F32)
    ff_sum = ff_sum.astype(BF16).reshape(8, 128, -1)
    gate_rows = jnp.stack(exchange_blocks(ff_sum[..., :ff_part], me))
    ff_rows = jnp.concatenate([gate_rows, ff_sum[..., ff_part:]], axis=2)
    ff_rows = reduce_blocks(ff_rows, "ctx", chip).astype(BF16)
    ff_rows = place(gather_blocks(ff_rows, "ctx"), chip_where)
    ff_other = core_swap(ff_rows)
    ff_zero = jnp.where(first, ff_rows, ff_other)
    ff_one = jnp.where(first, ff_other, ff_rows)

    def in_order(half):
        half = half[:, :part, :ff_part]
        found = [
            lax.dynamic_index_in_dim(
                half, ((t // 2 - me // 2) % 4) * 2 + (t + me) % 2, 0, keepdims=False
            )
            for t in range(8)
        ]
        return jnp.concatenate(found, axis=1).astype(F32)

    grad_down = jnp.concatenate([ff_zero[..., ff_part:], ff_one[..., ff_part:]], axis=2)
    grad_down = unspread_rows(grad_down, part).T.astype(F32)

    g_normed, gain_two_term = norm_back(
        unspread(g_act_two, part), normed_two, inverse_two, gain_two
    )
    g_hidden = cot.astype(F32) + g_normed
    g_hid = g_hidden.astype(BF16)
    g_hid_wide = jnp.pad(g_hid, ((0, 0), (0, columns - width)))
    g_attn = unspread_rows(contract(full_ov, g_hid_wide, 1, 1).astype(BF16), part)

    g_query_rot, g_ours, g_theirs = attend_back(position, queries, g_attn, result, logs, blocks)
    g_pairs = g_ours.astype(F32) + core_swap(g_theirs).astype(F32)
    g_query = turn(g_query_rot, cosine, sine, -1.0).astype(BF16)
    g_kv = reduce_earlier([g_pairs[k] for k in range(8)])
    g_key = turn(g_kv[:KVWIDTH], cosine, sine, -1.0).astype(BF16)
    g_value = g_kv[KVWIDTH:].astype(BF16)
    g_qk = jnp.concatenate([g_query, g_key], axis=0)
    g_ov = jnp.pad(g_value, ((width, 0), (0, 0)))
    g_act_one = contract(g_qk, full_qk, 0, 1) + contract(g_ov, full_ov, 0, 1)
    g_inputs, gain_one_term = norm_back(
        unspread(g_act_one, part), normed_one, inverse_one, gain_one
    )
    input_grad = (g_hidden + g_inputs).astype(BF16)

    def fsdp_sum(zero, one):
        mine = jnp.where(first, zero, one)
        other = jnp.where(first, one, zero).astype(BF16)
        total = (mine + core_swap(other).astype(F32)).astype(BF16)
        return reduce_blocks(total.reshape(8, 128, -1), "fsdp", me)

    wide_sum = fsdp_sum(contract(act_one, g_query, 0, 1), contract(attn, g_hid, 1, 0))
    gain_terms = jnp.stack(
        [gain_one_term.reshape(8, part), gain_two_term.reshape(8, part)], axis=1
    )
    gain_terms = jnp.pad(gain_terms, ((0, 0), (part, 126 - part), (0, KVWIDTH - part)))
    grad_key = contract(act_one, g_key, 0, 1) + gain_terms.reshape(1024, KVWIDTH)
    narrow_sum = fsdp_sum(grad_key, contract(act_one, g_value, 0, 1))
    sums = jnp.concatenate([wide_sum, narrow_sum], axis=1).astype(BF16)
    sums = reduce_blocks(sums.reshape(8, 16, columns), "ctx", chip).astype(BF16)
    sums = place(gather_blocks(sums, "ctx"), chip_where).reshape(128, columns)
    sums_other = core_swap(sums)
    sums_qk = jnp.where(first, sums, sums_other).astype(F32)
    sums_ov = jnp.where(first, sums_other, sums).astype(F32)
    return (
        output[None],
        input_grad[None],
        sums_qk[part, width : width + part],
        sums_qk[:part, :width],
        sums_qk[:part, width:],
        sums_ov[:part, width:],
        sums_ov[:part, :width],
        sums_qk[part + 1, width : width + part],
        in_order(ff_zero),
        in_order(ff_one),
        grad_down,
    )


def solution(mesh):
    rows = P("fsdp", None)
    tokens = P("fsdp", "ctx", None)
    in_specs = (
        tokens,
        P("fsdp"),
        rows,
        rows,
        rows,
        rows,
        P("fsdp"),
        rows,
        rows,
        rows,
        tokens,
    )
    out_specs = (
        tokens,
        tokens,
        P("fsdp"),
        rows,
        rows,
        rows,
        rows,
        P("fsdp"),
        rows,
        rows,
        rows,
    )
    return jax.shard_map(body, mesh=mesh, in_specs=in_specs, out_specs=out_specs, check_vma=False)
```

```python
import functools

import jax
import jax.numpy as jnp
from jax import lax
from jax.experimental import pallas as pl
from jax.experimental.pallas import tpu as pltpu
from jax.sharding import PartitionSpec as P

HEADS = 15
KV_HEADS = 5
GROUP = HEADS // KV_HEADS
HEAD = 64
QWIDTH = HEADS * HEAD
KVWIDTH = KV_HEADS * HEAD

EPSILON = 1e-05
ROPE_BASE = 10000.0
MASK_VALUE = -1e30
SCALE = HEAD ** (-0.5)

BF16 = jnp.bfloat16
F32 = jnp.float32
WIDE_SPLIT = 512
VMEM_LIMIT = 48 * 1024 * 1024

STEPS = [(ring, pair) for ring in range(4) for pair in range(2)]


def moved(index, axis, ring, pair):
    low = 1 if axis == "fsdp" else 2
    core = index % low
    place = index // low
    place = ((place // 2 + ring) % 4) * 2 + (place % 2 + pair) % 2
    return place * low + core


def take(value, axis, ring, pair):
    size = 8 if axis == "fsdp" else 16
    return lax.ppermute(
        value, axis, [(i, moved(i, axis, -ring, pair)) for i in range(size)]
    )


def core_swap(value):
    return lax.ppermute(value, "ctx", [(i, i ^ 1) for i in range(16)])


def gather_blocks(value, axis):
    found = {(0, 0): value, (0, 1): take(value, axis, 0, 1)}
    found[1, 0] = take(value, axis, 1, 0)
    found[3, 0] = take(value, axis, 3, 0)
    found[1, 1] = take(found[0, 1], axis, 1, 0)
    found[3, 1] = take(found[0, 1], axis, 3, 0)
    found[2, 0] = take(found[1, 0], axis, 1, 0)
    found[2, 1] = take(found[3, 1], axis, 3, 0)
    return [found[step] for step in STEPS]


def steps_from(me, sign):
    return jnp.stack([moved(me, "fsdp", sign * ring, pair) for ring, pair in STEPS]).astype(
        jnp.int32
    )


def reduce_terms(terms, axis):
    term = dict(zip(STEPS, terms))

    def plus(first, *others):
        return sum((other.astype(F32) for other in others), first.astype(F32))

    one = plus(term[1, 0], take(term[2, 0], axis, 3, 0)).astype(BF16)
    three = plus(term[3, 1], take(term[2, 1], axis, 1, 0)).astype(BF16)
    pair = plus(term[0, 1], take(term[1, 1], axis, 3, 0), take(three, axis, 1, 0)).astype(BF16)
    return plus(
        term[0, 0], take(term[3, 0], axis, 1, 0), take(one, axis, 3, 0), take(pair, axis, 0, 1)
    )


def exchange_parts(parts, axis):
    return [parts[0]] + [take(part, axis, *step) for step, part in zip(STEPS[1:], parts[1:])]


def ring_sum(parts):
    return sum_parts(
        [parts[0]] + [take(parts[r], "ctx", 4 - r, 0) for r in range(1, 4)]
    ).astype(BF16)


def pair_sum(parts):
    return sum_parts([parts[0], take(parts[1], "ctx", 0, 1)]).astype(BF16)


def ctx_gather(piece, ring, pair):
    both = place([piece, take(piece, "ctx", 0, 1)], pair)
    return place([both] + [take(both, "ctx", r, 0) for r in range(1, 4)], ring)


def sum_parts(parts):
    return sum((part.astype(F32) for part in parts[1:]), parts[0].astype(F32))


def later(value, ring):
    pairs = [(i, i + 4 * ring) for i in range(16 - 4 * ring)]
    return lax.ppermute(value, "ctx", pairs)


def sooner(value, ring):
    pairs = [(i, i - 4 * ring) for i in range(4 * ring, 16)]
    return lax.ppermute(value, "ctx", pairs)


def gather_earlier(value):
    found = {(0, 0): value, (1, 0): later(value, 1)}
    found[0, 1] = take(value, "ctx", 0, 1)
    found[1, 1] = later(found[0, 1], 1)
    for p in range(2):
        found[3, p] = later(found[0, p], 3)
        found[2, p] = later(found[1, p], 1)
    return [found[step] for step in STEPS]


def reduce_earlier(terms):
    term = dict(zip(STEPS, terms))
    home = []
    for p in (1, 0):
        one = term[1, p] + sooner(term[2, p].astype(BF16), 1).astype(F32)
        total = term[0, p] + sooner(term[3, p].astype(BF16), 3).astype(F32)
        home.append(total + sooner(one.astype(BF16), 1).astype(F32))
    return home[1] + take(home[0].astype(BF16), "ctx", 0, 1).astype(F32)


def copy_all(pairs, semaphores):
    copies = [
        pltpu.make_async_copy(source, goal, semaphores.at[i])
        for i, (source, goal) in enumerate(pairs)
    ]
    for copy in copies:
        copy.start()
    for copy in copies:
        copy.wait()


def place_kernel(where_ref, *refs):
    blocks, out_ref, semaphores = refs[:-2], refs[-2], refs[-1]
    copy_all([(block, out_ref.at[where_ref[r]]) for r, block in enumerate(blocks)], semaphores)


def place(blocks, where):
    count, shape = len(blocks), blocks[0].shape
    return pl.pallas_call(
        place_kernel,
        out_shape=jax.ShapeDtypeStruct((count,) + shape, blocks[0].dtype),
        in_specs=[pl.BlockSpec(memory_space=pltpu.SMEM)]
        + [pl.BlockSpec(memory_space=pl.ANY)] * count,
        out_specs=pl.BlockSpec(memory_space=pltpu.VMEM),
        scratch_shapes=[pltpu.SemaphoreType.DMA((count,))],
        compiler_params=pltpu.CompilerParams(vmem_limit_bytes=VMEM_LIMIT),
        name="place",
    )(where, *blocks)


def deal_kernel(which_ref, source_ref, *refs):
    outs, semaphores = refs[:-1], refs[-1]
    copy_all([(source_ref.at[which_ref[r]], out) for r, out in enumerate(outs)], semaphores)


def deal(blocks, which):
    count = blocks.shape[0]
    shape = jax.ShapeDtypeStruct(blocks.shape[1:], blocks.dtype)
    return pl.pallas_call(
        deal_kernel,
        out_shape=[shape] * count,
        in_specs=[pl.BlockSpec(memory_space=pltpu.SMEM), pl.BlockSpec(memory_space=pl.ANY)],
        out_specs=[pl.BlockSpec(memory_space=pltpu.VMEM)] * count,
        scratch_shapes=[pltpu.SemaphoreType.DMA((count,))],
        compiler_params=pltpu.CompilerParams(vmem_limit_bytes=VMEM_LIMIT),
        name="deal",
    )(which, blocks)


def split_kernel(which_ref, gate_ref, up_ref, *refs):
    outs, blocks = refs[:8], refs[8]
    part, unit = gate_ref.shape[0], gate_ref.shape[1] // 8
    blocks[...] = jnp.zeros(blocks.shape, BF16)

    def lay(source):
        for t in range(8):
            blocks[t, :part] = source[:, t * unit : (t + 1) * unit]

    pl.when(which_ref[8] == 0)(lambda: lay(gate_ref))
    pl.when(which_ref[8] == 1)(lambda: lay(up_ref))
    for r, out in enumerate(outs):
        out[...] = blocks[which_ref[r]]


def split_columns(gate, up, which):
    shape = jax.ShapeDtypeStruct((128, gate.shape[1] // 8), BF16)
    return pl.pallas_call(
        split_kernel,
        out_shape=[shape] * 8,
        in_specs=[pl.BlockSpec(memory_space=pltpu.SMEM)]
        + [pl.BlockSpec(memory_space=pltpu.VMEM)] * 2,
        out_specs=[pl.BlockSpec(memory_space=pltpu.VMEM)] * 8,
        scratch_shapes=[pltpu.VMEM((8,) + shape.shape, BF16)],
        compiler_params=pltpu.CompilerParams(vmem_limit_bytes=VMEM_LIMIT),
        name="split_columns",
    )(which, gate, up)


def place_pair_kernel(where_ref, *refs):
    ours, theirs, zero_ref, one_ref, semaphores = refs[:8], refs[8:16], refs[16], refs[17], refs[18]

    def lay(zero, one):
        pairs = [(zero[r], zero_ref.at[where_ref[r]]) for r in range(8)]
        copy_all(pairs + [(one[r], one_ref.at[where_ref[r]]) for r in range(8)], semaphores)

    pl.when(where_ref[8] == 0)(lambda: lay(ours, theirs))
    pl.when(where_ref[8] == 1)(lambda: lay(theirs, ours))


def place_pair(ours, theirs, where):
    shape = (8,) + ours[0].shape
    return pl.pallas_call(
        place_pair_kernel,
        out_shape=[jax.ShapeDtypeStruct(shape, BF16)] * 2,
        in_specs=[pl.BlockSpec(memory_space=pltpu.SMEM)]
        + [pl.BlockSpec(memory_space=pl.ANY)] * 16,
        out_specs=[pl.BlockSpec(memory_space=pltpu.VMEM)] * 2,
        scratch_shapes=[pltpu.SemaphoreType.DMA((16,))],
        compiler_params=pltpu.CompilerParams(vmem_limit_bytes=VMEM_LIMIT),
        name="place_pair",
    )(where, *ours, *theirs)


def spread(value):
    rows = value.shape[0]
    groups = value.reshape(rows, 8, -1)
    return jnp.pad(groups, ((0, 0), (0, 0), (0, 128 - groups.shape[2]))).reshape(rows, 1024)


def unspread(value, part):
    rows = value.shape[0]
    return value.reshape(rows, 8, 128)[:, :, :part].reshape(rows, 8 * part)


def spread_rows(value, part):
    groups = value.reshape(8, part, -1)
    return jnp.pad(groups, ((0, 0), (0, 128 - part), (0, 0))).reshape(1024, -1)


def unspread_rows(value, part):
    return value.reshape(8, 128, -1)[:, :part].reshape(8 * part, -1)


def contract(left, right, left_dim, right_dim):
    return lax.dot_general(
        left, right, (((left_dim,), (right_dim,)), ((), ())), preferred_element_type=F32
    )


def lanes_of_group(ref, h):
    return jnp.concatenate(
        [ref[(GROUP * h + g) * HEAD : (GROUP * h + g + 1) * HEAD, :] for g in range(GROUP)], axis=1
    )


def allowed_at_home(rows, core):
    key = lax.broadcasted_iota(jnp.int32, (2 * rows, GROUP * rows), 0)
    query = lax.broadcasted_iota(jnp.int32, (2 * rows, GROUP * rows), 1) % rows
    return key <= jnp.where(key < rows, query, jnp.where(core == 1, 2 * rows, 0))


def present(ctx, k):
    x, z_hi = ctx // 4, (ctx // 2) % 2
    ring, pair = k // 2, k % 2
    return jnp.logical_and(x >= ring, jnp.logical_or(ring > 0, (z_hi + pair) % 2 < z_hi))


def keys_of(kv_s, k, h):
    return kv_s[k, h * HEAD : (h + 1) * HEAD, :]


def values_of(kv_s, k, h):
    return kv_s[k, KVWIDTH + h * HEAD : KVWIDTH + (h + 1) * HEAD, :]


def attend_kernel(ctx_ref, q_ref, *refs):
    blocks = refs[:16]
    out_ref, log_ref, kv_s, q_s, acc_s, max_s, sum_s = refs[16:]
    rows = q_ref.shape[1]
    ctx = ctx_ref[0]
    for k in range(8):
        kv_s[k, :, :rows] = blocks[2 * k][...]
        kv_s[k, :, rows:] = blocks[2 * k + 1][...]
    for h in range(KV_HEADS):
        q_s[h] = lanes_of_group(q_ref, h) * BF16(SCALE)

    allowed = allowed_at_home(rows, ctx % 2)
    for h in range(KV_HEADS):
        scores = jnp.where(allowed, contract(keys_of(kv_s, 0, h), q_s[h], 0, 0), MASK_VALUE)
        top = jnp.max(scores, axis=0, keepdims=True)
        weights = jnp.exp(scores - top)
        max_s[h] = top
        sum_s[h] = jnp.sum(weights, axis=0, keepdims=True)
        acc_s[h] = contract(values_of(kv_s, 0, h), weights.astype(BF16), 1, 0)

    def absorb(k):
        for h in range(KV_HEADS):
            scores = contract(keys_of(kv_s, k, h), q_s[h], 0, 0)
            old = max_s[h]
            top = jnp.maximum(old, jnp.max(scores, axis=0, keepdims=True))
            weights = jnp.exp(scores - top)
            factor = jnp.exp(old - top)
            max_s[h] = top
            sum_s[h] = sum_s[h] * factor + jnp.sum(weights, axis=0, keepdims=True)
            acc_s[h] = acc_s[h] * factor + contract(
                values_of(kv_s, k, h), weights.astype(BF16), 1, 0
            )

    def step(k, carry):
        pl.when(present(ctx, k))(functools.partial(absorb, k))
        return carry

    lax.fori_loop(1, 8, step, 0)
    for h in range(KV_HEADS):
        result = acc_s[h] / sum_s[h]
        logs = max_s[h] + jnp.log(sum_s[h])
        for g in range(GROUP):
            head = GROUP * h + g
            out_ref[head * HEAD : (head + 1) * HEAD, :] = result[:, g * rows : (g + 1) * rows]
            log_ref[head : head + 1, :] = logs[:, g * rows : (g + 1) * rows]


def attend(ctx, queries, blocks):
    rows = queries.shape[1]
    return pl.pallas_call(
        attend_kernel,
        out_shape=[
            jax.ShapeDtypeStruct((QWIDTH, rows), F32),
            jax.ShapeDtypeStruct((HEADS, rows), F32),
        ],
        in_specs=[pl.BlockSpec(memory_space=pltpu.SMEM)]
        + [pl.BlockSpec(memory_space=pltpu.VMEM)] * 17,
        out_specs=[pl.BlockSpec(memory_space=pltpu.VMEM)] * 2,
        scratch_shapes=[
            pltpu.VMEM((8, 2 * KVWIDTH, 2 * rows), BF16),
            pltpu.VMEM((KV_HEADS, HEAD, GROUP * rows), BF16),
            pltpu.VMEM((KV_HEADS, HEAD, GROUP * rows), F32),
            pltpu.VMEM((KV_HEADS, 1, GROUP * rows), F32),
            pltpu.VMEM((KV_HEADS, 1, GROUP * rows), F32),
        ],
        compiler_params=pltpu.CompilerParams(vmem_limit_bytes=VMEM_LIMIT),
        cost_estimate=pl.CostEstimate(
            flops=14000000000, bytes_accessed=5000000, transcendentals=4000000
        ),
        name="attend",
    )(ctx, queries, *blocks)


def attend_back_kernel(ctx_ref, q_ref, g_ref, out_ref, log_ref, *refs):
    blocks = refs[:16]
    gq_ref, ours_ref, theirs_ref, kv_s, q_s, g_s, gq_s, log_s, delta_s = refs[16:]
    rows = q_ref.shape[1]
    ctx = ctx_ref[0]
    for k in range(8):
        kv_s[k, :, :rows] = blocks[2 * k][...]
        kv_s[k, :, rows:] = blocks[2 * k + 1][...]
    for h in range(KV_HEADS):
        q_s[h] = lanes_of_group(q_ref, h) * BF16(SCALE)
        grads = lanes_of_group(g_ref, h)
        g_s[h] = grads
        delta_s[h] = jnp.sum(
            grads.astype(F32) * lanes_of_group(out_ref, h), axis=0, keepdims=True
        )
        log_s[h] = jnp.concatenate(
            [log_ref[GROUP * h + g : GROUP * h + g + 1, :] for g in range(GROUP)], axis=1
        )

    def absorb(k, h, allowed):
        keys = keys_of(kv_s, k, h)
        probs = jnp.exp(contract(keys, q_s[h], 0, 0) - log_s[h])
        if allowed is not None:
            probs = jnp.where(allowed, probs, 0.0)
        g_probs = contract(values_of(kv_s, k, h), g_s[h], 0, 0)
        g_scores = (probs * (g_probs - delta_s[h])).astype(BF16)
        g_keys = contract(q_s[h], g_scores, 1, 1).astype(BF16)
        g_values = contract(g_s[h], probs.astype(BF16), 1, 1).astype(BF16)
        for at, grads in ((h * HEAD, g_keys), (KVWIDTH + h * HEAD, g_values)):
            ours_ref[k, at : at + HEAD, :] = grads[:, :rows]
            theirs_ref[k, at : at + HEAD, :] = grads[:, rows:]
        return contract(keys, g_scores, 1, 0)

    allowed = allowed_at_home(rows, ctx % 2)
    for h in range(KV_HEADS):
        gq_s[h] = absorb(0, h, allowed)

    def step(k, carry):
        here = present(ctx, k)

        @pl.when(here)
        def _():
            for h in range(KV_HEADS):
                gq_s[h] += absorb(k, h, None)

        @pl.when(jnp.logical_not(here))
        def _():
            ours_ref[k] = jnp.zeros(ours_ref.shape[1:], BF16)
            theirs_ref[k] = jnp.zeros(theirs_ref.shape[1:], BF16)

        return carry

    lax.fori_loop(1, 8, step, 0)
    for h in range(KV_HEADS):
        result = gq_s[h] * SCALE
        for g in range(GROUP):
            head = GROUP * h + g
            gq_ref[head * HEAD : (head + 1) * HEAD, :] = result[:, g * rows : (g + 1) * rows]


def attend_back(ctx, queries, grads, result, logs, blocks):
    rows = queries.shape[1]
    half = jax.ShapeDtypeStruct((8, 2 * KVWIDTH, rows), BF16)
    wide = (KV_HEADS, HEAD, GROUP * rows)
    return pl.pallas_call(
        attend_back_kernel,
        out_shape=[jax.ShapeDtypeStruct((QWIDTH, rows), F32), half, half],
        in_specs=[pl.BlockSpec(memory_space=pltpu.SMEM)]
        + [pl.BlockSpec(memory_space=pltpu.VMEM)] * 20,
        out_specs=[pl.BlockSpec(memory_space=pltpu.VMEM)] * 3,
        scratch_shapes=[
            pltpu.VMEM((8, 2 * KVWIDTH, 2 * rows), BF16),
            pltpu.VMEM(wide, BF16),
            pltpu.VMEM(wide, BF16),
            pltpu.VMEM(wide, F32),
            pltpu.VMEM((KV_HEADS, 1, GROUP * rows), F32),
            pltpu.VMEM((KV_HEADS, 1, GROUP * rows), F32),
        ],
        compiler_params=pltpu.CompilerParams(vmem_limit_bytes=VMEM_LIMIT),
        cost_estimate=pl.CostEstimate(
            flops=18000000000, bytes_accessed=5000000, transcendentals=4000000
        ),
        name="attend_back",
    )(ctx, queries, grads, result, logs, *blocks)


def turn(heads, cosine, sine, sign):
    parts = heads.reshape(-1, 2, HEAD // 2, heads.shape[-1])
    first, second = parts[:, 0], parts[:, 1]
    sine = sign * sine
    return jnp.stack(
        [first * cosine - second * sine, second * cosine + first * sine], axis=1
    ).reshape(heads.shape)


def project_kernel(act_ref, qk_ref, ov_ref, cos_ref, sin_ref, q_ref, kv_ref, v_s, semaphore):
    start = QWIDTH // 128 * 128
    copy = pltpu.make_async_copy(ov_ref.at[:, start:], v_s, semaphore)
    copy.start()
    cosine, sine = cos_ref[...], sin_ref[...]
    half = HEAD // 2
    turned = contract(act_ref[...], qk_ref[...], 1, 0).T
    for head in range(HEADS + KV_HEADS):
        first = turned[head * HEAD : head * HEAD + half]
        second = turned[head * HEAD + half : (head + 1) * HEAD]
        goal = q_ref if head < HEADS else kv_ref
        at = (head if head < HEADS else head - HEADS) * HEAD
        goal[at : at + half] = (first * cosine - second * sine).astype(BF16)
        goal[at + half : at + HEAD] = (second * cosine + first * sine).astype(BF16)
    copy.wait()
    values = contract(act_ref[...], v_s[...], 1, 0).T
    kv_ref[KVWIDTH:] = values[QWIDTH - start :].astype(BF16)


def project(act, full_qk, full_ov, cosine, sine):
    rows = act.shape[0]
    spec = pl.BlockSpec(memory_space=pltpu.VMEM)
    tail = full_ov.shape[1] - QWIDTH // 128 * 128
    return pl.pallas_call(
        project_kernel,
        out_shape=[
            jax.ShapeDtypeStruct((QWIDTH, rows), BF16),
            jax.ShapeDtypeStruct((2 * KVWIDTH, rows), BF16),
        ],
        in_specs=[spec, spec, pl.BlockSpec(memory_space=pl.ANY), spec, spec],
        out_specs=[spec, spec],
        scratch_shapes=[pltpu.VMEM((full_ov.shape[0], tail), BF16), pltpu.SemaphoreType.DMA],
        compiler_params=pltpu.CompilerParams(vmem_limit_bytes=VMEM_LIMIT),
        name="project",
    )(act, full_qk, full_ov, cosine, sine)


def store_halves(core, mine_ref, other_ref, t, zero, one):
    @pl.when(core == 0)
    def _():
        mine_ref[t] = zero
        other_ref[t] = one

    @pl.when(core == 1)
    def _():
        mine_ref[t] = one
        other_ref[t] = zero


def halves_kernel(
    core_ref, act_ref, query_ref, attn_ref, hid_ref, kv_ref, gain_ref, mine_ref, other_ref
):
    split = WIDE_SPLIT
    for t in range(8):
        at = slice(t * 128, (t + 1) * 128)
        act = act_ref[:, at]
        query = contract(act, query_ref[...], 0, 1).astype(BF16)
        out = contract(attn_ref[at], hid_ref[...], 1, 0).astype(BF16)
        key = contract(act, kv_ref[:KVWIDTH], 0, 1)
        value = contract(act, kv_ref[KVWIDTH:], 0, 1).astype(BF16)
        gains = jnp.concatenate([jnp.zeros((120, 128), F32), gain_ref[t]], axis=0)
        key = jnp.concatenate([key[:, :128] + gains, key[:, 128:]], axis=1).astype(BF16)
        zero = jnp.concatenate([query[:, :split], out[:, split:], key], axis=1)
        one = jnp.concatenate([out[:, :split], query[:, split:], value], axis=1)
        store_halves(core_ref[0], mine_ref, other_ref, t, zero, one)


def halves(core, act, query, attn, hid, kv, gains):
    shape = jax.ShapeDtypeStruct((8, 128, QWIDTH + KVWIDTH), BF16)
    return pl.pallas_call(
        halves_kernel,
        out_shape=[shape, shape],
        in_specs=[pl.BlockSpec(memory_space=pltpu.SMEM)]
        + [pl.BlockSpec(memory_space=pltpu.VMEM)] * 6,
        out_specs=[pl.BlockSpec(memory_space=pltpu.VMEM)] * 2,
        compiler_params=pltpu.CompilerParams(vmem_limit_bytes=VMEM_LIMIT),
        name="halves",
    )(core, act, query, attn, hid, kv, gains)


def add_kernel(which_ref, mine_ref, other_ref, *outs):
    for r, out in enumerate(outs):
        at = which_ref[r]
        out[...] = (mine_ref[at].astype(F32) + other_ref[at].astype(F32)).astype(BF16)


def add_terms(mine, other, which):
    shape = jax.ShapeDtypeStruct(mine.shape[1:], BF16)
    return pl.pallas_call(
        add_kernel,
        out_shape=[shape] * 8,
        in_specs=[pl.BlockSpec(memory_space=pltpu.SMEM)]
        + [pl.BlockSpec(memory_space=pltpu.VMEM)] * 2,
        out_specs=[pl.BlockSpec(memory_space=pltpu.VMEM)] * 8,
        compiler_params=pltpu.CompilerParams(vmem_limit_bytes=VMEM_LIMIT),
        name="add_terms",
    )(which, mine, other)


def norm_back(grad, normed, inverse, gain):
    scaled = grad * gain
    mean = jnp.mean(scaled * normed, axis=-1, keepdims=True)
    return inverse * (scaled - normed * mean), jnp.sum(grad * normed, axis=0)


def body(
    tokens, norm_attn, w_query, w_key, w_value, w_out, norm_ffn, w_gate, w_up, w_down, cotangent
):
    rows, width = tokens.shape[1:]
    part = norm_attn.shape[0]
    ff_part = w_down.shape[0]
    ctx = lax.axis_index("ctx")
    me = lax.axis_index("fsdp")
    chip = ctx // 2
    first = ctx % 2 == 0
    inputs = tokens.reshape(rows, width).astype(F32)
    cot = cotangent.reshape(rows, width)
    ahead = [moved(me, "fsdp", *step) for step in STEPS]
    where = jnp.stack(ahead + [ctx % 2]).astype(jnp.int32)
    chips_ahead = [moved(chip, "fsdp", *step) for step in STEPS]
    chip_where = jnp.stack(chips_ahead).astype(jnp.int32)

    half = jnp.where(
        first,
        jnp.concatenate([w_query, w_key], axis=1),
        jnp.concatenate([w_out, w_value], axis=1),
    )
    columns = half.shape[1]
    gain_rows = jnp.zeros((128 - part, columns), BF16)
    gain_rows = gain_rows.at[0, :part].set(norm_attn).at[1, :part].set(norm_ffn)
    ours = gather_blocks(jnp.concatenate([half, gain_rows], axis=0), "fsdp")
    theirs = [core_swap(block) for block in ours]
    cot_late, _ = lax.optimization_barrier((cot, ours[7]))
    ff_parts = split_columns(w_gate, w_up, jnp.append(steps_from(me, -1), where[8]))
    full_qk, full_ov = place_pair(ours, theirs, where)
    gains = full_qk[:, part : part + 2, :part].astype(F32)
    gain_one = gains[:, 0].reshape(1, width)
    gain_two = gains[:, 1].reshape(1, width)
    full_qk = full_qk.reshape(1024, columns)
    full_ov = full_ov.reshape(1024, columns)

    inverse_one = lax.rsqrt(jnp.mean(inputs * inputs, axis=-1, keepdims=True) + EPSILON)
    normed_one = inputs * inverse_one
    act_one = spread((normed_one * gain_one).astype(BF16))
    inverse_freq = ROPE_BASE ** (-(jnp.arange(HEAD // 2, dtype=F32) * 2.0 / HEAD))
    positions = (ctx * rows + jnp.arange(rows, dtype=jnp.int32)).astype(F32)
    angles = inverse_freq[:, None] * positions[None, :]
    cosine, sine = jnp.cos(angles), jnp.sin(angles)
    queries, local_kv = project(act_one, full_qk, full_ov, cosine, sine)
    kv_blocks = gather_earlier(local_kv)
    ff_parts, kv_blocks[5] = lax.optimization_barrier((ff_parts, kv_blocks[5]))
    ff_ours = exchange_parts(ff_parts, "fsdp")
    blocks = []
    for block in kv_blocks:
        blocks += [block, core_swap(block)]
    blocks, ff_ours = lax.optimization_barrier((blocks, ff_ours))
    ff_ours = place(ff_ours, where).reshape(1024, ff_part)
    ff_theirs = core_swap(ff_ours)
    gate_cols = jnp.where(first, ff_ours, ff_theirs)
    up_cols = jnp.where(first, ff_theirs, ff_ours)
    position = ctx.astype(jnp.int32).reshape(1)
    result, logs = attend(position, queries, blocks)
    attn = spread_rows(result.astype(BF16), part)
    hidden = inputs + contract(attn, full_ov, 0, 0)[:, :width]

    inverse_two = lax.rsqrt(jnp.mean(hidden * hidden, axis=-1, keepdims=True) + EPSILON)
    normed_two = hidden * inverse_two
    act_two = spread((normed_two * gain_two).astype(BF16))
    every = 8 * rows
    cot_all = lax.all_gather(spread(cot_late), "fsdp", axis=0, tiled=True)
    g_inner = contract(cot_all, spread(w_down), 1, 1)
    act_all = place(gather_blocks(act_two, "fsdp"), where).reshape(every, 1024)
    gate = contract(act_all, gate_cols, 1, 0)
    up = contract(act_all, up_cols, 1, 0)
    sigmoid = jax.nn.sigmoid(gate)
    silu = gate * sigmoid
    inner = (silu * up).astype(BF16)
    g_gate = (g_inner * up * sigmoid * (1.0 + gate * (1.0 - sigmoid))).astype(BF16)
    g_up = (g_inner * silu).astype(BF16)
    g_act_part = contract(g_gate, gate_cols, 1, 1) + contract(g_up, up_cols, 1, 1)
    g_act_parts = deal(g_act_part.astype(BF16).reshape(8, rows, 1024), steps_from(me, 1))
    g_act_two = reduce_terms(g_act_parts, "fsdp")
    unit = ff_part // 2
    gate_mine = contract(act_all, jnp.where(first, g_gate, g_up), 0, 0)
    gate_other = contract(act_all, jnp.where(first, g_up, g_gate), 0, 0)
    down_mine = contract(cot_all, jnp.where(first, inner[:, :unit], inner[:, unit:]), 0, 0)
    down_other = contract(cot_all, jnp.where(first, inner[:, unit:], inner[:, :unit]), 0, 0)
    gate_other, down_other = core_swap(gate_other.astype(BF16)), core_swap(down_other.astype(BF16))
    ff_sum = jnp.concatenate(
        [gate_mine + gate_other.astype(F32), down_mine + down_other.astype(F32)], axis=1
    ).astype(BF16)

    g_normed, gain_two_term = norm_back(
        unspread(g_act_two, part), normed_two, inverse_two, gain_two
    )
    g_hidden = cot.astype(F32) + g_normed
    g_hid = g_hidden.astype(BF16)
    g_hid_wide = jnp.pad(g_hid, ((0, 0), (0, columns - width)))
    g_attn = unspread_rows(contract(full_ov, g_hid_wide, 1, 1).astype(BF16), part)

    pair_at = chip % 2
    ring = jnp.stack([(chip // 2 + r) % 4 for r in range(4)]).astype(jnp.int32)
    pair = jnp.stack([pair_at, 1 - pair_at]).astype(jnp.int32)
    ff_parts = deal(ff_sum.reshape(4, 2, 128, -1), ring)
    g_attn, ff_parts = lax.optimization_barrier((g_attn, ff_parts))
    ff_sum = ring_sum(ff_parts)
    down_part = contract(inner, w_down, 1, 0).astype(BF16)
    down_part, g_hid = lax.optimization_barrier((down_part, g_hid))
    down = lax.psum_scatter(down_part, "fsdp", scatter_dimension=0, tiled=True)
    output = (hidden + down.astype(F32)).astype(BF16)

    g_query_rot, g_ours, g_theirs = attend_back(position, queries, g_attn, result, logs, blocks)
    g_theirs = core_swap(g_theirs)
    g_pairs = g_ours.astype(F32) + g_theirs.astype(F32)
    g_query = turn(g_query_rot, cosine, sine, -1.0).astype(BF16)
    g_kv = reduce_earlier([g_pairs[k] for k in range(8)])
    g_key = turn(g_kv[:KVWIDTH], cosine, sine, -1.0).astype(BF16)
    g_value = g_kv[KVWIDTH:].astype(BF16)
    g_qk = jnp.concatenate([g_query, g_key], axis=0)
    g_ov = jnp.pad(g_value, ((width, 0), (0, 0)))
    g_act_one = contract(g_qk, full_qk, 0, 1) + contract(g_ov, full_ov, 0, 1)
    g_inputs, gain_one_term = norm_back(
        unspread(g_act_one, part), normed_one, inverse_one, gain_one
    )
    input_grad = (g_hidden + g_inputs).astype(BF16)

    core = (ctx % 2).astype(jnp.int32).reshape(1)
    gain_terms = jnp.stack(
        [gain_one_term.reshape(8, part), gain_two_term.reshape(8, part)], axis=1
    )
    gain_terms = jnp.pad(gain_terms, ((0, 0), (0, 6), (0, 128 - part)))
    g_kv = jnp.concatenate([g_key, g_value], axis=0)
    mine, other = halves(core, act_one, g_query, attn, g_hid, g_kv, gain_terms)
    terms = add_terms(mine, core_swap(other), steps_from(me, 1))
    row_sum = reduce_terms(terms, "fsdp").astype(BF16)

    ff_sum, _ = lax.optimization_barrier((ff_sum, mine))
    ff_sum = ctx_gather(pair_sum(deal(ff_sum, pair)), ring, pair).reshape(1024, -1)
    sums = ring_sum(deal(row_sum.reshape(4, 2, 16, columns), ring))
    sums = ctx_gather(pair_sum(deal(sums, pair)), ring, pair).reshape(128, columns)
    sums_other = core_swap(sums)
    sums_zero = jnp.where(first, sums, sums_other).astype(F32)
    sums_one = jnp.where(first, sums_other, sums).astype(F32)

    ff_sum, _ = lax.optimization_barrier((ff_sum, row_sum))
    gate_sum, down_sum = ff_sum[:, :ff_part], ff_sum[:, ff_part:]
    ff_rows = deal(gate_sum.reshape(8, 128, ff_part), steps_from(me, -1))
    ff_rows = place(exchange_parts(ff_rows, "fsdp"), where)
    ff_rows = ff_rows[:, :part].transpose(1, 0, 2).reshape(part, 8 * ff_part)
    ff_other = core_swap(ff_rows)
    grad_gate = jnp.where(first, ff_rows, ff_other).astype(F32)
    grad_up = jnp.where(first, ff_other, ff_rows).astype(F32)
    down_other = core_swap(down_sum)
    grad_down = jnp.concatenate(
        [jnp.where(first, down_sum, down_other), jnp.where(first, down_other, down_sum)], axis=1
    )
    grad_down = unspread_rows(grad_down, part).T.astype(F32)
    split = WIDE_SPLIT
    return (
        output[None],
        input_grad[None],
        sums_zero[part, width : width + part],
        jnp.concatenate([sums_zero[:part, :split], sums_one[:part, split:width]], axis=1),
        sums_zero[:part, width:],
        sums_one[:part, width:],
        jnp.concatenate([sums_one[:part, :split], sums_zero[:part, split:width]], axis=1),
        sums_zero[part + 1, width : width + part],
        grad_gate,
        grad_up,
        grad_down,
    )


def solution(mesh):
    rows = P("fsdp", None)
    tokens = P("fsdp", "ctx", None)
    in_specs = (
        tokens,
        P("fsdp"),
        rows,
        rows,
        rows,
        rows,
        P("fsdp"),
        rows,
        rows,
        rows,
        tokens,
    )
    out_specs = (
        tokens,
        tokens,
        P("fsdp"),
        rows,
        rows,
        rows,
        rows,
        P("fsdp"),
        rows,
        rows,
        rows,
    )
    return jax.shard_map(body, mesh=mesh, in_specs=in_specs, out_specs=out_specs, check_vma=False)
```

```python
import functools

import jax
import jax.numpy as jnp
from jax import lax
from jax.experimental import pallas as pl
from jax.experimental.pallas import tpu as pltpu
from jax.sharding import PartitionSpec as P

HEADS = 15
KV_HEADS = 5
GROUP = HEADS // KV_HEADS
HEAD = 64
QWIDTH = HEADS * HEAD
KVWIDTH = KV_HEADS * HEAD

EPSILON = 1e-05
ROPE_BASE = 10000.0
MASK_VALUE = -1e30
SCALE = HEAD ** (-0.5)

BF16 = jnp.bfloat16
F32 = jnp.float32
WIDE_SPLIT = 512
VMEM_LIMIT = 48 * 1024 * 1024

STEPS = [(ring, pair) for ring in range(4) for pair in range(2)]


def moved(index, axis, ring, pair):
    low = 1 if axis == "fsdp" else 2
    core = index % low
    place = index // low
    place = ((place // 2 + ring) % 4) * 2 + (place % 2 + pair) % 2
    return place * low + core


def take(value, axis, ring, pair):
    size = 8 if axis == "fsdp" else 16
    return lax.ppermute(
        value, axis, [(i, moved(i, axis, -ring, pair)) for i in range(size)]
    )


def core_swap(value):
    return lax.ppermute(value, "ctx", [(i, i ^ 1) for i in range(16)])


def gather_blocks(value, axis):
    found = {(0, 0): value, (0, 1): take(value, axis, 0, 1)}
    found[1, 0] = take(value, axis, 1, 0)
    found[3, 0] = take(value, axis, 3, 0)
    found[1, 1] = take(found[0, 1], axis, 1, 0)
    found[3, 1] = take(found[0, 1], axis, 3, 0)
    found[2, 0] = take(found[1, 0], axis, 1, 0)
    found[2, 1] = take(found[3, 1], axis, 3, 0)
    return [found[step] for step in STEPS]


def steps_from(me, sign):
    return jnp.stack([moved(me, "fsdp", sign * ring, pair) for ring, pair in STEPS]).astype(
        jnp.int32
    )


def reduce_terms(terms, axis):
    term = dict(zip(STEPS, terms))

    def plus(first, *others):
        return sum((other.astype(F32) for other in others), first.astype(F32))

    one = plus(term[1, 0], take(term[2, 0], axis, 3, 0)).astype(BF16)
    three = plus(term[3, 1], take(term[2, 1], axis, 1, 0)).astype(BF16)
    pair = plus(term[0, 1], take(term[1, 1], axis, 3, 0), take(three, axis, 1, 0)).astype(BF16)
    total = plus(
        term[0, 0], take(term[3, 0], axis, 1, 0), take(one, axis, 3, 0), take(pair, axis, 0, 1)
    )
    return total, one, pair


def exchange_parts(parts, axis):
    return [parts[0]] + [take(part, axis, *step) for step, part in zip(STEPS[1:], parts[1:])]


def ring_sum(parts):
    return sum_parts(
        [parts[0]] + [take(parts[r], "ctx", 4 - r, 0) for r in range(1, 4)]
    ).astype(BF16)


def pair_sum(parts):
    return sum_parts([parts[0], take(parts[1], "ctx", 0, 1)]).astype(BF16)


def pair_gather(piece, pair):
    return place([piece, take(piece, "ctx", 0, 1)], pair)


def ring_gather(both):
    return [both] + [take(both, "ctx", r, 0) for r in range(1, 4)]


def sum_parts(parts):
    return sum((part.astype(F32) for part in parts[1:]), parts[0].astype(F32))


def later(value, ring):
    return take(value, "ctx", 4 - ring, 0)


def sooner(value, ring):
    return take(value, "ctx", ring, 0)


def gather_earlier(value):
    found = {(0, 0): value, (1, 0): later(value, 1)}
    found[0, 1] = take(value, "ctx", 0, 1)
    found[1, 1] = later(found[0, 1], 1)
    for p in range(2):
        found[3, p] = later(found[0, p], 3)
        found[2, p] = later(found[1, p], 1)
    return [found[step] for step in STEPS]


def reduce_earlier(terms):
    term = dict(zip(STEPS, terms))
    home = []
    for p in (1, 0):
        one = term[1, p] + sooner(term[2, p].astype(BF16), 1).astype(F32)
        total = term[0, p] + sooner(term[3, p].astype(BF16), 3).astype(F32)
        home.append(total + sooner(one.astype(BF16), 1).astype(F32))
    return home[1] + take(home[0].astype(BF16), "ctx", 0, 1).astype(F32)


def copy_all(pairs, semaphores):
    copies = [
        pltpu.make_async_copy(source, goal, semaphores.at[i])
        for i, (source, goal) in enumerate(pairs)
    ]
    for copy in copies:
        copy.start()
    for copy in copies:
        copy.wait()


def place_kernel(where_ref, *refs):
    blocks, out_ref, semaphores = refs[:-2], refs[-2], refs[-1]
    copy_all([(block, out_ref.at[where_ref[r]]) for r, block in enumerate(blocks)], semaphores)


def place(blocks, where):
    count, shape = len(blocks), blocks[0].shape
    return pl.pallas_call(
        place_kernel,
        out_shape=jax.ShapeDtypeStruct((count,) + shape, blocks[0].dtype),
        in_specs=[pl.BlockSpec(memory_space=pltpu.SMEM)]
        + [pl.BlockSpec(memory_space=pl.ANY)] * count,
        out_specs=pl.BlockSpec(memory_space=pltpu.VMEM),
        scratch_shapes=[pltpu.SemaphoreType.DMA((count,))],
        compiler_params=pltpu.CompilerParams(vmem_limit_bytes=VMEM_LIMIT),
        name="place",
    )(where, *blocks)


def deal_kernel(which_ref, source_ref, *refs):
    outs, semaphores = refs[:-1], refs[-1]
    copy_all([(source_ref.at[which_ref[r]], out) for r, out in enumerate(outs)], semaphores)


def deal(blocks, which):
    count = blocks.shape[0]
    shape = jax.ShapeDtypeStruct(blocks.shape[1:], blocks.dtype)
    return pl.pallas_call(
        deal_kernel,
        out_shape=[shape] * count,
        in_specs=[pl.BlockSpec(memory_space=pltpu.SMEM), pl.BlockSpec(memory_space=pl.ANY)],
        out_specs=[pl.BlockSpec(memory_space=pltpu.VMEM)] * count,
        scratch_shapes=[pltpu.SemaphoreType.DMA((count,))],
        compiler_params=pltpu.CompilerParams(vmem_limit_bytes=VMEM_LIMIT),
        name="deal",
    )(which, blocks)


def split_kernel(which_ref, gate_ref, up_ref, *refs):
    outs, blocks = refs[:8], refs[8]
    part, unit = gate_ref.shape[0], gate_ref.shape[1] // 8
    blocks[...] = jnp.zeros(blocks.shape, BF16)

    def lay(source):
        for t in range(8):
            blocks[t, :part] = source[:, t * unit : (t + 1) * unit]

    pl.when(which_ref[8] == 0)(lambda: lay(gate_ref))
    pl.when(which_ref[8] == 1)(lambda: lay(up_ref))
    for r, out in enumerate(outs):
        out[...] = blocks[which_ref[r]]


def split_columns(gate, up, which):
    shape = jax.ShapeDtypeStruct((128, gate.shape[1] // 8), BF16)
    return pl.pallas_call(
        split_kernel,
        out_shape=[shape] * 8,
        in_specs=[pl.BlockSpec(memory_space=pltpu.SMEM)]
        + [pl.BlockSpec(memory_space=pltpu.VMEM)] * 2,
        out_specs=[pl.BlockSpec(memory_space=pltpu.VMEM)] * 8,
        scratch_shapes=[pltpu.VMEM((8,) + shape.shape, BF16)],
        compiler_params=pltpu.CompilerParams(vmem_limit_bytes=VMEM_LIMIT),
        name="split_columns",
    )(which, gate, up)


def place_pair_kernel(where_ref, *refs):
    ours, theirs, zero_ref, one_ref, semaphores = refs[:8], refs[8:16], refs[16], refs[17], refs[18]

    def lay(zero, one):
        pairs = [(zero[r], zero_ref.at[where_ref[r]]) for r in range(8)]
        copy_all(pairs + [(one[r], one_ref.at[where_ref[r]]) for r in range(8)], semaphores)

    pl.when(where_ref[8] == 0)(lambda: lay(ours, theirs))
    pl.when(where_ref[8] == 1)(lambda: lay(theirs, ours))


def place_pair(ours, theirs, where):
    shape = (8,) + ours[0].shape
    return pl.pallas_call(
        place_pair_kernel,
        out_shape=[jax.ShapeDtypeStruct(shape, BF16)] * 2,
        in_specs=[pl.BlockSpec(memory_space=pltpu.SMEM)]
        + [pl.BlockSpec(memory_space=pl.ANY)] * 16,
        out_specs=[pl.BlockSpec(memory_space=pltpu.VMEM)] * 2,
        scratch_shapes=[pltpu.SemaphoreType.DMA((16,))],
        compiler_params=pltpu.CompilerParams(vmem_limit_bytes=VMEM_LIMIT),
        name="place_pair",
    )(where, *ours, *theirs)


def spread(value):
    rows = value.shape[0]
    groups = value.reshape(rows, 8, -1)
    return jnp.pad(groups, ((0, 0), (0, 0), (0, 128 - groups.shape[2]))).reshape(rows, 1024)


def unspread(value, part):
    rows = value.shape[0]
    return value.reshape(rows, 8, 128)[:, :, :part].reshape(rows, 8 * part)


def spread_rows(value, part):
    groups = value.reshape(8, part, -1)
    return jnp.pad(groups, ((0, 0), (0, 128 - part), (0, 0))).reshape(1024, -1)


def unspread_rows(value, part):
    return value.reshape(8, 128, -1)[:, :part].reshape(8 * part, -1)


def contract(left, right, left_dim, right_dim):
    return lax.dot_general(
        left, right, (((left_dim,), (right_dim,)), ((), ())), preferred_element_type=F32
    )


def lanes_of_group(ref, h):
    return jnp.concatenate(
        [ref[(GROUP * h + g) * HEAD : (GROUP * h + g + 1) * HEAD, :] for g in range(GROUP)], axis=1
    )


def allowed_at_home(rows, core):
    key = lax.broadcasted_iota(jnp.int32, (2 * rows, GROUP * rows), 0)
    query = lax.broadcasted_iota(jnp.int32, (2 * rows, GROUP * rows), 1) % rows
    return key <= jnp.where(key < rows, query, jnp.where(core == 1, 2 * rows, 0))


def present(ctx, k):
    x, z_hi = ctx // 4, (ctx // 2) % 2
    ring, pair = k // 2, k % 2
    return jnp.logical_and(x >= ring, jnp.logical_or(ring > 0, (z_hi + pair) % 2 < z_hi))


def keys_of(kv_s, k, h):
    return kv_s[k, h * HEAD : (h + 1) * HEAD, :]


def values_of(kv_s, k, h):
    return kv_s[k, KVWIDTH + h * HEAD : KVWIDTH + (h + 1) * HEAD, :]


def attend_kernel(ctx_ref, q_ref, *refs):
    blocks = refs[:16]
    out_ref, log_ref, kv_s, q_s, acc_s, max_s, sum_s = refs[16:]
    rows = q_ref.shape[1]
    ctx = ctx_ref[0]
    for k in range(8):
        kv_s[k, :, :rows] = blocks[2 * k][...]
        kv_s[k, :, rows:] = blocks[2 * k + 1][...]
    for h in range(KV_HEADS):
        q_s[h] = lanes_of_group(q_ref, h) * BF16(SCALE)

    allowed = allowed_at_home(rows, ctx % 2)
    for h in range(KV_HEADS):
        scores = jnp.where(allowed, contract(keys_of(kv_s, 0, h), q_s[h], 0, 0), MASK_VALUE)
        top = jnp.max(scores, axis=0, keepdims=True)
        weights = jnp.exp(scores - top)
        max_s[h] = top
        sum_s[h] = jnp.sum(weights, axis=0, keepdims=True)
        acc_s[h] = contract(values_of(kv_s, 0, h), weights.astype(BF16), 1, 0)

    def absorb(k):
        for h in range(KV_HEADS):
            scores = contract(keys_of(kv_s, k, h), q_s[h], 0, 0)
            old = max_s[h]
            top = jnp.maximum(old, jnp.max(scores, axis=0, keepdims=True))
            weights = jnp.exp(scores - top)
            factor = jnp.exp(old - top)
            max_s[h] = top
            sum_s[h] = sum_s[h] * factor + jnp.sum(weights, axis=0, keepdims=True)
            acc_s[h] = acc_s[h] * factor + contract(
                values_of(kv_s, k, h), weights.astype(BF16), 1, 0
            )

    def step(k, carry):
        pl.when(present(ctx, k))(functools.partial(absorb, k))
        return carry

    lax.fori_loop(1, 8, step, 0)
    for h in range(KV_HEADS):
        result = acc_s[h] / sum_s[h]
        logs = max_s[h] + jnp.log(sum_s[h])
        for g in range(GROUP):
            head = GROUP * h + g
            out_ref[head * HEAD : (head + 1) * HEAD, :] = result[:, g * rows : (g + 1) * rows]
            log_ref[head : head + 1, :] = logs[:, g * rows : (g + 1) * rows]


def attend(ctx, queries, blocks):
    rows = queries.shape[1]
    return pl.pallas_call(
        attend_kernel,
        out_shape=[
            jax.ShapeDtypeStruct((QWIDTH, rows), F32),
            jax.ShapeDtypeStruct((HEADS, rows), F32),
        ],
        in_specs=[pl.BlockSpec(memory_space=pltpu.SMEM)]
        + [pl.BlockSpec(memory_space=pltpu.VMEM)] * 17,
        out_specs=[pl.BlockSpec(memory_space=pltpu.VMEM)] * 2,
        scratch_shapes=[
            pltpu.VMEM((8, 2 * KVWIDTH, 2 * rows), BF16),
            pltpu.VMEM((KV_HEADS, HEAD, GROUP * rows), BF16),
            pltpu.VMEM((KV_HEADS, HEAD, GROUP * rows), F32),
            pltpu.VMEM((KV_HEADS, 1, GROUP * rows), F32),
            pltpu.VMEM((KV_HEADS, 1, GROUP * rows), F32),
        ],
        compiler_params=pltpu.CompilerParams(vmem_limit_bytes=VMEM_LIMIT),
        cost_estimate=pl.CostEstimate(
            flops=14000000000, bytes_accessed=5000000, transcendentals=4000000
        ),
        name="attend",
    )(ctx, queries, *blocks)


def attend_back_kernel(ctx_ref, q_ref, g_ref, out_ref, log_ref, *refs):
    blocks = refs[:16]
    gq_ref, ours_ref, theirs_ref, kv_s, q_s, g_s, gq_s, log_s, delta_s = refs[16:]
    rows = q_ref.shape[1]
    ctx = ctx_ref[0]
    for k in range(8):
        kv_s[k, :, :rows] = blocks[2 * k][...]
        kv_s[k, :, rows:] = blocks[2 * k + 1][...]
    for h in range(KV_HEADS):
        q_s[h] = lanes_of_group(q_ref, h) * BF16(SCALE)
        grads = lanes_of_group(g_ref, h)
        g_s[h] = grads
        delta_s[h] = jnp.sum(
            grads.astype(F32) * lanes_of_group(out_ref, h), axis=0, keepdims=True
        )
        log_s[h] = jnp.concatenate(
            [log_ref[GROUP * h + g : GROUP * h + g + 1, :] for g in range(GROUP)], axis=1
        )

    def absorb(k, h, allowed):
        keys = keys_of(kv_s, k, h)
        probs = jnp.exp(contract(keys, q_s[h], 0, 0) - log_s[h])
        if allowed is not None:
            probs = jnp.where(allowed, probs, 0.0)
        g_probs = contract(values_of(kv_s, k, h), g_s[h], 0, 0)
        g_scores = (probs * (g_probs - delta_s[h])).astype(BF16)
        g_keys = contract(q_s[h], g_scores, 1, 1).astype(BF16)
        g_values = contract(g_s[h], probs.astype(BF16), 1, 1).astype(BF16)
        for at, grads in ((h * HEAD, g_keys), (KVWIDTH + h * HEAD, g_values)):
            ours_ref[k, at : at + HEAD, :] = grads[:, :rows]
            theirs_ref[k, at : at + HEAD, :] = grads[:, rows:]
        return contract(keys, g_scores, 1, 0)

    allowed = allowed_at_home(rows, ctx % 2)
    for h in range(KV_HEADS):
        gq_s[h] = absorb(0, h, allowed)

    def step(k, carry):
        here = present(ctx, k)

        @pl.when(here)
        def _():
            for h in range(KV_HEADS):
                gq_s[h] += absorb(k, h, None)

        @pl.when(jnp.logical_not(here))
        def _():
            ours_ref[k] = jnp.zeros(ours_ref.shape[1:], BF16)
            theirs_ref[k] = jnp.zeros(theirs_ref.shape[1:], BF16)

        return carry

    lax.fori_loop(1, 8, step, 0)
    for h in range(KV_HEADS):
        result = gq_s[h] * SCALE
        for g in range(GROUP):
            head = GROUP * h + g
            gq_ref[head * HEAD : (head + 1) * HEAD, :] = result[:, g * rows : (g + 1) * rows]


def attend_back(ctx, queries, grads, result, logs, blocks):
    rows = queries.shape[1]
    half = jax.ShapeDtypeStruct((8, 2 * KVWIDTH, rows), BF16)
    wide = (KV_HEADS, HEAD, GROUP * rows)
    return pl.pallas_call(
        attend_back_kernel,
        out_shape=[jax.ShapeDtypeStruct((QWIDTH, rows), F32), half, half],
        in_specs=[pl.BlockSpec(memory_space=pltpu.SMEM)]
        + [pl.BlockSpec(memory_space=pltpu.VMEM)] * 20,
        out_specs=[pl.BlockSpec(memory_space=pltpu.VMEM)] * 3,
        scratch_shapes=[
            pltpu.VMEM((8, 2 * KVWIDTH, 2 * rows), BF16),
            pltpu.VMEM(wide, BF16),
            pltpu.VMEM(wide, BF16),
            pltpu.VMEM(wide, F32),
            pltpu.VMEM((KV_HEADS, 1, GROUP * rows), F32),
            pltpu.VMEM((KV_HEADS, 1, GROUP * rows), F32),
        ],
        compiler_params=pltpu.CompilerParams(vmem_limit_bytes=VMEM_LIMIT),
        cost_estimate=pl.CostEstimate(
            flops=18000000000, bytes_accessed=5000000, transcendentals=4000000
        ),
        name="attend_back",
    )(ctx, queries, grads, result, logs, *blocks)


def turn(heads, cosine, sine, sign):
    parts = heads.reshape(-1, 2, HEAD // 2, heads.shape[-1])
    first, second = parts[:, 0], parts[:, 1]
    sine = sign * sine
    return jnp.stack(
        [first * cosine - second * sine, second * cosine + first * sine], axis=1
    ).reshape(heads.shape)


def project_kernel(act_ref, qk_ref, ov_ref, cos_ref, sin_ref, q_ref, kv_ref, v_s, semaphore):
    start = QWIDTH // 128 * 128
    copy = pltpu.make_async_copy(ov_ref.at[:, start:], v_s, semaphore)
    copy.start()
    cosine, sine = cos_ref[...], sin_ref[...]
    half = HEAD // 2
    turned = contract(act_ref[...], qk_ref[...], 1, 0).T
    for head in range(HEADS + KV_HEADS):
        first = turned[head * HEAD : head * HEAD + half]
        second = turned[head * HEAD + half : (head + 1) * HEAD]
        goal = q_ref if head < HEADS else kv_ref
        at = (head if head < HEADS else head - HEADS) * HEAD
        goal[at : at + half] = (first * cosine - second * sine).astype(BF16)
        goal[at + half : at + HEAD] = (second * cosine + first * sine).astype(BF16)
    copy.wait()
    values = contract(act_ref[...], v_s[...], 1, 0).T
    kv_ref[KVWIDTH:] = values[QWIDTH - start :].astype(BF16)


def project(act, full_qk, full_ov, cosine, sine):
    rows = act.shape[0]
    spec = pl.BlockSpec(memory_space=pltpu.VMEM)
    tail = full_ov.shape[1] - QWIDTH // 128 * 128
    return pl.pallas_call(
        project_kernel,
        out_shape=[
            jax.ShapeDtypeStruct((QWIDTH, rows), BF16),
            jax.ShapeDtypeStruct((2 * KVWIDTH, rows), BF16),
        ],
        in_specs=[spec, spec, pl.BlockSpec(memory_space=pl.ANY), spec, spec],
        out_specs=[spec, spec],
        scratch_shapes=[pltpu.VMEM((full_ov.shape[0], tail), BF16), pltpu.SemaphoreType.DMA],
        compiler_params=pltpu.CompilerParams(vmem_limit_bytes=VMEM_LIMIT),
        name="project",
    )(act, full_qk, full_ov, cosine, sine)


def store_halves(core, mine_ref, other_ref, t, zero, one):
    @pl.when(core == 0)
    def _():
        mine_ref[t] = zero
        other_ref[t] = one

    @pl.when(core == 1)
    def _():
        mine_ref[t] = one
        other_ref[t] = zero


def halves_kernel(
    core_ref, act_ref, query_ref, attn_ref, hid_ref, kv_ref, gain_ref, mine_ref, other_ref
):
    split = WIDE_SPLIT
    for t in range(8):
        at = slice(t * 128, (t + 1) * 128)
        act = act_ref[:, at]
        query = contract(act, query_ref[...], 0, 1).astype(BF16)
        out = contract(attn_ref[at], hid_ref[...], 1, 0).astype(BF16)
        key = contract(act, kv_ref[:KVWIDTH], 0, 1)
        value = contract(act, kv_ref[KVWIDTH:], 0, 1).astype(BF16)
        gains = jnp.concatenate([jnp.zeros((120, 128), F32), gain_ref[t]], axis=0)
        key = jnp.concatenate([key[:, :128] + gains, key[:, 128:]], axis=1).astype(BF16)
        zero = jnp.concatenate([query[:, :split], out[:, split:], key], axis=1)
        one = jnp.concatenate([out[:, :split], query[:, split:], value], axis=1)
        store_halves(core_ref[0], mine_ref, other_ref, t, zero, one)


def halves(core, act, query, attn, hid, kv, gains):
    shape = jax.ShapeDtypeStruct((8, 128, QWIDTH + KVWIDTH), BF16)
    return pl.pallas_call(
        halves_kernel,
        out_shape=[shape, shape],
        in_specs=[pl.BlockSpec(memory_space=pltpu.SMEM)]
        + [pl.BlockSpec(memory_space=pltpu.VMEM)] * 6,
        out_specs=[pl.BlockSpec(memory_space=pltpu.VMEM)] * 2,
        compiler_params=pltpu.CompilerParams(vmem_limit_bytes=VMEM_LIMIT),
        name="halves",
    )(core, act, query, attn, hid, kv, gains)


def add_kernel(which_ref, mine_ref, other_ref, *outs):
    for r, out in enumerate(outs):
        at = which_ref[r]
        out[...] = (mine_ref[at].astype(F32) + other_ref[at].astype(F32)).astype(BF16)


def add_terms(mine, other, which):
    shape = jax.ShapeDtypeStruct(mine.shape[1:], BF16)
    return pl.pallas_call(
        add_kernel,
        out_shape=[shape] * 8,
        in_specs=[pl.BlockSpec(memory_space=pltpu.SMEM)]
        + [pl.BlockSpec(memory_space=pltpu.VMEM)] * 2,
        out_specs=[pl.BlockSpec(memory_space=pltpu.VMEM)] * 8,
        compiler_params=pltpu.CompilerParams(vmem_limit_bytes=VMEM_LIMIT),
        name="add_terms",
    )(which, mine, other)


def norm_back(grad, normed, inverse, gain):
    scaled = grad * gain
    mean = jnp.mean(scaled * normed, axis=-1, keepdims=True)
    return inverse * (scaled - normed * mean), jnp.sum(grad * normed, axis=0)


def body(
    tokens, norm_attn, w_query, w_key, w_value, w_out, norm_ffn, w_gate, w_up, w_down, cotangent
):
    rows, width = tokens.shape[1:]
    part = norm_attn.shape[0]
    ff_part = w_down.shape[0]
    ctx = lax.axis_index("ctx")
    me = lax.axis_index("fsdp")
    chip = ctx // 2
    first = ctx % 2 == 0
    inputs = tokens.reshape(rows, width).astype(F32)
    cot = cotangent.reshape(rows, width)
    ahead = [moved(me, "fsdp", *step) for step in STEPS]
    where = jnp.stack(ahead + [ctx % 2]).astype(jnp.int32)
    chips_ahead = [moved(chip, "fsdp", *step) for step in STEPS]
    chip_where = jnp.stack(chips_ahead).astype(jnp.int32)

    half = jnp.where(
        first,
        jnp.concatenate([w_query, w_key], axis=1),
        jnp.concatenate([w_out, w_value], axis=1),
    )
    columns = half.shape[1]
    gain_rows = jnp.zeros((128 - part, columns), BF16)
    gain_rows = gain_rows.at[0, :part].set(norm_attn).at[1, :part].set(norm_ffn)
    ours = gather_blocks(jnp.concatenate([half, gain_rows], axis=0), "fsdp")
    theirs = [core_swap(block) for block in ours]
    cot_late, _ = lax.optimization_barrier((cot, ours[7]))
    ff_parts = split_columns(w_gate, w_up, jnp.append(steps_from(me, -1), where[8]))
    full_qk, full_ov = place_pair(ours, theirs, where)
    gains = full_qk[:, part : part + 2, :part].astype(F32)
    gain_one = gains[:, 0].reshape(1, width)
    gain_two = gains[:, 1].reshape(1, width)
    full_qk = full_qk.reshape(1024, columns)
    full_ov = full_ov.reshape(1024, columns)

    inverse_one = lax.rsqrt(jnp.mean(inputs * inputs, axis=-1, keepdims=True) + EPSILON)
    normed_one = inputs * inverse_one
    act_one = spread((normed_one * gain_one).astype(BF16))
    inverse_freq = ROPE_BASE ** (-(jnp.arange(HEAD // 2, dtype=F32) * 2.0 / HEAD))
    positions = (ctx * rows + jnp.arange(rows, dtype=jnp.int32)).astype(F32)
    angles = inverse_freq[:, None] * positions[None, :]
    cosine, sine = jnp.cos(angles), jnp.sin(angles)
    queries, local_kv = project(act_one, full_qk, full_ov, cosine, sine)
    kv_blocks = gather_earlier(local_kv)
    ff_parts, kv_blocks[5] = lax.optimization_barrier((ff_parts, kv_blocks[5]))
    ff_ours = exchange_parts(ff_parts, "fsdp")
    blocks = []
    for block in kv_blocks:
        blocks += [block, core_swap(block)]
    blocks, ff_ours = lax.optimization_barrier((blocks, ff_ours))
    ff_ours = place(ff_ours, where).reshape(1024, ff_part)
    ff_theirs = core_swap(ff_ours)
    gate_cols = jnp.where(first, ff_ours, ff_theirs)
    up_cols = jnp.where(first, ff_theirs, ff_ours)
    position = ctx.astype(jnp.int32).reshape(1)
    result, logs = attend(position, queries, blocks)
    attn = spread_rows(result.astype(BF16), part)
    hidden = inputs + contract(attn, full_ov, 0, 0)[:, :width]

    inverse_two = lax.rsqrt(jnp.mean(hidden * hidden, axis=-1, keepdims=True) + EPSILON)
    normed_two = hidden * inverse_two
    act_two = spread((normed_two * gain_two).astype(BF16))
    every = 8 * rows
    cot_all = lax.all_gather(spread(cot_late), "fsdp", axis=0, tiled=True)
    g_inner = contract(cot_all, spread(w_down), 1, 1)
    act_all = place(gather_blocks(act_two, "fsdp"), where).reshape(every, 1024)
    gate = contract(act_all, gate_cols, 1, 0)
    up = contract(act_all, up_cols, 1, 0)
    sigmoid = jax.nn.sigmoid(gate)
    silu = gate * sigmoid
    inner = (silu * up).astype(BF16)
    g_gate = (g_inner * up * sigmoid * (1.0 + gate * (1.0 - sigmoid))).astype(BF16)
    g_up = (g_inner * silu).astype(BF16)
    g_act_part = contract(g_gate, gate_cols, 1, 1) + contract(g_up, up_cols, 1, 1)
    g_act_parts = deal(g_act_part.astype(BF16).reshape(8, rows, 1024), steps_from(me, 1))
    g_act_two = reduce_terms(g_act_parts, "fsdp")[0]
    unit = ff_part // 2
    gate_mine = contract(act_all, jnp.where(first, g_gate, g_up), 0, 0)
    gate_other = contract(act_all, jnp.where(first, g_up, g_gate), 0, 0)
    down_mine = contract(cot_all, jnp.where(first, inner[:, :unit], inner[:, unit:]), 0, 0)
    down_other = contract(cot_all, jnp.where(first, inner[:, unit:], inner[:, :unit]), 0, 0)
    gate_other, down_other = core_swap(gate_other.astype(BF16)), core_swap(down_other.astype(BF16))
    ff_sum = jnp.concatenate(
        [gate_mine + gate_other.astype(F32), down_mine + down_other.astype(F32)], axis=1
    ).astype(BF16)

    g_normed, gain_two_term = norm_back(
        unspread(g_act_two, part), normed_two, inverse_two, gain_two
    )
    g_hidden = cot.astype(F32) + g_normed
    g_hid = g_hidden.astype(BF16)
    g_hid_wide = jnp.pad(g_hid, ((0, 0), (0, columns - width)))
    g_attn = unspread_rows(contract(full_ov, g_hid_wide, 1, 1).astype(BF16), part)

    pair_at = chip % 2
    ring = jnp.stack([(chip // 2 + r) % 4 for r in range(4)]).astype(jnp.int32)
    pair = jnp.stack([pair_at, 1 - pair_at]).astype(jnp.int32)
    ff_parts = deal(ff_sum.reshape(4, 2, 128, -1), ring)
    g_attn, ff_parts = lax.optimization_barrier((g_attn, ff_parts))
    ff_sum = ring_sum(ff_parts)
    down_part = contract(inner, w_down, 1, 0).astype(BF16)
    down = lax.psum_scatter(down_part, "fsdp", scatter_dimension=0, tiled=True)

    g_query_rot, g_ours, g_theirs = attend_back(position, queries, g_attn, result, logs, blocks)
    g_theirs = core_swap(g_theirs)
    g_pairs = g_ours.astype(F32) + g_theirs.astype(F32)
    g_query = turn(g_query_rot, cosine, sine, -1.0).astype(BF16)
    ff_sum, _ = lax.optimization_barrier((ff_sum, g_theirs))
    ff_sum = pair_gather(pair_sum(deal(ff_sum, pair)), pair)
    g_kv = reduce_earlier([g_pairs[k] for k in range(8)])
    g_kv, down, ff_sum = lax.optimization_barrier((g_kv, down, ff_sum))
    output = (hidden + down.astype(F32)).astype(BF16)
    g_key = turn(g_kv[:KVWIDTH], cosine, sine, -1.0).astype(BF16)
    g_value = g_kv[KVWIDTH:].astype(BF16)
    g_qk = jnp.concatenate([g_query, g_key], axis=0)
    g_ov = jnp.pad(g_value, ((width, 0), (0, 0)))
    g_act_one = contract(g_qk, full_qk, 0, 1) + contract(g_ov, full_ov, 0, 1)
    g_inputs, gain_one_term = norm_back(
        unspread(g_act_one, part), normed_one, inverse_one, gain_one
    )
    input_grad = (g_hidden + g_inputs).astype(BF16)

    core = (ctx % 2).astype(jnp.int32).reshape(1)
    gain_terms = jnp.stack(
        [gain_one_term.reshape(8, part), gain_two_term.reshape(8, part)], axis=1
    )
    gain_terms = jnp.pad(gain_terms, ((0, 0), (0, 6), (0, 128 - part)))
    g_kv = jnp.concatenate([g_key, g_value], axis=0)
    mine, other = halves(core, act_one, g_query, attn, g_hid, g_kv, gain_terms)
    terms = add_terms(mine, core_swap(other), steps_from(me, 1))
    row_sum, one, last = reduce_terms(terms, "fsdp")
    row_sum = row_sum.astype(BF16)

    sums = ring_sum(deal(row_sum.reshape(4, 2, 16, columns), ring))
    sums = pair_gather(pair_sum(deal(sums, pair)), pair)
    sums = place(ring_gather(sums), ring).reshape(128, columns)
    sums_other = core_swap(sums)
    sums_zero = jnp.where(first, sums, sums_other).astype(F32)
    sums_one = jnp.where(first, sums_other, sums).astype(F32)

    ff_sum, _ = lax.optimization_barrier((ff_sum, one))
    ff_sum, _ = lax.optimization_barrier((ring_gather(ff_sum), last))
    ff_sum = place(ff_sum, ring).reshape(1024, -1)
    gate_sum, down_sum = ff_sum[:, :ff_part], ff_sum[:, ff_part:]
    ff_rows = deal(gate_sum.reshape(8, 128, ff_part), steps_from(me, -1))
    ff_rows = place(exchange_parts(ff_rows, "fsdp"), where)
    ff_rows = ff_rows[:, :part].transpose(1, 0, 2).reshape(part, 8 * ff_part)
    ff_other = core_swap(ff_rows)
    grad_gate = jnp.where(first, ff_rows, ff_other).astype(F32)
    grad_up = jnp.where(first, ff_other, ff_rows).astype(F32)
    down_other = core_swap(down_sum)
    grad_down = jnp.concatenate(
        [jnp.where(first, down_sum, down_other), jnp.where(first, down_other, down_sum)], axis=1
    )
    grad_down = unspread_rows(grad_down, part).T.astype(F32)
    split = WIDE_SPLIT
    return (
        output[None],
        input_grad[None],
        sums_zero[part, width : width + part],
        jnp.concatenate([sums_zero[:part, :split], sums_one[:part, split:width]], axis=1),
        sums_zero[:part, width:],
        sums_one[:part, width:],
        jnp.concatenate([sums_one[:part, :split], sums_zero[:part, split:width]], axis=1),
        sums_zero[part + 1, width : width + part],
        grad_gate,
        grad_up,
        grad_down,
    )


def solution(mesh):
    rows = P("fsdp", None)
    tokens = P("fsdp", "ctx", None)
    in_specs = (
        tokens,
        P("fsdp"),
        rows,
        rows,
        rows,
        rows,
        P("fsdp"),
        rows,
        rows,
        rows,
        tokens,
    )
    out_specs = (
        tokens,
        tokens,
        P("fsdp"),
        rows,
        rows,
        rows,
        rows,
        P("fsdp"),
        rows,
        rows,
        rows,
    )
    return jax.shard_map(body, mesh=mesh, in_specs=in_specs, out_specs=out_specs, check_vma=False)
```

```python
import functools

import jax
import jax.numpy as jnp
from jax import lax
from jax.experimental import pallas as pl
from jax.experimental.pallas import tpu as pltpu
from jax.sharding import PartitionSpec as P

HEADS = 15
KV_HEADS = 5
GROUP = HEADS // KV_HEADS
HEAD = 64
QWIDTH = HEADS * HEAD
KVWIDTH = KV_HEADS * HEAD

EPSILON = 1e-05
ROPE_BASE = 10000.0
MASK_VALUE = -1e30
SCALE = HEAD ** (-0.5)

BF16 = jnp.bfloat16
F32 = jnp.float32
WIDE_SPLIT = 512
VMEM_LIMIT = 48 * 1024 * 1024

STEPS = [(ring, pair) for ring in range(4) for pair in range(2)]


def moved(index, axis, ring, pair):
    low = 1 if axis == "fsdp" else 2
    core = index % low
    place = index // low
    place = ((place // 2 + ring) % 4) * 2 + (place % 2 + pair) % 2
    return place * low + core


def take(value, axis, ring, pair):
    size = 8 if axis == "fsdp" else 16
    return lax.ppermute(
        value, axis, [(i, moved(i, axis, -ring, pair)) for i in range(size)]
    )


def core_swap(value):
    return lax.ppermute(value, "ctx", [(i, i ^ 1) for i in range(16)])


def gather_blocks(value, axis):
    found = {(0, 0): value, (0, 1): take(value, axis, 0, 1)}
    found[1, 0] = take(value, axis, 1, 0)
    found[3, 0] = take(value, axis, 3, 0)
    found[1, 1] = take(found[0, 1], axis, 1, 0)
    found[3, 1] = take(found[0, 1], axis, 3, 0)
    found[2, 0] = take(found[1, 0], axis, 1, 0)
    found[2, 1] = take(found[3, 1], axis, 3, 0)
    return [found[step] for step in STEPS]


def steps_from(me, sign):
    return jnp.stack([moved(me, "fsdp", sign * ring, pair) for ring, pair in STEPS]).astype(
        jnp.int32
    )


def reduce_terms(terms, axis):
    term = dict(zip(STEPS, terms))

    def plus(first, *others):
        return sum((other.astype(F32) for other in others), first.astype(F32))

    one = plus(term[1, 0], take(term[2, 0], axis, 3, 0)).astype(BF16)
    three = plus(term[3, 1], take(term[2, 1], axis, 1, 0)).astype(BF16)
    pair = plus(term[0, 1], take(term[1, 1], axis, 3, 0), take(three, axis, 1, 0)).astype(BF16)
    last = [term[0, 0], take(term[3, 0], axis, 1, 0), take(one, axis, 3, 0), take(pair, axis, 0, 1)]
    return last, one, pair


def exchange_parts(parts, axis):
    return [parts[0]] + [take(part, axis, *step) for step, part in zip(STEPS[1:], parts[1:])]


def ring_sum(parts):
    return sum_parts(
        [parts[0]] + [take(parts[r], "ctx", 4 - r, 0) for r in range(1, 4)]
    ).astype(BF16)


def pair_sum(parts):
    return sum_parts([parts[0], take(parts[1], "ctx", 0, 1)]).astype(BF16)


def pair_gather(piece, pair):
    return place([piece, take(piece, "ctx", 0, 1)], pair)


def ring_gather(both):
    return [both] + [take(both, "ctx", r, 0) for r in range(1, 4)]


def sum_parts(parts):
    return sum((part.astype(F32) for part in parts[1:]), parts[0].astype(F32))


def later(value, ring):
    return take(value, "ctx", 4 - ring, 0)


def sooner(value, ring):
    return take(value, "ctx", ring, 0)


def gather_earlier(value):
    found = {(0, 0): value, (1, 0): later(value, 1)}
    found[0, 1] = take(value, "ctx", 0, 1)
    found[1, 1] = later(found[0, 1], 1)
    for p in range(2):
        found[3, p] = later(found[0, p], 3)
        found[2, p] = later(found[1, p], 1)
    return [found[step] for step in STEPS]


def reduce_earlier(terms):
    term = dict(zip(STEPS, terms))
    home = []
    for p in (1, 0):
        one = term[1, p] + sooner(term[2, p].astype(BF16), 1).astype(F32)
        total = term[0, p] + sooner(term[3, p].astype(BF16), 3).astype(F32)
        home.append(total + sooner(one.astype(BF16), 1).astype(F32))
    return home[1] + take(home[0].astype(BF16), "ctx", 0, 1).astype(F32)


def copy_all(pairs, semaphores):
    copies = [
        pltpu.make_async_copy(source, goal, semaphores.at[i])
        for i, (source, goal) in enumerate(pairs)
    ]
    for copy in copies:
        copy.start()
    for copy in copies:
        copy.wait()


def place_kernel(where_ref, *refs):
    blocks, out_ref, semaphores = refs[:-2], refs[-2], refs[-1]
    copy_all([(block, out_ref.at[where_ref[r]]) for r, block in enumerate(blocks)], semaphores)


def place(blocks, where):
    count, shape = len(blocks), blocks[0].shape
    return pl.pallas_call(
        place_kernel,
        out_shape=jax.ShapeDtypeStruct((count,) + shape, blocks[0].dtype),
        in_specs=[pl.BlockSpec(memory_space=pltpu.SMEM)]
        + [pl.BlockSpec(memory_space=pl.ANY)] * count,
        out_specs=pl.BlockSpec(memory_space=pltpu.VMEM),
        scratch_shapes=[pltpu.SemaphoreType.DMA((count,))],
        compiler_params=pltpu.CompilerParams(vmem_limit_bytes=VMEM_LIMIT),
        name="place",
    )(where, *blocks)


def deal_kernel(which_ref, source_ref, *refs):
    outs, semaphores = refs[:-1], refs[-1]
    copy_all([(source_ref.at[which_ref[r]], out) for r, out in enumerate(outs)], semaphores)


def deal(blocks, which):
    count = blocks.shape[0]
    shape = jax.ShapeDtypeStruct(blocks.shape[1:], blocks.dtype)
    return pl.pallas_call(
        deal_kernel,
        out_shape=[shape] * count,
        in_specs=[pl.BlockSpec(memory_space=pltpu.SMEM), pl.BlockSpec(memory_space=pl.ANY)],
        out_specs=[pl.BlockSpec(memory_space=pltpu.VMEM)] * count,
        scratch_shapes=[pltpu.SemaphoreType.DMA((count,))],
        compiler_params=pltpu.CompilerParams(vmem_limit_bytes=VMEM_LIMIT),
        name="deal",
    )(which, blocks)


def split_kernel(which_ref, gate_ref, up_ref, *refs):
    outs, blocks = refs[:8], refs[8]
    part, unit = gate_ref.shape[0], gate_ref.shape[1] // 8
    blocks[...] = jnp.zeros(blocks.shape, BF16)

    def lay(source):
        for t in range(8):
            blocks[t, :part] = source[:, t * unit : (t + 1) * unit]

    pl.when(which_ref[8] == 0)(lambda: lay(gate_ref))
    pl.when(which_ref[8] == 1)(lambda: lay(up_ref))
    for r, out in enumerate(outs):
        out[...] = blocks[which_ref[r]]


def split_columns(gate, up, which):
    shape = jax.ShapeDtypeStruct((128, gate.shape[1] // 8), BF16)
    return pl.pallas_call(
        split_kernel,
        out_shape=[shape] * 8,
        in_specs=[pl.BlockSpec(memory_space=pltpu.SMEM)]
        + [pl.BlockSpec(memory_space=pltpu.VMEM)] * 2,
        out_specs=[pl.BlockSpec(memory_space=pltpu.VMEM)] * 8,
        scratch_shapes=[pltpu.VMEM((8,) + shape.shape, BF16)],
        compiler_params=pltpu.CompilerParams(vmem_limit_bytes=VMEM_LIMIT),
        name="split_columns",
    )(which, gate, up)


def place_pair_kernel(where_ref, *refs):
    ours, theirs, zero_ref, one_ref, semaphores = refs[:8], refs[8:16], refs[16], refs[17], refs[18]

    def lay(zero, one):
        pairs = [(zero[r], zero_ref.at[where_ref[r]]) for r in range(8)]
        copy_all(pairs + [(one[r], one_ref.at[where_ref[r]]) for r in range(8)], semaphores)

    pl.when(where_ref[8] == 0)(lambda: lay(ours, theirs))
    pl.when(where_ref[8] == 1)(lambda: lay(theirs, ours))


def place_pair(ours, theirs, where):
    shape = (8,) + ours[0].shape
    return pl.pallas_call(
        place_pair_kernel,
        out_shape=[jax.ShapeDtypeStruct(shape, BF16)] * 2,
        in_specs=[pl.BlockSpec(memory_space=pltpu.SMEM)]
        + [pl.BlockSpec(memory_space=pl.ANY)] * 16,
        out_specs=[pl.BlockSpec(memory_space=pltpu.VMEM)] * 2,
        scratch_shapes=[pltpu.SemaphoreType.DMA((16,))],
        compiler_params=pltpu.CompilerParams(vmem_limit_bytes=VMEM_LIMIT),
        name="place_pair",
    )(where, *ours, *theirs)


def spread(value):
    rows = value.shape[0]
    groups = value.reshape(rows, 8, -1)
    return jnp.pad(groups, ((0, 0), (0, 0), (0, 128 - groups.shape[2]))).reshape(rows, 1024)


def unspread(value, part):
    rows = value.shape[0]
    return value.reshape(rows, 8, 128)[:, :, :part].reshape(rows, 8 * part)


def unspread_kernel(*refs):
    parts, out_ref = refs[:-1], refs[-1]
    part = out_ref.shape[1] // 8
    total = sum((ref[...].astype(F32) for ref in parts[1:]), parts[0][...].astype(F32))
    for t in range(8):
        out_ref[:, t * part : (t + 1) * part] = total[:, t * 128 : t * 128 + part]


def sum_unspread(parts, part):
    return pl.pallas_call(
        unspread_kernel,
        out_shape=jax.ShapeDtypeStruct((parts[0].shape[0], 8 * part), F32),
        in_specs=[pl.BlockSpec(memory_space=pltpu.VMEM)] * len(parts),
        out_specs=pl.BlockSpec(memory_space=pltpu.VMEM),
        compiler_params=pltpu.CompilerParams(vmem_limit_bytes=VMEM_LIMIT),
        name="sum_unspread",
    )(*parts)


def spread_rows(value, part):
    groups = value.reshape(8, part, -1)
    return jnp.pad(groups, ((0, 0), (0, 128 - part), (0, 0))).reshape(1024, -1)


def unspread_rows(value, part):
    return value.reshape(8, 128, -1)[:, :part].reshape(8 * part, -1)


def contract(left, right, left_dim, right_dim):
    return lax.dot_general(
        left, right, (((left_dim,), (right_dim,)), ((), ())), preferred_element_type=F32
    )


def lanes_of_group(ref, h):
    return jnp.concatenate(
        [ref[(GROUP * h + g) * HEAD : (GROUP * h + g + 1) * HEAD, :] for g in range(GROUP)], axis=1
    )


def allowed_at_home(rows, core):
    key = lax.broadcasted_iota(jnp.int32, (2 * rows, GROUP * rows), 0)
    query = lax.broadcasted_iota(jnp.int32, (2 * rows, GROUP * rows), 1) % rows
    return key <= jnp.where(key < rows, query, jnp.where(core == 1, 2 * rows, 0))


def present(ctx, k):
    x, z_hi = ctx // 4, (ctx // 2) % 2
    ring, pair = k // 2, k % 2
    return jnp.logical_and(x >= ring, jnp.logical_or(ring > 0, (z_hi + pair) % 2 < z_hi))


def keys_of(kv_s, k, h):
    return kv_s[k, h * HEAD : (h + 1) * HEAD, :]


def values_of(kv_s, k, h):
    return kv_s[k, KVWIDTH + h * HEAD : KVWIDTH + (h + 1) * HEAD, :]


def attend_kernel(ctx_ref, q_ref, *refs):
    blocks = refs[:16]
    out_ref, log_ref, kv_s, q_s, acc_s, max_s, sum_s = refs[16:]
    rows = q_ref.shape[1]
    ctx = ctx_ref[0]
    for k in range(8):
        kv_s[k, :, :rows] = blocks[2 * k][...]
        kv_s[k, :, rows:] = blocks[2 * k + 1][...]
    for h in range(KV_HEADS):
        q_s[h] = lanes_of_group(q_ref, h) * BF16(SCALE)

    allowed = allowed_at_home(rows, ctx % 2)
    for h in range(KV_HEADS):
        scores = jnp.where(allowed, contract(keys_of(kv_s, 0, h), q_s[h], 0, 0), MASK_VALUE)
        top = jnp.max(scores, axis=0, keepdims=True)
        weights = jnp.exp(scores - top)
        max_s[h] = top
        sum_s[h] = jnp.sum(weights, axis=0, keepdims=True)
        acc_s[h] = contract(values_of(kv_s, 0, h), weights.astype(BF16), 1, 0)

    def absorb(k):
        for h in range(KV_HEADS):
            scores = contract(keys_of(kv_s, k, h), q_s[h], 0, 0)
            old = max_s[h]
            top = jnp.maximum(old, jnp.max(scores, axis=0, keepdims=True))
            weights = jnp.exp(scores - top)
            factor = jnp.exp(old - top)
            max_s[h] = top
            sum_s[h] = sum_s[h] * factor + jnp.sum(weights, axis=0, keepdims=True)
            acc_s[h] = acc_s[h] * factor + contract(
                values_of(kv_s, k, h), weights.astype(BF16), 1, 0
            )

    def step(k, carry):
        pl.when(present(ctx, k))(functools.partial(absorb, k))
        return carry

    lax.fori_loop(1, 8, step, 0)
    for h in range(KV_HEADS):
        result = acc_s[h] / sum_s[h]
        logs = max_s[h] + jnp.log(sum_s[h])
        for g in range(GROUP):
            head = GROUP * h + g
            out_ref[head * HEAD : (head + 1) * HEAD, :] = result[:, g * rows : (g + 1) * rows]
            log_ref[head : head + 1, :] = logs[:, g * rows : (g + 1) * rows]


def attend(ctx, queries, blocks):
    rows = queries.shape[1]
    return pl.pallas_call(
        attend_kernel,
        out_shape=[
            jax.ShapeDtypeStruct((QWIDTH, rows), F32),
            jax.ShapeDtypeStruct((HEADS, rows), F32),
        ],
        in_specs=[pl.BlockSpec(memory_space=pltpu.SMEM)]
        + [pl.BlockSpec(memory_space=pltpu.VMEM)] * 17,
        out_specs=[pl.BlockSpec(memory_space=pltpu.VMEM)] * 2,
        scratch_shapes=[
            pltpu.VMEM((8, 2 * KVWIDTH, 2 * rows), BF16),
            pltpu.VMEM((KV_HEADS, HEAD, GROUP * rows), BF16),
            pltpu.VMEM((KV_HEADS, HEAD, GROUP * rows), F32),
            pltpu.VMEM((KV_HEADS, 1, GROUP * rows), F32),
            pltpu.VMEM((KV_HEADS, 1, GROUP * rows), F32),
        ],
        compiler_params=pltpu.CompilerParams(vmem_limit_bytes=VMEM_LIMIT),
        cost_estimate=pl.CostEstimate(
            flops=14000000000, bytes_accessed=5000000, transcendentals=4000000
        ),
        name="attend",
    )(ctx, queries, *blocks)


def attend_back_kernel(ctx_ref, q_ref, g_ref, out_ref, log_ref, *refs):
    blocks = refs[:16]
    gq_ref, ours_ref, theirs_ref, kv_s, q_s, g_s, gq_s, log_s, delta_s = refs[16:]
    rows = q_ref.shape[1]
    ctx = ctx_ref[0]
    for k in range(8):
        kv_s[k, :, :rows] = blocks[2 * k][...]
        kv_s[k, :, rows:] = blocks[2 * k + 1][...]
    for h in range(KV_HEADS):
        q_s[h] = lanes_of_group(q_ref, h) * BF16(SCALE)
        grads = lanes_of_group(g_ref, h)
        g_s[h] = grads
        delta_s[h] = jnp.sum(
            grads.astype(F32) * lanes_of_group(out_ref, h), axis=0, keepdims=True
        )
        log_s[h] = jnp.concatenate(
            [log_ref[GROUP * h + g : GROUP * h + g + 1, :] for g in range(GROUP)], axis=1
        )

    def absorb(k, h, allowed):
        keys = keys_of(kv_s, k, h)
        probs = jnp.exp(contract(keys, q_s[h], 0, 0) - log_s[h])
        if allowed is not None:
            probs = jnp.where(allowed, probs, 0.0)
        g_probs = contract(values_of(kv_s, k, h), g_s[h], 0, 0)
        g_scores = (probs * (g_probs - delta_s[h])).astype(BF16)
        g_keys = contract(q_s[h], g_scores, 1, 1).astype(BF16)
        g_values = contract(g_s[h], probs.astype(BF16), 1, 1).astype(BF16)
        for at, grads in ((h * HEAD, g_keys), (KVWIDTH + h * HEAD, g_values)):
            ours_ref[k, at : at + HEAD, :] = grads[:, :rows]
            theirs_ref[k, at : at + HEAD, :] = grads[:, rows:]
        return contract(keys, g_scores, 1, 0)

    allowed = allowed_at_home(rows, ctx % 2)
    for h in range(KV_HEADS):
        gq_s[h] = absorb(0, h, allowed)

    def step(k, carry):
        here = present(ctx, k)

        @pl.when(here)
        def _():
            for h in range(KV_HEADS):
                gq_s[h] += absorb(k, h, None)

        @pl.when(jnp.logical_not(here))
        def _():
            ours_ref[k] = jnp.zeros(ours_ref.shape[1:], BF16)
            theirs_ref[k] = jnp.zeros(theirs_ref.shape[1:], BF16)

        return carry

    lax.fori_loop(1, 8, step, 0)
    for h in range(KV_HEADS):
        result = gq_s[h] * SCALE
        for g in range(GROUP):
            head = GROUP * h + g
            gq_ref[head * HEAD : (head + 1) * HEAD, :] = result[:, g * rows : (g + 1) * rows]


def attend_back(ctx, queries, grads, result, logs, blocks):
    rows = queries.shape[1]
    half = jax.ShapeDtypeStruct((8, 2 * KVWIDTH, rows), BF16)
    wide = (KV_HEADS, HEAD, GROUP * rows)
    return pl.pallas_call(
        attend_back_kernel,
        out_shape=[jax.ShapeDtypeStruct((QWIDTH, rows), F32), half, half],
        in_specs=[pl.BlockSpec(memory_space=pltpu.SMEM)]
        + [pl.BlockSpec(memory_space=pltpu.VMEM)] * 20,
        out_specs=[pl.BlockSpec(memory_space=pltpu.VMEM)] * 3,
        scratch_shapes=[
            pltpu.VMEM((8, 2 * KVWIDTH, 2 * rows), BF16),
            pltpu.VMEM(wide, BF16),
            pltpu.VMEM(wide, BF16),
            pltpu.VMEM(wide, F32),
            pltpu.VMEM((KV_HEADS, 1, GROUP * rows), F32),
            pltpu.VMEM((KV_HEADS, 1, GROUP * rows), F32),
        ],
        compiler_params=pltpu.CompilerParams(vmem_limit_bytes=VMEM_LIMIT),
        cost_estimate=pl.CostEstimate(
            flops=18000000000, bytes_accessed=5000000, transcendentals=4000000
        ),
        name="attend_back",
    )(ctx, queries, grads, result, logs, *blocks)


def turn(heads, cosine, sine, sign):
    parts = heads.reshape(-1, 2, HEAD // 2, heads.shape[-1])
    first, second = parts[:, 0], parts[:, 1]
    sine = sign * sine
    return jnp.stack(
        [first * cosine - second * sine, second * cosine + first * sine], axis=1
    ).reshape(heads.shape)


def project_kernel(act_ref, qk_ref, ov_ref, cos_ref, sin_ref, q_ref, kv_ref, v_s, semaphore):
    start = QWIDTH // 128 * 128
    copy = pltpu.make_async_copy(ov_ref.at[:, start:], v_s, semaphore)
    copy.start()
    cosine, sine = cos_ref[...], sin_ref[...]
    half = HEAD // 2
    turned = contract(act_ref[...], qk_ref[...], 1, 0).T
    for head in range(HEADS + KV_HEADS):
        first = turned[head * HEAD : head * HEAD + half]
        second = turned[head * HEAD + half : (head + 1) * HEAD]
        goal = q_ref if head < HEADS else kv_ref
        at = (head if head < HEADS else head - HEADS) * HEAD
        goal[at : at + half] = (first * cosine - second * sine).astype(BF16)
        goal[at + half : at + HEAD] = (second * cosine + first * sine).astype(BF16)
    copy.wait()
    values = contract(act_ref[...], v_s[...], 1, 0).T
    kv_ref[KVWIDTH:] = values[QWIDTH - start :].astype(BF16)


def project(act, full_qk, full_ov, cosine, sine):
    rows = act.shape[0]
    spec = pl.BlockSpec(memory_space=pltpu.VMEM)
    tail = full_ov.shape[1] - QWIDTH // 128 * 128
    return pl.pallas_call(
        project_kernel,
        out_shape=[
            jax.ShapeDtypeStruct((QWIDTH, rows), BF16),
            jax.ShapeDtypeStruct((2 * KVWIDTH, rows), BF16),
        ],
        in_specs=[spec, spec, pl.BlockSpec(memory_space=pl.ANY), spec, spec],
        out_specs=[spec, spec],
        scratch_shapes=[pltpu.VMEM((full_ov.shape[0], tail), BF16), pltpu.SemaphoreType.DMA],
        compiler_params=pltpu.CompilerParams(vmem_limit_bytes=VMEM_LIMIT),
        name="project",
    )(act, full_qk, full_ov, cosine, sine)


def store_halves(core, mine_ref, other_ref, t, zero, one):
    @pl.when(core == 0)
    def _():
        mine_ref[t] = zero
        other_ref[t] = one

    @pl.when(core == 1)
    def _():
        mine_ref[t] = one
        other_ref[t] = zero


def halves_kernel(
    core_ref, act_ref, query_ref, attn_ref, hid_ref, kv_ref, gain_ref, mine_ref, other_ref
):
    split = WIDE_SPLIT
    for t in range(8):
        at = slice(t * 128, (t + 1) * 128)
        act = act_ref[:, at]
        query = contract(act, query_ref[...], 0, 1).astype(BF16)
        out = contract(attn_ref[at], hid_ref[...], 1, 0).astype(BF16)
        key = contract(act, kv_ref[:KVWIDTH], 0, 1)
        value = contract(act, kv_ref[KVWIDTH:], 0, 1).astype(BF16)
        gains = jnp.concatenate([jnp.zeros((120, 128), F32), gain_ref[t]], axis=0)
        key = jnp.concatenate([key[:, :128] + gains, key[:, 128:]], axis=1).astype(BF16)
        zero = jnp.concatenate([query[:, :split], out[:, split:], key], axis=1)
        one = jnp.concatenate([out[:, :split], query[:, split:], value], axis=1)
        store_halves(core_ref[0], mine_ref, other_ref, t, zero, one)


def halves(core, act, query, attn, hid, kv, gains):
    shape = jax.ShapeDtypeStruct((8, 128, QWIDTH + KVWIDTH), BF16)
    return pl.pallas_call(
        halves_kernel,
        out_shape=[shape, shape],
        in_specs=[pl.BlockSpec(memory_space=pltpu.SMEM)]
        + [pl.BlockSpec(memory_space=pltpu.VMEM)] * 6,
        out_specs=[pl.BlockSpec(memory_space=pltpu.VMEM)] * 2,
        compiler_params=pltpu.CompilerParams(vmem_limit_bytes=VMEM_LIMIT),
        name="halves",
    )(core, act, query, attn, hid, kv, gains)


def add_kernel(which_ref, mine_ref, other_ref, *outs):
    for r, out in enumerate(outs):
        at = which_ref[r]
        out[...] = (mine_ref[at].astype(F32) + other_ref[at].astype(F32)).astype(BF16)


def add_terms(mine, other, which):
    shape = jax.ShapeDtypeStruct(mine.shape[1:], BF16)
    return pl.pallas_call(
        add_kernel,
        out_shape=[shape] * 8,
        in_specs=[pl.BlockSpec(memory_space=pltpu.SMEM)]
        + [pl.BlockSpec(memory_space=pltpu.VMEM)] * 2,
        out_specs=[pl.BlockSpec(memory_space=pltpu.VMEM)] * 8,
        compiler_params=pltpu.CompilerParams(vmem_limit_bytes=VMEM_LIMIT),
        name="add_terms",
    )(which, mine, other)


def norm_back(grad, normed, inverse, gain):
    scaled = grad * gain
    mean = jnp.mean(scaled * normed, axis=-1, keepdims=True)
    return inverse * (scaled - normed * mean), jnp.sum(grad * normed, axis=0)


def body(
    tokens, norm_attn, w_query, w_key, w_value, w_out, norm_ffn, w_gate, w_up, w_down, cotangent
):
    rows, width = tokens.shape[1:]
    part = norm_attn.shape[0]
    ff_part = w_down.shape[0]
    ctx = lax.axis_index("ctx")
    me = lax.axis_index("fsdp")
    chip = ctx // 2
    first = ctx % 2 == 0
    inputs = tokens.reshape(rows, width).astype(F32)
    cot = cotangent.reshape(rows, width)
    ahead = [moved(me, "fsdp", *step) for step in STEPS]
    where = jnp.stack(ahead + [ctx % 2]).astype(jnp.int32)
    chips_ahead = [moved(chip, "fsdp", *step) for step in STEPS]
    chip_where = jnp.stack(chips_ahead).astype(jnp.int32)

    half = jnp.where(
        first,
        jnp.concatenate([w_query, w_key], axis=1),
        jnp.concatenate([w_out, w_value], axis=1),
    )
    columns = half.shape[1]
    gain_rows = jnp.zeros((128 - part, columns), BF16)
    gain_rows = gain_rows.at[0, :part].set(norm_attn).at[1, :part].set(norm_ffn)
    ours = gather_blocks(jnp.concatenate([half, gain_rows], axis=0), "fsdp")
    theirs = [core_swap(block) for block in ours]
    cot_late, _ = lax.optimization_barrier((cot, ours[7]))
    ff_parts = split_columns(w_gate, w_up, jnp.append(steps_from(me, -1), where[8]))
    full_qk, full_ov = place_pair(ours, theirs, where)
    gains = full_qk[:, part : part + 2, :part].astype(F32)
    gain_one = gains[:, 0].reshape(1, width)
    gain_two = gains[:, 1].reshape(1, width)
    full_qk = full_qk.reshape(1024, columns)
    full_ov = full_ov.reshape(1024, columns)

    inverse_one = lax.rsqrt(jnp.mean(inputs * inputs, axis=-1, keepdims=True) + EPSILON)
    normed_one = inputs * inverse_one
    act_one = spread((normed_one * gain_one).astype(BF16))
    inverse_freq = ROPE_BASE ** (-(jnp.arange(HEAD // 2, dtype=F32) * 2.0 / HEAD))
    positions = (ctx * rows + jnp.arange(rows, dtype=jnp.int32)).astype(F32)
    angles = inverse_freq[:, None] * positions[None, :]
    cosine, sine = jnp.cos(angles), jnp.sin(angles)
    queries, local_kv = project(act_one, full_qk, full_ov, cosine, sine)
    kv_blocks = gather_earlier(local_kv)
    ff_parts, kv_blocks[5] = lax.optimization_barrier((ff_parts, kv_blocks[5]))
    ff_ours = exchange_parts(ff_parts, "fsdp")
    blocks = []
    for block in kv_blocks:
        blocks += [block, core_swap(block)]
    blocks, ff_ours = lax.optimization_barrier((blocks, ff_ours))
    position = ctx.astype(jnp.int32).reshape(1)
    result, logs = attend(position, queries, blocks)
    attn = spread_rows(result.astype(BF16), part)
    hidden = inputs + contract(attn, full_ov, 0, 0)[:, :width]

    inverse_two = lax.rsqrt(jnp.mean(hidden * hidden, axis=-1, keepdims=True) + EPSILON)
    normed_two = hidden * inverse_two
    act_two = spread((normed_two * gain_two).astype(BF16))
    every = 8 * rows
    cot_all = lax.all_gather(spread(cot_late), "fsdp", axis=0, tiled=True)
    g_inner = contract(cot_all, spread(w_down), 1, 1)
    act_blocks = gather_blocks(act_two, "fsdp")
    ff_ours, _ = lax.optimization_barrier((ff_ours, act_blocks[2]))
    ff_ours = place(ff_ours, where).reshape(1024, ff_part)
    ff_theirs = core_swap(ff_ours)
    gate_cols = jnp.where(first, ff_ours, ff_theirs)
    up_cols = jnp.where(first, ff_theirs, ff_ours)
    act_all = place(act_blocks, where).reshape(every, 1024)
    gate = contract(act_all, gate_cols, 1, 0)
    up = contract(act_all, up_cols, 1, 0)
    sigmoid = jax.nn.sigmoid(gate)
    silu = gate * sigmoid
    inner = (silu * up).astype(BF16)
    g_gate = (g_inner * up * sigmoid * (1.0 + gate * (1.0 - sigmoid))).astype(BF16)
    g_up = (g_inner * silu).astype(BF16)
    g_act_part = contract(g_gate, gate_cols, 1, 1) + contract(g_up, up_cols, 1, 1)
    g_act_parts = deal(g_act_part.astype(BF16).reshape(8, rows, 1024), steps_from(me, 1))
    g_act_two = sum_unspread(reduce_terms(g_act_parts, "fsdp")[0], part)
    unit = ff_part // 2
    gate_mine = contract(act_all, jnp.where(first, g_gate, g_up), 0, 0)
    gate_other = contract(act_all, jnp.where(first, g_up, g_gate), 0, 0)
    down_mine = contract(cot_all, jnp.where(first, inner[:, :unit], inner[:, unit:]), 0, 0)
    down_other = contract(cot_all, jnp.where(first, inner[:, unit:], inner[:, :unit]), 0, 0)
    gate_other, down_other = core_swap(gate_other.astype(BF16)), core_swap(down_other.astype(BF16))
    ff_sum = jnp.concatenate(
        [gate_mine + gate_other.astype(F32), down_mine + down_other.astype(F32)], axis=1
    ).astype(BF16)

    g_normed, gain_two_term = norm_back(g_act_two, normed_two, inverse_two, gain_two)
    g_hidden = cot.astype(F32) + g_normed
    g_hid = g_hidden.astype(BF16)
    g_hid_wide = jnp.pad(g_hid, ((0, 0), (0, columns - width)))
    g_attn = unspread_rows(contract(full_ov, g_hid_wide, 1, 1).astype(BF16), part)

    pair_at = chip % 2
    ring = jnp.stack([(chip // 2 + r) % 4 for r in range(4)]).astype(jnp.int32)
    pair = jnp.stack([pair_at, 1 - pair_at]).astype(jnp.int32)
    ff_parts = deal(ff_sum.reshape(4, 2, 128, -1), ring)
    g_attn, ff_parts = lax.optimization_barrier((g_attn, ff_parts))
    ff_sum = ring_sum(ff_parts)
    down_part = contract(inner, w_down, 1, 0).astype(BF16)
    down_part, _ = lax.optimization_barrier((down_part, g_act_two))
    down = lax.psum_scatter(down_part, "fsdp", scatter_dimension=0, tiled=True)

    g_query_rot, g_ours, g_theirs = attend_back(position, queries, g_attn, result, logs, blocks)
    g_theirs = core_swap(g_theirs)
    g_pairs = g_ours.astype(F32) + g_theirs.astype(F32)
    g_query = turn(g_query_rot, cosine, sine, -1.0).astype(BF16)
    ff_sum, _ = lax.optimization_barrier((ff_sum, g_theirs))
    ff_sum = pair_gather(pair_sum(deal(ff_sum, pair)), pair)
    g_kv = reduce_earlier([g_pairs[k] for k in range(8)])
    g_kv, down, ff_sum = lax.optimization_barrier((g_kv, down, ff_sum))
    output = (hidden + down.astype(F32)).astype(BF16)
    g_key = turn(g_kv[:KVWIDTH], cosine, sine, -1.0).astype(BF16)
    g_value = g_kv[KVWIDTH:].astype(BF16)
    g_qk = jnp.concatenate([g_query, g_key], axis=0)
    g_ov = jnp.pad(g_value, ((width, 0), (0, 0)))
    g_act_one = contract(g_qk, full_qk, 0, 1) + contract(g_ov, full_ov, 0, 1)
    g_inputs, gain_one_term = norm_back(
        unspread(g_act_one, part), normed_one, inverse_one, gain_one
    )
    input_grad = (g_hidden + g_inputs).astype(BF16)

    core = (ctx % 2).astype(jnp.int32).reshape(1)
    gain_terms = jnp.stack(
        [gain_one_term.reshape(8, part), gain_two_term.reshape(8, part)], axis=1
    )
    gain_terms = jnp.pad(gain_terms, ((0, 0), (0, 6), (0, 128 - part)))
    g_kv = jnp.concatenate([g_key, g_value], axis=0)
    mine, other = halves(core, act_one, g_query, attn, g_hid, g_kv, gain_terms)
    terms = add_terms(mine, core_swap(other), steps_from(me, 1))
    row_sum, one, last = reduce_terms(terms, "fsdp")
    row_sum = sum_parts(row_sum).astype(BF16)

    sums = ring_sum(deal(row_sum.reshape(4, 2, 16, columns), ring))
    sums = pair_gather(pair_sum(deal(sums, pair)), pair)
    sums = place(ring_gather(sums), ring).reshape(128, columns)
    sums_other = core_swap(sums)
    sums_zero = jnp.where(first, sums, sums_other).astype(F32)
    sums_one = jnp.where(first, sums_other, sums).astype(F32)

    ff_sum, _ = lax.optimization_barrier((ff_sum, one))
    ff_sum, _ = lax.optimization_barrier((ring_gather(ff_sum), last))
    ff_sum = place(ff_sum, ring).reshape(1024, -1)
    gate_sum, down_sum = ff_sum[:, :ff_part], ff_sum[:, ff_part:]
    ff_rows = deal(gate_sum.reshape(8, 128, ff_part), steps_from(me, -1))
    ff_rows = place(exchange_parts(ff_rows, "fsdp"), where)
    ff_rows = ff_rows[:, :part].transpose(1, 0, 2).reshape(part, 8 * ff_part)
    ff_other = core_swap(ff_rows)
    grad_gate = jnp.where(first, ff_rows, ff_other).astype(F32)
    grad_up = jnp.where(first, ff_other, ff_rows).astype(F32)
    down_other = core_swap(down_sum)
    grad_down = jnp.concatenate(
        [jnp.where(first, down_sum, down_other), jnp.where(first, down_other, down_sum)], axis=1
    )
    grad_down = unspread_rows(grad_down, part).T.astype(F32)
    split = WIDE_SPLIT
    return (
        output[None],
        input_grad[None],
        sums_zero[part, width : width + part],
        jnp.concatenate([sums_zero[:part, :split], sums_one[:part, split:width]], axis=1),
        sums_zero[:part, width:],
        sums_one[:part, width:],
        jnp.concatenate([sums_one[:part, :split], sums_zero[:part, split:width]], axis=1),
        sums_zero[part + 1, width : width + part],
        grad_gate,
        grad_up,
        grad_down,
    )


def solution(mesh):
    rows = P("fsdp", None)
    tokens = P("fsdp", "ctx", None)
    in_specs = (
        tokens,
        P("fsdp"),
        rows,
        rows,
        rows,
        rows,
        P("fsdp"),
        rows,
        rows,
        rows,
        tokens,
    )
    out_specs = (
        tokens,
        tokens,
        P("fsdp"),
        rows,
        rows,
        rows,
        rows,
        P("fsdp"),
        rows,
        rows,
        rows,
    )
    return jax.shard_map(body, mesh=mesh, in_specs=in_specs, out_specs=out_specs, check_vma=False)
```

```python
import functools

import jax
import jax.numpy as jnp
from jax import lax
from jax.experimental import pallas as pl
from jax.experimental.pallas import tpu as pltpu
from jax.sharding import PartitionSpec as P

HEADS = 15
KV_HEADS = 5
GROUP = HEADS // KV_HEADS
HEAD = 64
QWIDTH = HEADS * HEAD
KVWIDTH = KV_HEADS * HEAD

EPSILON = 1e-05
ROPE_BASE = 10000.0
MASK_VALUE = -1e30
SCALE = HEAD ** (-0.5)

BF16 = jnp.bfloat16
F32 = jnp.float32
WIDE_SPLIT = 512
VMEM_LIMIT = 48 * 1024 * 1024
VMEM_LIMIT_ALONE = 60 * 1024 * 1024

STEPS = [(ring, pair) for ring in range(4) for pair in range(2)]


def moved(index, axis, ring, pair):
    low = 1 if axis == "fsdp" else 2
    core = index % low
    place = index // low
    place = ((place // 2 + ring) % 4) * 2 + (place % 2 + pair) % 2
    return place * low + core


def take(value, axis, ring, pair):
    size = 8 if axis == "fsdp" else 16
    return lax.ppermute(
        value, axis, [(i, moved(i, axis, -ring, pair)) for i in range(size)]
    )


def core_swap(value):
    return lax.ppermute(value, "ctx", [(i, i ^ 1) for i in range(16)])


def gather_blocks(value, axis):
    found = {(0, 0): value, (0, 1): take(value, axis, 0, 1)}
    found[1, 0] = take(value, axis, 1, 0)
    found[3, 0] = take(value, axis, 3, 0)
    found[1, 1] = take(found[0, 1], axis, 1, 0)
    found[3, 1] = take(found[0, 1], axis, 3, 0)
    found[2, 0] = take(found[1, 0], axis, 1, 0)
    found[2, 1] = take(found[3, 1], axis, 3, 0)
    return [found[step] for step in STEPS]


def steps_from(me, sign):
    return jnp.stack([moved(me, "fsdp", sign * ring, pair) for ring, pair in STEPS]).astype(
        jnp.int32
    )


def reduce_terms(terms, axis):
    term = dict(zip(STEPS, terms))

    def plus(first, *others):
        return sum((other.astype(F32) for other in others), first.astype(F32))

    one = plus(term[1, 0], take(term[2, 0], axis, 3, 0)).astype(BF16)
    three = plus(term[3, 1], take(term[2, 1], axis, 1, 0)).astype(BF16)
    pair = plus(term[0, 1], take(term[1, 1], axis, 3, 0), take(three, axis, 1, 0)).astype(BF16)
    last = [term[0, 0], take(term[3, 0], axis, 1, 0), take(one, axis, 3, 0), take(pair, axis, 0, 1)]
    return last, one, pair


def exchange_parts(parts, axis):
    return [parts[0]] + [take(part, axis, *step) for step, part in zip(STEPS[1:], parts[1:])]


def ring_sum(parts):
    return sum_parts(
        [parts[0]] + [take(parts[r], "ctx", 4 - r, 0) for r in range(1, 4)]
    ).astype(BF16)


def pair_sum(parts):
    return sum_parts([parts[0], take(parts[1], "ctx", 0, 1)]).astype(BF16)


def pair_gather(piece, pair):
    return place([piece, take(piece, "ctx", 0, 1)], pair)


def ring_gather(both):
    return [both] + [take(both, "ctx", r, 0) for r in range(1, 4)]


def sum_parts(parts):
    return sum((part.astype(F32) for part in parts[1:]), parts[0].astype(F32))


def later(value, ring):
    return take(value, "ctx", 4 - ring, 0)


def sooner(value, ring):
    return take(value, "ctx", ring, 0)


def gather_earlier(value):
    found = {(0, 0): value, (1, 0): later(value, 1)}
    found[0, 1] = take(value, "ctx", 0, 1)
    found[1, 1] = later(found[0, 1], 1)
    for p in range(2):
        found[3, p] = later(found[0, p], 3)
        found[2, p] = later(found[1, p], 1)
    return [found[step] for step in STEPS]


def reduce_earlier(terms):
    term = dict(zip(STEPS, terms))
    home = []
    for p in (1, 0):
        one = term[1, p] + sooner(term[2, p].astype(BF16), 1).astype(F32)
        total = term[0, p] + sooner(term[3, p].astype(BF16), 3).astype(F32)
        home.append(total + sooner(one.astype(BF16), 1).astype(F32))
    return home[1] + take(home[0].astype(BF16), "ctx", 0, 1).astype(F32)


def copy_all(pairs, semaphores):
    copies = [
        pltpu.make_async_copy(source, goal, semaphores.at[i])
        for i, (source, goal) in enumerate(pairs)
    ]
    for copy in copies:
        copy.start()
    for copy in copies:
        copy.wait()


def place_kernel(where_ref, *refs):
    blocks, out_ref, semaphores = refs[:-2], refs[-2], refs[-1]
    copy_all([(block, out_ref.at[where_ref[r]]) for r, block in enumerate(blocks)], semaphores)


def place(blocks, where, limit=VMEM_LIMIT):
    count, shape = len(blocks), blocks[0].shape
    return pl.pallas_call(
        place_kernel,
        out_shape=jax.ShapeDtypeStruct((count,) + shape, blocks[0].dtype),
        in_specs=[pl.BlockSpec(memory_space=pltpu.SMEM)]
        + [pl.BlockSpec(memory_space=pl.ANY)] * count,
        out_specs=pl.BlockSpec(memory_space=pltpu.VMEM),
        scratch_shapes=[pltpu.SemaphoreType.DMA((count,))],
        compiler_params=pltpu.CompilerParams(vmem_limit_bytes=limit),
        name="place",
    )(where, *blocks)


def deal_kernel(which_ref, source_ref, *refs):
    outs, semaphores = refs[:-1], refs[-1]
    copy_all([(source_ref.at[which_ref[r]], out) for r, out in enumerate(outs)], semaphores)


def deal(blocks, which):
    count = blocks.shape[0]
    shape = jax.ShapeDtypeStruct(blocks.shape[1:], blocks.dtype)
    return pl.pallas_call(
        deal_kernel,
        out_shape=[shape] * count,
        in_specs=[pl.BlockSpec(memory_space=pltpu.SMEM), pl.BlockSpec(memory_space=pl.ANY)],
        out_specs=[pl.BlockSpec(memory_space=pltpu.VMEM)] * count,
        scratch_shapes=[pltpu.SemaphoreType.DMA((count,))],
        compiler_params=pltpu.CompilerParams(vmem_limit_bytes=VMEM_LIMIT),
        name="deal",
    )(which, blocks)


def split_kernel(which_ref, gate_ref, up_ref, *refs):
    outs, blocks = refs[:8], refs[8]
    part, unit = gate_ref.shape[0], gate_ref.shape[1] // 8
    blocks[...] = jnp.zeros(blocks.shape, BF16)

    def lay(source):
        for t in range(8):
            blocks[t, :part] = source[:, t * unit : (t + 1) * unit]

    pl.when(which_ref[8] == 0)(lambda: lay(gate_ref))
    pl.when(which_ref[8] == 1)(lambda: lay(up_ref))
    for r, out in enumerate(outs):
        out[...] = blocks[which_ref[r]]


def split_columns(gate, up, which):
    shape = jax.ShapeDtypeStruct((128, gate.shape[1] // 8), BF16)
    return pl.pallas_call(
        split_kernel,
        out_shape=[shape] * 8,
        in_specs=[pl.BlockSpec(memory_space=pltpu.SMEM)]
        + [pl.BlockSpec(memory_space=pltpu.VMEM)] * 2,
        out_specs=[pl.BlockSpec(memory_space=pltpu.VMEM)] * 8,
        scratch_shapes=[pltpu.VMEM((8,) + shape.shape, BF16)],
        compiler_params=pltpu.CompilerParams(vmem_limit_bytes=VMEM_LIMIT),
        name="split_columns",
    )(which, gate, up)


def place_pair_kernel(where_ref, *refs):
    ours, theirs, zero_ref, one_ref, semaphores = refs[:8], refs[8:16], refs[16], refs[17], refs[18]

    def lay(zero, one):
        pairs = [(zero[r], zero_ref.at[where_ref[r]]) for r in range(8)]
        copy_all(pairs + [(one[r], one_ref.at[where_ref[r]]) for r in range(8)], semaphores)

    pl.when(where_ref[8] == 0)(lambda: lay(ours, theirs))
    pl.when(where_ref[8] == 1)(lambda: lay(theirs, ours))


def place_pair(ours, theirs, where):
    shape = (8,) + ours[0].shape
    return pl.pallas_call(
        place_pair_kernel,
        out_shape=[jax.ShapeDtypeStruct(shape, BF16)] * 2,
        in_specs=[pl.BlockSpec(memory_space=pltpu.SMEM)]
        + [pl.BlockSpec(memory_space=pl.ANY)] * 16,
        out_specs=[pl.BlockSpec(memory_space=pltpu.VMEM)] * 2,
        scratch_shapes=[pltpu.SemaphoreType.DMA((16,))],
        compiler_params=pltpu.CompilerParams(vmem_limit_bytes=VMEM_LIMIT),
        name="place_pair",
    )(where, *ours, *theirs)


def spread(value):
    rows = value.shape[0]
    groups = value.reshape(rows, 8, -1)
    return jnp.pad(groups, ((0, 0), (0, 0), (0, 128 - groups.shape[2]))).reshape(rows, 1024)


def unspread(value, part):
    rows = value.shape[0]
    return value.reshape(rows, 8, 128)[:, :, :part].reshape(rows, 8 * part)


def unspread_kernel(*refs):
    parts, out_ref = refs[:-1], refs[-1]
    part = out_ref.shape[1] // 8
    total = sum((ref[...].astype(F32) for ref in parts[1:]), parts[0][...].astype(F32))
    for t in range(8):
        out_ref[:, t * part : (t + 1) * part] = total[:, t * 128 : t * 128 + part]


def sum_unspread(parts, part):
    return pl.pallas_call(
        unspread_kernel,
        out_shape=jax.ShapeDtypeStruct((parts[0].shape[0], 8 * part), F32),
        in_specs=[pl.BlockSpec(memory_space=pltpu.VMEM)] * len(parts),
        out_specs=pl.BlockSpec(memory_space=pltpu.VMEM),
        compiler_params=pltpu.CompilerParams(vmem_limit_bytes=VMEM_LIMIT),
        name="sum_unspread",
    )(*parts)


def spread_rows(value, part):
    groups = value.reshape(8, part, -1)
    return jnp.pad(groups, ((0, 0), (0, 128 - part), (0, 0))).reshape(1024, -1)


def unspread_rows(value, part):
    return value.reshape(8, 128, -1)[:, :part].reshape(8 * part, -1)


def contract(left, right, left_dim, right_dim):
    return lax.dot_general(
        left, right, (((left_dim,), (right_dim,)), ((), ())), preferred_element_type=F32
    )


def lanes_of_group(ref, h):
    return jnp.concatenate(
        [ref[(GROUP * h + g) * HEAD : (GROUP * h + g + 1) * HEAD, :] for g in range(GROUP)], axis=1
    )


def allowed_at_home(rows, core):
    key = lax.broadcasted_iota(jnp.int32, (2 * rows, GROUP * rows), 0)
    query = lax.broadcasted_iota(jnp.int32, (2 * rows, GROUP * rows), 1) % rows
    return key <= jnp.where(key < rows, query, jnp.where(core == 1, 2 * rows, 0))


def present(ctx, k):
    x, z_hi = ctx // 4, (ctx // 2) % 2
    ring, pair = k // 2, k % 2
    return jnp.logical_and(x >= ring, jnp.logical_or(ring > 0, (z_hi + pair) % 2 < z_hi))


def keys_of(kv_s, k, h):
    return kv_s[k, h * HEAD : (h + 1) * HEAD, :]


def values_of(kv_s, k, h):
    return kv_s[k, KVWIDTH + h * HEAD : KVWIDTH + (h + 1) * HEAD, :]


def attend_kernel(ctx_ref, q_ref, *refs):
    blocks = refs[:16]
    out_ref, log_ref, kv_s, q_s, acc_s, max_s, sum_s = refs[16:]
    rows = q_ref.shape[1]
    ctx = ctx_ref[0]
    for k in range(8):
        kv_s[k, :, :rows] = blocks[2 * k][...]
        kv_s[k, :, rows:] = blocks[2 * k + 1][...]
    for h in range(KV_HEADS):
        q_s[h] = lanes_of_group(q_ref, h) * BF16(SCALE)

    allowed = allowed_at_home(rows, ctx % 2)
    for h in range(KV_HEADS):
        scores = jnp.where(allowed, contract(keys_of(kv_s, 0, h), q_s[h], 0, 0), MASK_VALUE)
        top = jnp.max(scores, axis=0, keepdims=True)
        weights = jnp.exp(scores - top)
        max_s[h] = top
        sum_s[h] = jnp.sum(weights, axis=0, keepdims=True)
        acc_s[h] = contract(values_of(kv_s, 0, h), weights.astype(BF16), 1, 0)

    def absorb(k):
        for h in range(KV_HEADS):
            scores = contract(keys_of(kv_s, k, h), q_s[h], 0, 0)
            old = max_s[h]
            top = jnp.maximum(old, jnp.max(scores, axis=0, keepdims=True))
            weights = jnp.exp(scores - top)
            factor = jnp.exp(old - top)
            max_s[h] = top
            sum_s[h] = sum_s[h] * factor + jnp.sum(weights, axis=0, keepdims=True)
            acc_s[h] = acc_s[h] * factor + contract(
                values_of(kv_s, k, h), weights.astype(BF16), 1, 0
            )

    def step(k, carry):
        pl.when(present(ctx, k))(functools.partial(absorb, k))
        return carry

    lax.fori_loop(1, 8, step, 0)
    for h in range(KV_HEADS):
        result = acc_s[h] / sum_s[h]
        logs = max_s[h] + jnp.log(sum_s[h])
        for g in range(GROUP):
            head = GROUP * h + g
            out_ref[head * HEAD : (head + 1) * HEAD, :] = result[:, g * rows : (g + 1) * rows]
            log_ref[head : head + 1, :] = logs[:, g * rows : (g + 1) * rows]


def attend(ctx, queries, blocks):
    rows = queries.shape[1]
    return pl.pallas_call(
        attend_kernel,
        out_shape=[
            jax.ShapeDtypeStruct((QWIDTH, rows), F32),
            jax.ShapeDtypeStruct((HEADS, rows), F32),
        ],
        in_specs=[pl.BlockSpec(memory_space=pltpu.SMEM)]
        + [pl.BlockSpec(memory_space=pltpu.VMEM)] * 17,
        out_specs=[pl.BlockSpec(memory_space=pltpu.VMEM)] * 2,
        scratch_shapes=[
            pltpu.VMEM((8, 2 * KVWIDTH, 2 * rows), BF16),
            pltpu.VMEM((KV_HEADS, HEAD, GROUP * rows), BF16),
            pltpu.VMEM((KV_HEADS, HEAD, GROUP * rows), F32),
            pltpu.VMEM((KV_HEADS, 1, GROUP * rows), F32),
            pltpu.VMEM((KV_HEADS, 1, GROUP * rows), F32),
        ],
        compiler_params=pltpu.CompilerParams(vmem_limit_bytes=VMEM_LIMIT_ALONE),
        cost_estimate=pl.CostEstimate(
            flops=14000000000, bytes_accessed=5000000, transcendentals=4000000
        ),
        name="attend",
    )(ctx, queries, *blocks)


def attend_back_kernel(ctx_ref, q_ref, g_ref, out_ref, log_ref, *refs):
    blocks = refs[:16]
    gq_ref, ours_ref, theirs_ref, kv_s, q_s, g_s, gq_s, log_s, delta_s = refs[16:]
    rows = q_ref.shape[1]
    ctx = ctx_ref[0]
    for k in range(8):
        kv_s[k, :, :rows] = blocks[2 * k][...]
        kv_s[k, :, rows:] = blocks[2 * k + 1][...]
    for h in range(KV_HEADS):
        q_s[h] = lanes_of_group(q_ref, h) * BF16(SCALE)
        grads = lanes_of_group(g_ref, h)
        g_s[h] = grads
        delta_s[h] = jnp.sum(
            grads.astype(F32) * lanes_of_group(out_ref, h), axis=0, keepdims=True
        )
        log_s[h] = jnp.concatenate(
            [log_ref[GROUP * h + g : GROUP * h + g + 1, :] for g in range(GROUP)], axis=1
        )

    def absorb(k, h, allowed):
        keys = keys_of(kv_s, k, h)
        probs = jnp.exp(contract(keys, q_s[h], 0, 0) - log_s[h])
        if allowed is not None:
            probs = jnp.where(allowed, probs, 0.0)
        g_probs = contract(values_of(kv_s, k, h), g_s[h], 0, 0)
        g_scores = (probs * (g_probs - delta_s[h])).astype(BF16)
        g_keys = contract(q_s[h], g_scores, 1, 1).astype(BF16)
        g_values = contract(g_s[h], probs.astype(BF16), 1, 1).astype(BF16)
        for at, grads in ((h * HEAD, g_keys), (KVWIDTH + h * HEAD, g_values)):
            ours_ref[k, at : at + HEAD, :] = grads[:, :rows]
            theirs_ref[k, at : at + HEAD, :] = grads[:, rows:]
        return contract(keys, g_scores, 1, 0)

    allowed = allowed_at_home(rows, ctx % 2)
    for h in range(KV_HEADS):
        gq_s[h] = absorb(0, h, allowed)

    def step(k, carry):
        here = present(ctx, k)

        @pl.when(here)
        def _():
            for h in range(KV_HEADS):
                gq_s[h] += absorb(k, h, None)

        @pl.when(jnp.logical_not(here))
        def _():
            ours_ref[k] = jnp.zeros(ours_ref.shape[1:], BF16)
            theirs_ref[k] = jnp.zeros(theirs_ref.shape[1:], BF16)

        return carry

    lax.fori_loop(1, 8, step, 0)
    for h in range(KV_HEADS):
        result = gq_s[h] * SCALE
        for g in range(GROUP):
            head = GROUP * h + g
            gq_ref[head * HEAD : (head + 1) * HEAD, :] = result[:, g * rows : (g + 1) * rows]


def attend_back(ctx, queries, grads, result, logs, blocks):
    rows = queries.shape[1]
    half = jax.ShapeDtypeStruct((8, 2 * KVWIDTH, rows), BF16)
    wide = (KV_HEADS, HEAD, GROUP * rows)
    return pl.pallas_call(
        attend_back_kernel,
        out_shape=[jax.ShapeDtypeStruct((QWIDTH, rows), F32), half, half],
        in_specs=[pl.BlockSpec(memory_space=pltpu.SMEM)]
        + [pl.BlockSpec(memory_space=pltpu.VMEM)] * 20,
        out_specs=[pl.BlockSpec(memory_space=pltpu.VMEM)] * 3,
        scratch_shapes=[
            pltpu.VMEM((8, 2 * KVWIDTH, 2 * rows), BF16),
            pltpu.VMEM(wide, BF16),
            pltpu.VMEM(wide, BF16),
            pltpu.VMEM(wide, F32),
            pltpu.VMEM((KV_HEADS, 1, GROUP * rows), F32),
            pltpu.VMEM((KV_HEADS, 1, GROUP * rows), F32),
        ],
        compiler_params=pltpu.CompilerParams(vmem_limit_bytes=VMEM_LIMIT_ALONE),
        cost_estimate=pl.CostEstimate(
            flops=18000000000, bytes_accessed=5000000, transcendentals=4000000
        ),
        name="attend_back",
    )(ctx, queries, grads, result, logs, *blocks)


def turn(heads, cosine, sine, sign):
    parts = heads.reshape(-1, 2, HEAD // 2, heads.shape[-1])
    first, second = parts[:, 0], parts[:, 1]
    sine = sign * sine
    return jnp.stack(
        [first * cosine - second * sine, second * cosine + first * sine], axis=1
    ).reshape(heads.shape)


def project_kernel(act_ref, qk_ref, ov_ref, cos_ref, sin_ref, q_ref, kv_ref, v_s, semaphore):
    start = QWIDTH // 128 * 128
    copy = pltpu.make_async_copy(ov_ref.at[:, start:], v_s, semaphore)
    copy.start()
    cosine, sine = cos_ref[...], sin_ref[...]
    half = HEAD // 2
    turned = contract(act_ref[...], qk_ref[...], 1, 0).T
    for head in range(HEADS + KV_HEADS):
        first = turned[head * HEAD : head * HEAD + half]
        second = turned[head * HEAD + half : (head + 1) * HEAD]
        goal = q_ref if head < HEADS else kv_ref
        at = (head if head < HEADS else head - HEADS) * HEAD
        goal[at : at + half] = (first * cosine - second * sine).astype(BF16)
        goal[at + half : at + HEAD] = (second * cosine + first * sine).astype(BF16)
    copy.wait()
    values = contract(act_ref[...], v_s[...], 1, 0).T
    kv_ref[KVWIDTH:] = values[QWIDTH - start :].astype(BF16)


def project(act, full_qk, full_ov, cosine, sine):
    rows = act.shape[0]
    spec = pl.BlockSpec(memory_space=pltpu.VMEM)
    tail = full_ov.shape[1] - QWIDTH // 128 * 128
    return pl.pallas_call(
        project_kernel,
        out_shape=[
            jax.ShapeDtypeStruct((QWIDTH, rows), BF16),
            jax.ShapeDtypeStruct((2 * KVWIDTH, rows), BF16),
        ],
        in_specs=[spec, spec, pl.BlockSpec(memory_space=pl.ANY), spec, spec],
        out_specs=[spec, spec],
        scratch_shapes=[pltpu.VMEM((full_ov.shape[0], tail), BF16), pltpu.SemaphoreType.DMA],
        compiler_params=pltpu.CompilerParams(vmem_limit_bytes=VMEM_LIMIT),
        name="project",
    )(act, full_qk, full_ov, cosine, sine)


def store_halves(core, mine_ref, other_ref, t, zero, one):
    @pl.when(core == 0)
    def _():
        mine_ref[t] = zero
        other_ref[t] = one

    @pl.when(core == 1)
    def _():
        mine_ref[t] = one
        other_ref[t] = zero


def halves_kernel(
    core_ref, act_ref, query_ref, attn_ref, hid_ref, kv_ref, gain_ref, mine_ref, other_ref
):
    split = WIDE_SPLIT
    for t in range(8):
        at = slice(t * 128, (t + 1) * 128)
        act = act_ref[:, at]
        query = contract(act, query_ref[...], 0, 1).astype(BF16)
        out = contract(attn_ref[at], hid_ref[...], 1, 0).astype(BF16)
        key = contract(act, kv_ref[:KVWIDTH], 0, 1)
        value = contract(act, kv_ref[KVWIDTH:], 0, 1).astype(BF16)
        gains = jnp.concatenate([jnp.zeros((120, 128), F32), gain_ref[t]], axis=0)
        key = jnp.concatenate([key[:, :128] + gains, key[:, 128:]], axis=1).astype(BF16)
        zero = jnp.concatenate([query[:, :split], out[:, split:], key], axis=1)
        one = jnp.concatenate([out[:, :split], query[:, split:], value], axis=1)
        store_halves(core_ref[0], mine_ref, other_ref, t, zero, one)


def halves(core, act, query, attn, hid, kv, gains):
    shape = jax.ShapeDtypeStruct((8, 128, QWIDTH + KVWIDTH), BF16)
    return pl.pallas_call(
        halves_kernel,
        out_shape=[shape, shape],
        in_specs=[pl.BlockSpec(memory_space=pltpu.SMEM)]
        + [pl.BlockSpec(memory_space=pltpu.VMEM)] * 6,
        out_specs=[pl.BlockSpec(memory_space=pltpu.VMEM)] * 2,
        compiler_params=pltpu.CompilerParams(vmem_limit_bytes=VMEM_LIMIT),
        name="halves",
    )(core, act, query, attn, hid, kv, gains)


def add_kernel(which_ref, mine_ref, other_ref, *outs):
    for r, out in enumerate(outs):
        at = which_ref[r]
        out[...] = (mine_ref[at].astype(F32) + other_ref[at].astype(F32)).astype(BF16)


def add_terms(mine, other, which):
    shape = jax.ShapeDtypeStruct(mine.shape[1:], BF16)
    return pl.pallas_call(
        add_kernel,
        out_shape=[shape] * 8,
        in_specs=[pl.BlockSpec(memory_space=pltpu.SMEM)]
        + [pl.BlockSpec(memory_space=pltpu.VMEM)] * 2,
        out_specs=[pl.BlockSpec(memory_space=pltpu.VMEM)] * 8,
        compiler_params=pltpu.CompilerParams(vmem_limit_bytes=VMEM_LIMIT),
        name="add_terms",
    )(which, mine, other)


def norm_back(grad, normed, inverse, gain):
    scaled = grad * gain
    mean = jnp.mean(scaled * normed, axis=-1, keepdims=True)
    return inverse * (scaled - normed * mean), jnp.sum(grad * normed, axis=0)


def body(
    tokens, norm_attn, w_query, w_key, w_value, w_out, norm_ffn, w_gate, w_up, w_down, cotangent
):
    rows, width = tokens.shape[1:]
    part = norm_attn.shape[0]
    ff_part = w_down.shape[0]
    ctx = lax.axis_index("ctx")
    me = lax.axis_index("fsdp")
    chip = ctx // 2
    first = ctx % 2 == 0
    inputs = tokens.reshape(rows, width).astype(F32)
    cot = cotangent.reshape(rows, width)
    ahead = [moved(me, "fsdp", *step) for step in STEPS]
    where = jnp.stack(ahead + [ctx % 2]).astype(jnp.int32)
    chips_ahead = [moved(chip, "fsdp", *step) for step in STEPS]
    chip_where = jnp.stack(chips_ahead).astype(jnp.int32)

    half = jnp.where(
        first,
        jnp.concatenate([w_query, w_key], axis=1),
        jnp.concatenate([w_out, w_value], axis=1),
    )
    columns = half.shape[1]
    gain_rows = jnp.zeros((128 - part, columns), BF16)
    gain_rows = gain_rows.at[0, :part].set(norm_attn).at[1, :part].set(norm_ffn)
    ours = gather_blocks(jnp.concatenate([half, gain_rows], axis=0), "fsdp")
    theirs = [core_swap(block) for block in ours]
    cot_late, _ = lax.optimization_barrier((cot, ours[7]))
    ff_parts = split_columns(w_gate, w_up, jnp.append(steps_from(me, -1), where[8]))
    full_qk, full_ov = place_pair(ours, theirs, where)
    gains = full_qk[:, part : part + 2, :part].astype(F32)
    gain_one = gains[:, 0].reshape(1, width)
    gain_two = gains[:, 1].reshape(1, width)
    full_qk = full_qk.reshape(1024, columns)
    full_ov = full_ov.reshape(1024, columns)

    inverse_one = lax.rsqrt(jnp.mean(inputs * inputs, axis=-1, keepdims=True) + EPSILON)
    normed_one = inputs * inverse_one
    act_one = spread((normed_one * gain_one).astype(BF16))
    inverse_freq = ROPE_BASE ** (-(jnp.arange(HEAD // 2, dtype=F32) * 2.0 / HEAD))
    positions = (ctx * rows + jnp.arange(rows, dtype=jnp.int32)).astype(F32)
    angles = inverse_freq[:, None] * positions[None, :]
    cosine, sine = jnp.cos(angles), jnp.sin(angles)
    queries, local_kv = project(act_one, full_qk, full_ov, cosine, sine)
    kv_blocks = gather_earlier(local_kv)
    ff_parts, kv_blocks[5] = lax.optimization_barrier((ff_parts, kv_blocks[5]))
    ff_ours = exchange_parts(ff_parts, "fsdp")
    blocks = []
    for block in kv_blocks:
        blocks += [block, core_swap(block)]
    blocks, ff_ours = lax.optimization_barrier((blocks, ff_ours))
    position = ctx.astype(jnp.int32).reshape(1)
    result, logs = attend(position, queries, blocks)
    attn = spread_rows(result.astype(BF16), part)
    hidden = inputs + contract(attn, full_ov, 0, 0)[:, :width]

    inverse_two = lax.rsqrt(jnp.mean(hidden * hidden, axis=-1, keepdims=True) + EPSILON)
    normed_two = hidden * inverse_two
    act_two = spread((normed_two * gain_two).astype(BF16))
    every = 8 * rows
    cot_all = lax.all_gather(spread(cot_late), "fsdp", axis=0, tiled=True)
    g_inner = contract(cot_all, spread(w_down), 1, 1)
    act_blocks = gather_blocks(act_two, "fsdp")
    ff_ours, _ = lax.optimization_barrier((ff_ours, act_blocks[2]))
    ff_ours = place(ff_ours, where, VMEM_LIMIT_ALONE).reshape(1024, ff_part)
    ff_theirs = core_swap(ff_ours)
    gate_cols = jnp.where(first, ff_ours, ff_theirs)
    up_cols = jnp.where(first, ff_theirs, ff_ours)
    act_all = place(act_blocks, where).reshape(every, 1024)
    gate = contract(act_all, gate_cols, 1, 0)
    up = contract(act_all, up_cols, 1, 0)
    sigmoid = jax.nn.sigmoid(gate)
    silu = gate * sigmoid
    inner = (silu * up).astype(BF16)
    g_gate = (g_inner * up * sigmoid * (1.0 + gate * (1.0 - sigmoid))).astype(BF16)
    g_up = (g_inner * silu).astype(BF16)
    g_act_part = contract(g_gate, gate_cols, 1, 1) + contract(g_up, up_cols, 1, 1)
    g_act_parts = deal(g_act_part.astype(BF16).reshape(8, rows, 1024), steps_from(me, 1))
    g_act_two = sum_unspread(reduce_terms(g_act_parts, "fsdp")[0], part)
    unit = ff_part // 2
    gate_mine = contract(act_all, jnp.where(first, g_gate, g_up), 0, 0)
    gate_other = contract(act_all, jnp.where(first, g_up, g_gate), 0, 0)
    down_mine = contract(cot_all, jnp.where(first, inner[:, :unit], inner[:, unit:]), 0, 0)
    down_other = contract(cot_all, jnp.where(first, inner[:, unit:], inner[:, :unit]), 0, 0)
    gate_other, down_other = core_swap(gate_other.astype(BF16)), core_swap(down_other.astype(BF16))
    ff_sum = jnp.concatenate(
        [gate_mine + gate_other.astype(F32), down_mine + down_other.astype(F32)], axis=1
    ).astype(BF16)

    g_normed, gain_two_term = norm_back(g_act_two, normed_two, inverse_two, gain_two)
    g_hidden = cot.astype(F32) + g_normed
    g_hid = g_hidden.astype(BF16)
    g_hid_wide = jnp.pad(g_hid, ((0, 0), (0, columns - width)))
    g_attn = unspread_rows(contract(full_ov, g_hid_wide, 1, 1).astype(BF16), part)

    pair_at = chip % 2
    ring = jnp.stack([(chip // 2 + r) % 4 for r in range(4)]).astype(jnp.int32)
    pair = jnp.stack([pair_at, 1 - pair_at]).astype(jnp.int32)
    ff_parts = deal(ff_sum.reshape(4, 2, 128, -1), ring)
    g_attn, ff_parts = lax.optimization_barrier((g_attn, ff_parts))
    ff_sum = ring_sum(ff_parts)
    down_part = contract(inner, w_down, 1, 0).astype(BF16)
    down_part, _ = lax.optimization_barrier((down_part, g_act_two))
    down = lax.psum_scatter(down_part, "fsdp", scatter_dimension=0, tiled=True)

    g_query_rot, g_ours, g_theirs = attend_back(position, queries, g_attn, result, logs, blocks)
    g_theirs = core_swap(g_theirs)
    g_pairs = g_ours.astype(F32) + g_theirs.astype(F32)
    g_query = turn(g_query_rot, cosine, sine, -1.0).astype(BF16)
    ff_sum, _ = lax.optimization_barrier((ff_sum, g_theirs))
    ff_sum = pair_gather(pair_sum(deal(ff_sum, pair)), pair)
    g_kv = reduce_earlier([g_pairs[k] for k in range(8)])
    g_kv, down, ff_sum = lax.optimization_barrier((g_kv, down, ff_sum))
    output = (hidden + down.astype(F32)).astype(BF16)
    g_key = turn(g_kv[:KVWIDTH], cosine, sine, -1.0).astype(BF16)
    g_value = g_kv[KVWIDTH:].astype(BF16)
    g_qk = jnp.concatenate([g_query, g_key], axis=0)
    g_ov = jnp.pad(g_value, ((width, 0), (0, 0)))
    g_act_one = contract(g_qk, full_qk, 0, 1) + contract(g_ov, full_ov, 0, 1)
    g_inputs, gain_one_term = norm_back(
        unspread(g_act_one, part), normed_one, inverse_one, gain_one
    )
    input_grad = (g_hidden + g_inputs).astype(BF16)

    core = (ctx % 2).astype(jnp.int32).reshape(1)
    gain_terms = jnp.stack(
        [gain_one_term.reshape(8, part), gain_two_term.reshape(8, part)], axis=1
    )
    gain_terms = jnp.pad(gain_terms, ((0, 0), (0, 6), (0, 128 - part)))
    g_kv = jnp.concatenate([g_key, g_value], axis=0)
    mine, other = halves(core, act_one, g_query, attn, g_hid, g_kv, gain_terms)
    terms = add_terms(mine, core_swap(other), steps_from(me, 1))
    row_sum, one, last = reduce_terms(terms, "fsdp")
    row_sum = sum_parts(row_sum).astype(BF16)

    sums = ring_sum(deal(row_sum.reshape(4, 2, 16, columns), ring))
    sums = pair_gather(pair_sum(deal(sums, pair)), pair)
    sums = place(ring_gather(sums), ring).reshape(128, columns)
    sums_other = core_swap(sums)
    sums_zero = jnp.where(first, sums, sums_other).astype(F32)
    sums_one = jnp.where(first, sums_other, sums).astype(F32)

    ff_sum, _ = lax.optimization_barrier((ff_sum, one))
    ff_sum, _ = lax.optimization_barrier((ring_gather(ff_sum), last))
    ff_sum = place(ff_sum, ring).reshape(1024, -1)
    gate_sum, down_sum = ff_sum[:, :ff_part], ff_sum[:, ff_part:]
    ff_rows = deal(gate_sum.reshape(8, 128, ff_part), steps_from(me, -1))
    ff_rows = place(exchange_parts(ff_rows, "fsdp"), where)
    ff_rows = ff_rows[:, :part].transpose(1, 0, 2).reshape(part, 8 * ff_part)
    ff_other = core_swap(ff_rows)
    grad_gate = jnp.where(first, ff_rows, ff_other).astype(F32)
    grad_up = jnp.where(first, ff_other, ff_rows).astype(F32)
    down_other = core_swap(down_sum)
    grad_down = jnp.concatenate(
        [jnp.where(first, down_sum, down_other), jnp.where(first, down_other, down_sum)], axis=1
    )
    grad_down = unspread_rows(grad_down, part).T.astype(F32)
    split = WIDE_SPLIT
    return (
        output[None],
        input_grad[None],
        sums_zero[part, width : width + part],
        jnp.concatenate([sums_zero[:part, :split], sums_one[:part, split:width]], axis=1),
        sums_zero[:part, width:],
        sums_one[:part, width:],
        jnp.concatenate([sums_one[:part, :split], sums_zero[:part, split:width]], axis=1),
        sums_zero[part + 1, width : width + part],
        grad_gate,
        grad_up,
        grad_down,
    )


def solution(mesh):
    rows = P("fsdp", None)
    tokens = P("fsdp", "ctx", None)
    in_specs = (
        tokens,
        P("fsdp"),
        rows,
        rows,
        rows,
        rows,
        P("fsdp"),
        rows,
        rows,
        rows,
        tokens,
    )
    out_specs = (
        tokens,
        tokens,
        P("fsdp"),
        rows,
        rows,
        rows,
        rows,
        P("fsdp"),
        rows,
        rows,
        rows,
    )
    return jax.shard_map(body, mesh=mesh, in_specs=in_specs, out_specs=out_specs, check_vma=False)
```

```python
import functools

import jax
import jax.numpy as jnp
from jax import lax
from jax.experimental import pallas as pl
from jax.experimental.pallas import tpu as pltpu
from jax.sharding import PartitionSpec as P

HEADS = 15
KV_HEADS = 5
GROUP = HEADS // KV_HEADS
HEAD = 64
QWIDTH = HEADS * HEAD
KVWIDTH = KV_HEADS * HEAD

EPSILON = 1e-05
ROPE_BASE = 10000.0
MASK_VALUE = -1e30
SCALE = HEAD ** (-0.5)

BF16 = jnp.bfloat16
F32 = jnp.float32
WIDE_SPLIT = 512
VMEM_LIMIT = 48 * 1024 * 1024
VMEM_LIMIT_ALONE = 60 * 1024 * 1024

STEPS = [(ring, pair) for ring in range(4) for pair in range(2)]


def moved(index, axis, ring, pair):
    low = 1 if axis == "fsdp" else 2
    core = index % low
    place = index // low
    place = ((place // 2 + ring) % 4) * 2 + (place % 2 + pair) % 2
    return place * low + core


def take(value, axis, ring, pair):
    size = 8 if axis == "fsdp" else 16
    return lax.ppermute(
        value, axis, [(i, moved(i, axis, -ring, pair)) for i in range(size)]
    )


def core_swap(value):
    return lax.ppermute(value, "ctx", [(i, i ^ 1) for i in range(16)])


def gather_blocks(value, axis):
    found = {(0, 0): value, (0, 1): take(value, axis, 0, 1)}
    found[1, 0] = take(value, axis, 1, 0)
    found[3, 0] = take(value, axis, 3, 0)
    found[1, 1] = take(found[0, 1], axis, 1, 0)
    found[3, 1] = take(found[0, 1], axis, 3, 0)
    found[2, 0] = take(found[1, 0], axis, 1, 0)
    found[2, 1] = take(found[3, 1], axis, 3, 0)
    return [found[step] for step in STEPS]


def steps_from(me, sign):
    return jnp.stack([moved(me, "fsdp", sign * ring, pair) for ring, pair in STEPS]).astype(
        jnp.int32
    )


def reduce_terms(terms, axis):
    term = dict(zip(STEPS, terms))

    def plus(first, *others):
        return sum((other.astype(F32) for other in others), first.astype(F32))

    one = plus(term[1, 0], take(term[2, 0], axis, 3, 0)).astype(BF16)
    three = plus(term[3, 1], take(term[2, 1], axis, 1, 0)).astype(BF16)
    pair = plus(term[0, 1], take(term[1, 1], axis, 3, 0), take(three, axis, 1, 0)).astype(BF16)
    last = [term[0, 0], take(term[3, 0], axis, 1, 0), take(one, axis, 3, 0), take(pair, axis, 0, 1)]
    return last, one, pair


def exchange_parts(parts, axis):
    return [parts[0]] + [take(part, axis, *step) for step, part in zip(STEPS[1:], parts[1:])]


def ring_sum(parts):
    return sum_parts(
        [parts[0]] + [take(parts[r], "ctx", 4 - r, 0) for r in range(1, 4)]
    ).astype(BF16)


def pair_sum(parts):
    return sum_parts([parts[0], take(parts[1], "ctx", 0, 1)]).astype(BF16)


def pair_gather(piece, pair):
    return place([piece, take(piece, "ctx", 0, 1)], pair)


def ring_gather(both):
    return [both] + [take(both, "ctx", r, 0) for r in range(1, 4)]


def sum_parts(parts):
    return sum((part.astype(F32) for part in parts[1:]), parts[0].astype(F32))


def later(value, ring):
    return take(value, "ctx", 4 - ring, 0)


def sooner(value, ring):
    return take(value, "ctx", ring, 0)


def gather_earlier(value):
    found = {(0, 0): value, (1, 0): later(value, 1)}
    found[0, 1] = take(value, "ctx", 0, 1)
    found[1, 1] = later(found[0, 1], 1)
    for p in range(2):
        found[3, p] = later(found[0, p], 3)
        found[2, p] = later(found[1, p], 1)
    return [found[step] for step in STEPS]


def reduce_earlier(terms):
    term = dict(zip(STEPS, terms))
    home = []
    for p in (1, 0):
        one = term[1, p] + sooner(term[2, p].astype(BF16), 1).astype(F32)
        total = term[0, p] + sooner(term[3, p].astype(BF16), 3).astype(F32)
        home.append(total + sooner(one.astype(BF16), 1).astype(F32))
    return home[1] + take(home[0].astype(BF16), "ctx", 0, 1).astype(F32)


def copy_all(pairs, semaphores):
    copies = [
        pltpu.make_async_copy(source, goal, semaphores.at[i])
        for i, (source, goal) in enumerate(pairs)
    ]
    for copy in copies:
        copy.start()
    for copy in copies:
        copy.wait()


def place_kernel(where_ref, *refs):
    blocks, out_ref, semaphores = refs[:-2], refs[-2], refs[-1]
    copy_all([(block, out_ref.at[where_ref[r]]) for r, block in enumerate(blocks)], semaphores)


def place(blocks, where, limit=VMEM_LIMIT):
    count, shape = len(blocks), blocks[0].shape
    return pl.pallas_call(
        place_kernel,
        out_shape=jax.ShapeDtypeStruct((count,) + shape, blocks[0].dtype),
        in_specs=[pl.BlockSpec(memory_space=pltpu.SMEM)]
        + [pl.BlockSpec(memory_space=pl.ANY)] * count,
        out_specs=pl.BlockSpec(memory_space=pltpu.VMEM),
        scratch_shapes=[pltpu.SemaphoreType.DMA((count,))],
        compiler_params=pltpu.CompilerParams(vmem_limit_bytes=limit),
        name="place",
    )(where, *blocks)


def deal_kernel(which_ref, source_ref, *refs):
    outs, semaphores = refs[:-1], refs[-1]
    copy_all([(source_ref.at[which_ref[r]], out) for r, out in enumerate(outs)], semaphores)


def deal(blocks, which):
    count = blocks.shape[0]
    shape = jax.ShapeDtypeStruct(blocks.shape[1:], blocks.dtype)
    return pl.pallas_call(
        deal_kernel,
        out_shape=[shape] * count,
        in_specs=[pl.BlockSpec(memory_space=pltpu.SMEM), pl.BlockSpec(memory_space=pl.ANY)],
        out_specs=[pl.BlockSpec(memory_space=pltpu.VMEM)] * count,
        scratch_shapes=[pltpu.SemaphoreType.DMA((count,))],
        compiler_params=pltpu.CompilerParams(vmem_limit_bytes=VMEM_LIMIT),
        name="deal",
    )(which, blocks)


def split_kernel(which_ref, gate_ref, up_ref, *refs):
    outs, blocks = refs[:8], refs[8]
    part, unit = gate_ref.shape[0], gate_ref.shape[1] // 8
    blocks[...] = jnp.zeros(blocks.shape, BF16)

    def lay(source):
        for t in range(8):
            blocks[t, :part] = source[:, t * unit : (t + 1) * unit]

    pl.when(which_ref[8] == 0)(lambda: lay(gate_ref))
    pl.when(which_ref[8] == 1)(lambda: lay(up_ref))
    for r, out in enumerate(outs):
        out[...] = blocks[which_ref[r]]


def split_columns(gate, up, which):
    shape = jax.ShapeDtypeStruct((128, gate.shape[1] // 8), BF16)
    return pl.pallas_call(
        split_kernel,
        out_shape=[shape] * 8,
        in_specs=[pl.BlockSpec(memory_space=pltpu.SMEM)]
        + [pl.BlockSpec(memory_space=pltpu.VMEM)] * 2,
        out_specs=[pl.BlockSpec(memory_space=pltpu.VMEM)] * 8,
        scratch_shapes=[pltpu.VMEM((8,) + shape.shape, BF16)],
        compiler_params=pltpu.CompilerParams(vmem_limit_bytes=VMEM_LIMIT),
        name="split_columns",
    )(which, gate, up)


def place_pair_kernel(where_ref, *refs):
    ours, theirs, zero_ref, one_ref, semaphores = refs[:8], refs[8:16], refs[16], refs[17], refs[18]

    def lay(zero, one):
        pairs = [(zero[r], zero_ref.at[where_ref[r]]) for r in range(8)]
        copy_all(pairs + [(one[r], one_ref.at[where_ref[r]]) for r in range(8)], semaphores)

    pl.when(where_ref[8] == 0)(lambda: lay(ours, theirs))
    pl.when(where_ref[8] == 1)(lambda: lay(theirs, ours))


def place_pair(ours, theirs, where):
    shape = (8,) + ours[0].shape
    return pl.pallas_call(
        place_pair_kernel,
        out_shape=[jax.ShapeDtypeStruct(shape, BF16)] * 2,
        in_specs=[pl.BlockSpec(memory_space=pltpu.SMEM)]
        + [pl.BlockSpec(memory_space=pl.ANY)] * 16,
        out_specs=[pl.BlockSpec(memory_space=pltpu.VMEM)] * 2,
        scratch_shapes=[pltpu.SemaphoreType.DMA((16,))],
        compiler_params=pltpu.CompilerParams(vmem_limit_bytes=VMEM_LIMIT),
        name="place_pair",
    )(where, *ours, *theirs)


def spread(value):
    rows = value.shape[0]
    groups = value.reshape(rows, 8, -1)
    return jnp.pad(groups, ((0, 0), (0, 0), (0, 128 - groups.shape[2]))).reshape(rows, 1024)


def unspread(value, part):
    rows = value.shape[0]
    return value.reshape(rows, 8, 128)[:, :, :part].reshape(rows, 8 * part)


def unspread_kernel(*refs):
    parts, out_ref = refs[:-1], refs[-1]
    part = out_ref.shape[1] // 8
    total = sum((ref[...].astype(F32) for ref in parts[1:]), parts[0][...].astype(F32))
    for t in range(8):
        out_ref[:, t * part : (t + 1) * part] = total[:, t * 128 : t * 128 + part]


def sum_unspread(parts, part):
    return pl.pallas_call(
        unspread_kernel,
        out_shape=jax.ShapeDtypeStruct((parts[0].shape[0], 8 * part), F32),
        in_specs=[pl.BlockSpec(memory_space=pltpu.VMEM)] * len(parts),
        out_specs=pl.BlockSpec(memory_space=pltpu.VMEM),
        compiler_params=pltpu.CompilerParams(vmem_limit_bytes=VMEM_LIMIT),
        name="sum_unspread",
    )(*parts)


def spread_rows(value, part):
    groups = value.reshape(8, part, -1)
    return jnp.pad(groups, ((0, 0), (0, 128 - part), (0, 0))).reshape(1024, -1)


def unspread_rows(value, part):
    return value.reshape(8, 128, -1)[:, :part].reshape(8 * part, -1)


def contract(left, right, left_dim, right_dim):
    return lax.dot_general(
        left, right, (((left_dim,), (right_dim,)), ((), ())), preferred_element_type=F32
    )


def lanes_of_group(ref, h):
    return jnp.concatenate(
        [ref[(GROUP * h + g) * HEAD : (GROUP * h + g + 1) * HEAD, :] for g in range(GROUP)], axis=1
    )


def allowed_at_home(rows, core):
    key = lax.broadcasted_iota(jnp.int32, (2 * rows, GROUP * rows), 0)
    query = lax.broadcasted_iota(jnp.int32, (2 * rows, GROUP * rows), 1) % rows
    return key <= jnp.where(key < rows, query, jnp.where(core == 1, 2 * rows, 0))


def present(ctx, k):
    x, z_hi = ctx // 4, (ctx // 2) % 2
    ring, pair = k // 2, k % 2
    return jnp.logical_and(x >= ring, jnp.logical_or(ring > 0, (z_hi + pair) % 2 < z_hi))


def keys_of(kv_s, k, h):
    return kv_s[k, h * HEAD : (h + 1) * HEAD, :]


def values_of(kv_s, k, h):
    return kv_s[k, KVWIDTH + h * HEAD : KVWIDTH + (h + 1) * HEAD, :]


def attend_kernel(ctx_ref, q_ref, *refs):
    blocks = refs[:16]
    out_ref, log_ref, kv_s, q_s, acc_s, max_s, sum_s = refs[16:]
    rows = q_ref.shape[1]
    ctx = ctx_ref[0]
    for k in range(8):
        kv_s[k, :, :rows] = blocks[2 * k][...]
        kv_s[k, :, rows:] = blocks[2 * k + 1][...]
    for h in range(KV_HEADS):
        q_s[h] = lanes_of_group(q_ref, h) * BF16(SCALE)

    allowed = allowed_at_home(rows, ctx % 2)
    for h in range(KV_HEADS):
        scores = jnp.where(allowed, contract(keys_of(kv_s, 0, h), q_s[h], 0, 0), MASK_VALUE)
        top = jnp.max(scores, axis=0, keepdims=True)
        weights = jnp.exp(scores - top)
        max_s[h] = top
        sum_s[h] = jnp.sum(weights, axis=0, keepdims=True)
        acc_s[h] = contract(values_of(kv_s, 0, h), weights.astype(BF16), 1, 0)

    def absorb(k):
        for h in range(KV_HEADS):
            scores = contract(keys_of(kv_s, k, h), q_s[h], 0, 0)
            old = max_s[h]
            top = jnp.maximum(old, jnp.max(scores, axis=0, keepdims=True))
            weights = jnp.exp(scores - top)
            factor = jnp.exp(old - top)
            max_s[h] = top
            sum_s[h] = sum_s[h] * factor + jnp.sum(weights, axis=0, keepdims=True)
            acc_s[h] = acc_s[h] * factor + contract(
                values_of(kv_s, k, h), weights.astype(BF16), 1, 0
            )

    def step(k, carry):
        pl.when(present(ctx, k))(functools.partial(absorb, k))
        return carry

    lax.fori_loop(1, 8, step, 0)
    for h in range(KV_HEADS):
        result = acc_s[h] / sum_s[h]
        logs = max_s[h] + jnp.log(sum_s[h])
        for g in range(GROUP):
            head = GROUP * h + g
            out_ref[head * HEAD : (head + 1) * HEAD, :] = result[:, g * rows : (g + 1) * rows]
            log_ref[head : head + 1, :] = logs[:, g * rows : (g + 1) * rows]


def attend(ctx, queries, blocks):
    rows = queries.shape[1]
    return pl.pallas_call(
        attend_kernel,
        out_shape=[
            jax.ShapeDtypeStruct((QWIDTH, rows), F32),
            jax.ShapeDtypeStruct((HEADS, rows), F32),
        ],
        in_specs=[pl.BlockSpec(memory_space=pltpu.SMEM)]
        + [pl.BlockSpec(memory_space=pltpu.VMEM)] * 17,
        out_specs=[pl.BlockSpec(memory_space=pltpu.VMEM)] * 2,
        scratch_shapes=[
            pltpu.VMEM((8, 2 * KVWIDTH, 2 * rows), BF16),
            pltpu.VMEM((KV_HEADS, HEAD, GROUP * rows), BF16),
            pltpu.VMEM((KV_HEADS, HEAD, GROUP * rows), F32),
            pltpu.VMEM((KV_HEADS, 1, GROUP * rows), F32),
            pltpu.VMEM((KV_HEADS, 1, GROUP * rows), F32),
        ],
        compiler_params=pltpu.CompilerParams(vmem_limit_bytes=VMEM_LIMIT_ALONE),
        cost_estimate=pl.CostEstimate(
            flops=14000000000, bytes_accessed=5000000, transcendentals=4000000
        ),
        name="attend",
    )(ctx, queries, *blocks)


def attend_back_kernel(ctx_ref, q_ref, g_ref, out_ref, log_ref, *refs):
    blocks = refs[:16]
    gq_ref, ours_ref, theirs_ref, kv_s, q_s, g_s, gq_s, log_s, delta_s = refs[16:]
    rows = q_ref.shape[1]
    ctx = ctx_ref[0]
    for k in range(8):
        kv_s[k, :, :rows] = blocks[2 * k][...]
        kv_s[k, :, rows:] = blocks[2 * k + 1][...]
    for h in range(KV_HEADS):
        q_s[h] = lanes_of_group(q_ref, h) * BF16(SCALE)
        grads = lanes_of_group(g_ref, h)
        g_s[h] = grads
        delta_s[h] = jnp.sum(
            grads.astype(F32) * lanes_of_group(out_ref, h), axis=0, keepdims=True
        )
        log_s[h] = jnp.concatenate(
            [log_ref[GROUP * h + g : GROUP * h + g + 1, :] for g in range(GROUP)], axis=1
        )

    def absorb(k, h, allowed):
        keys = keys_of(kv_s, k, h)
        probs = jnp.exp(contract(keys, q_s[h], 0, 0) - log_s[h])
        if allowed is not None:
            probs = jnp.where(allowed, probs, 0.0)
        g_probs = contract(values_of(kv_s, k, h), g_s[h], 0, 0)
        g_scores = (probs * (g_probs - delta_s[h])).astype(BF16)
        g_keys = contract(q_s[h], g_scores, 1, 1).astype(BF16)
        g_values = contract(g_s[h], probs.astype(BF16), 1, 1).astype(BF16)
        for at, grads in ((h * HEAD, g_keys), (KVWIDTH + h * HEAD, g_values)):
            ours_ref[k, at : at + HEAD, :] = grads[:, :rows]
            theirs_ref[k, at : at + HEAD, :] = grads[:, rows:]
        return contract(keys, g_scores, 1, 0)

    allowed = allowed_at_home(rows, ctx % 2)
    for h in range(KV_HEADS):
        gq_s[h] = absorb(0, h, allowed)

    def step(k, carry):
        here = present(ctx, k)

        @pl.when(here)
        def _():
            for h in range(KV_HEADS):
                gq_s[h] += absorb(k, h, None)

        @pl.when(jnp.logical_not(here))
        def _():
            ours_ref[k] = jnp.zeros(ours_ref.shape[1:], BF16)
            theirs_ref[k] = jnp.zeros(theirs_ref.shape[1:], BF16)

        return carry

    lax.fori_loop(1, 8, step, 0)
    for h in range(KV_HEADS):
        result = gq_s[h] * SCALE
        for g in range(GROUP):
            head = GROUP * h + g
            gq_ref[head * HEAD : (head + 1) * HEAD, :] = result[:, g * rows : (g + 1) * rows]


def attend_back(ctx, queries, grads, result, logs, blocks):
    rows = queries.shape[1]
    half = jax.ShapeDtypeStruct((8, 2 * KVWIDTH, rows), BF16)
    wide = (KV_HEADS, HEAD, GROUP * rows)
    return pl.pallas_call(
        attend_back_kernel,
        out_shape=[jax.ShapeDtypeStruct((QWIDTH, rows), F32), half, half],
        in_specs=[pl.BlockSpec(memory_space=pltpu.SMEM)]
        + [pl.BlockSpec(memory_space=pltpu.VMEM)] * 20,
        out_specs=[pl.BlockSpec(memory_space=pltpu.VMEM)] * 3,
        scratch_shapes=[
            pltpu.VMEM((8, 2 * KVWIDTH, 2 * rows), BF16),
            pltpu.VMEM(wide, BF16),
            pltpu.VMEM(wide, BF16),
            pltpu.VMEM(wide, F32),
            pltpu.VMEM((KV_HEADS, 1, GROUP * rows), F32),
            pltpu.VMEM((KV_HEADS, 1, GROUP * rows), F32),
        ],
        compiler_params=pltpu.CompilerParams(vmem_limit_bytes=VMEM_LIMIT_ALONE),
        cost_estimate=pl.CostEstimate(
            flops=18000000000, bytes_accessed=5000000, transcendentals=4000000
        ),
        name="attend_back",
    )(ctx, queries, grads, result, logs, *blocks)


def turn(heads, cosine, sine, sign):
    parts = heads.reshape(-1, 2, HEAD // 2, heads.shape[-1])
    first, second = parts[:, 0], parts[:, 1]
    sine = sign * sine
    return jnp.stack(
        [first * cosine - second * sine, second * cosine + first * sine], axis=1
    ).reshape(heads.shape)


def project_kernel(act_ref, qk_ref, ov_ref, cos_ref, sin_ref, q_ref, kv_ref, v_s, semaphore):
    start = QWIDTH // 128 * 128
    copy = pltpu.make_async_copy(ov_ref.at[:, start:], v_s, semaphore)
    copy.start()
    cosine, sine = cos_ref[...], sin_ref[...]
    half = HEAD // 2
    turned = contract(act_ref[...], qk_ref[...], 1, 0).T
    for head in range(HEADS + KV_HEADS):
        first = turned[head * HEAD : head * HEAD + half]
        second = turned[head * HEAD + half : (head + 1) * HEAD]
        goal = q_ref if head < HEADS else kv_ref
        at = (head if head < HEADS else head - HEADS) * HEAD
        goal[at : at + half] = (first * cosine - second * sine).astype(BF16)
        goal[at + half : at + HEAD] = (second * cosine + first * sine).astype(BF16)
    copy.wait()
    values = contract(act_ref[...], v_s[...], 1, 0).T
    kv_ref[KVWIDTH:] = values[QWIDTH - start :].astype(BF16)


def project(act, full_qk, full_ov, cosine, sine):
    rows = act.shape[0]
    spec = pl.BlockSpec(memory_space=pltpu.VMEM)
    tail = full_ov.shape[1] - QWIDTH // 128 * 128
    return pl.pallas_call(
        project_kernel,
        out_shape=[
            jax.ShapeDtypeStruct((QWIDTH, rows), BF16),
            jax.ShapeDtypeStruct((2 * KVWIDTH, rows), BF16),
        ],
        in_specs=[spec, spec, pl.BlockSpec(memory_space=pl.ANY), spec, spec],
        out_specs=[spec, spec],
        scratch_shapes=[pltpu.VMEM((full_ov.shape[0], tail), BF16), pltpu.SemaphoreType.DMA],
        compiler_params=pltpu.CompilerParams(vmem_limit_bytes=VMEM_LIMIT),
        name="project",
    )(act, full_qk, full_ov, cosine, sine)


def store_halves(core, mine_ref, other_ref, t, zero, one):
    @pl.when(core == 0)
    def _():
        mine_ref[t] = zero
        other_ref[t] = one

    @pl.when(core == 1)
    def _():
        mine_ref[t] = one
        other_ref[t] = zero


def halves_kernel(
    core_ref, act_ref, query_ref, attn_ref, hid_ref, kv_ref, gain_ref, mine_ref, other_ref
):
    split = WIDE_SPLIT
    for t in range(8):
        at = slice(t * 128, (t + 1) * 128)
        act = act_ref[:, at]
        query = contract(act, query_ref[...], 0, 1).astype(BF16)
        out = contract(attn_ref[at], hid_ref[...], 1, 0).astype(BF16)
        key = contract(act, kv_ref[:KVWIDTH], 0, 1)
        value = contract(act, kv_ref[KVWIDTH:], 0, 1).astype(BF16)
        gains = jnp.concatenate([jnp.zeros((120, 128), F32), gain_ref[t]], axis=0)
        key = jnp.concatenate([key[:, :128] + gains, key[:, 128:]], axis=1).astype(BF16)
        zero = jnp.concatenate([query[:, :split], out[:, split:], key], axis=1)
        one = jnp.concatenate([out[:, :split], query[:, split:], value], axis=1)
        store_halves(core_ref[0], mine_ref, other_ref, t, zero, one)


def halves(core, act, query, attn, hid, kv, gains):
    shape = jax.ShapeDtypeStruct((8, 128, QWIDTH + KVWIDTH), BF16)
    return pl.pallas_call(
        halves_kernel,
        out_shape=[shape, shape],
        in_specs=[pl.BlockSpec(memory_space=pltpu.SMEM)]
        + [pl.BlockSpec(memory_space=pltpu.VMEM)] * 6,
        out_specs=[pl.BlockSpec(memory_space=pltpu.VMEM)] * 2,
        compiler_params=pltpu.CompilerParams(vmem_limit_bytes=VMEM_LIMIT),
        name="halves",
    )(core, act, query, attn, hid, kv, gains)


def add_kernel(which_ref, mine_ref, other_ref, *outs):
    for r, out in enumerate(outs):
        at = which_ref[r]
        out[...] = (mine_ref[at].astype(F32) + other_ref[at].astype(F32)).astype(BF16)


def add_terms(mine, other, which):
    shape = jax.ShapeDtypeStruct(mine.shape[1:], BF16)
    return pl.pallas_call(
        add_kernel,
        out_shape=[shape] * 8,
        in_specs=[pl.BlockSpec(memory_space=pltpu.SMEM)]
        + [pl.BlockSpec(memory_space=pltpu.VMEM)] * 2,
        out_specs=[pl.BlockSpec(memory_space=pltpu.VMEM)] * 8,
        compiler_params=pltpu.CompilerParams(vmem_limit_bytes=VMEM_LIMIT),
        name="add_terms",
    )(which, mine, other)


def norm_back(grad, normed, inverse, gain):
    scaled = grad * gain
    mean = jnp.mean(scaled * normed, axis=-1, keepdims=True)
    return inverse * (scaled - normed * mean), jnp.sum(grad * normed, axis=0)


def body(
    tokens, norm_attn, w_query, w_key, w_value, w_out, norm_ffn, w_gate, w_up, w_down, cotangent
):
    rows, width = tokens.shape[1:]
    part = norm_attn.shape[0]
    ff_part = w_down.shape[0]
    ctx = lax.axis_index("ctx")
    me = lax.axis_index("fsdp")
    chip = ctx // 2
    first = ctx % 2 == 0
    inputs = tokens.reshape(rows, width).astype(F32)
    cot = cotangent.reshape(rows, width)
    ahead = [moved(me, "fsdp", *step) for step in STEPS]
    where = jnp.stack(ahead + [ctx % 2]).astype(jnp.int32)
    chips_ahead = [moved(chip, "fsdp", *step) for step in STEPS]
    chip_where = jnp.stack(chips_ahead).astype(jnp.int32)

    half = jnp.where(
        first,
        jnp.concatenate([w_query, w_key], axis=1),
        jnp.concatenate([w_out, w_value], axis=1),
    )
    columns = half.shape[1]
    gain_rows = jnp.zeros((128 - part, columns), BF16)
    gain_rows = gain_rows.at[0, :part].set(norm_attn).at[1, :part].set(norm_ffn)
    ours = gather_blocks(jnp.concatenate([half, gain_rows], axis=0), "fsdp")
    theirs = [core_swap(block) for block in ours]
    cot_late, _ = lax.optimization_barrier((cot, ours[7]))
    ff_parts = split_columns(w_gate, w_up, jnp.append(steps_from(me, -1), where[8]))
    full_qk, full_ov = place_pair(ours, theirs, where)
    gains = full_qk[:, part : part + 2, :part].astype(F32)
    gain_one = gains[:, 0].reshape(1, width)
    gain_two = gains[:, 1].reshape(1, width)
    full_qk = full_qk.reshape(1024, columns)
    full_ov = full_ov.reshape(1024, columns)

    inverse_one = lax.rsqrt(jnp.mean(inputs * inputs, axis=-1, keepdims=True) + EPSILON)
    normed_one = inputs * inverse_one
    act_one = spread((normed_one * gain_one).astype(BF16))
    inverse_freq = ROPE_BASE ** (-(jnp.arange(HEAD // 2, dtype=F32) * 2.0 / HEAD))
    positions = (ctx * rows + jnp.arange(rows, dtype=jnp.int32)).astype(F32)
    angles = inverse_freq[:, None] * positions[None, :]
    cosine, sine = jnp.cos(angles), jnp.sin(angles)
    queries, local_kv = project(act_one, full_qk, full_ov, cosine, sine)
    kv_blocks = gather_earlier(local_kv)
    ff_parts, kv_blocks[5] = lax.optimization_barrier((ff_parts, kv_blocks[5]))
    ff_ours = exchange_parts(ff_parts, "fsdp")
    blocks = []
    for block in kv_blocks:
        blocks += [block, core_swap(block)]
    blocks, ff_ours = lax.optimization_barrier((blocks, ff_ours))
    position = ctx.astype(jnp.int32).reshape(1)
    result, logs = attend(position, queries, blocks)
    attn = spread_rows(result.astype(BF16), part)
    hidden = inputs + contract(attn, full_ov, 0, 0)[:, :width]

    inverse_two = lax.rsqrt(jnp.mean(hidden * hidden, axis=-1, keepdims=True) + EPSILON)
    normed_two = hidden * inverse_two
    act_two = spread((normed_two * gain_two).astype(BF16))
    every = 8 * rows
    cot_all = lax.all_gather(spread(cot_late), "fsdp", axis=0, tiled=True)
    g_inner = contract(cot_all, spread(w_down), 1, 1)
    act_blocks = gather_blocks(act_two, "fsdp")
    ff_ours, _ = lax.optimization_barrier((ff_ours, act_blocks[2]))
    ff_ours = place(ff_ours, where, VMEM_LIMIT_ALONE).reshape(1024, ff_part)
    ff_theirs = core_swap(ff_ours)
    gate_cols = jnp.where(first, ff_ours, ff_theirs)
    up_cols = jnp.where(first, ff_theirs, ff_ours)
    act_all = place(act_blocks, where).reshape(every, 1024)
    gate = contract(act_all, gate_cols, 1, 0)
    up = contract(act_all, up_cols, 1, 0)
    sigmoid = jax.nn.sigmoid(gate)
    silu = gate * sigmoid
    inner = (silu * up).astype(BF16)
    g_gate = (g_inner * up * sigmoid * (1.0 + gate * (1.0 - sigmoid))).astype(BF16)
    g_up = (g_inner * silu).astype(BF16)
    g_act_part = contract(g_gate, gate_cols, 1, 1) + contract(g_up, up_cols, 1, 1)
    g_act_parts = deal(g_act_part.astype(BF16).reshape(8, rows, 1024), steps_from(me, 1))
    g_act_two = sum_unspread(reduce_terms(g_act_parts, "fsdp")[0], part)
    unit = ff_part // 2
    gate_mine = contract(act_all, jnp.where(first, g_gate, g_up), 0, 0)
    gate_other = contract(act_all, jnp.where(first, g_up, g_gate), 0, 0)
    down_mine = contract(cot_all, jnp.where(first, inner[:, :unit], inner[:, unit:]), 0, 0)
    down_other = contract(cot_all, jnp.where(first, inner[:, unit:], inner[:, :unit]), 0, 0)
    gate_other, down_other = core_swap(gate_other.astype(BF16)), core_swap(down_other.astype(BF16))
    ff_sum = jnp.concatenate(
        [gate_mine + gate_other.astype(F32), down_mine + down_other.astype(F32)], axis=1
    ).astype(BF16)

    g_normed, gain_two_term = norm_back(g_act_two, normed_two, inverse_two, gain_two)
    g_hidden = cot.astype(F32) + g_normed
    g_hid = g_hidden.astype(BF16)
    g_hid_wide = jnp.pad(g_hid, ((0, 0), (0, columns - width)))
    g_attn = unspread_rows(contract(full_ov, g_hid_wide, 1, 1).astype(BF16), part)

    pair_at = chip % 2
    ring = jnp.stack([(chip // 2 + r) % 4 for r in range(4)]).astype(jnp.int32)
    pair = jnp.stack([pair_at, 1 - pair_at]).astype(jnp.int32)
    ff_parts = deal(ff_sum.reshape(4, 2, 128, -1), ring)
    g_attn, ff_parts = lax.optimization_barrier((g_attn, ff_parts))
    ff_sum = ring_sum(ff_parts)
    down_part = contract(inner, w_down, 1, 0).astype(BF16)
    down_part, _ = lax.optimization_barrier((down_part, g_act_two))
    down = lax.psum_scatter(down_part, "fsdp", scatter_dimension=0, tiled=True)

    g_query_rot, g_ours, g_theirs = attend_back(position, queries, g_attn, result, logs, blocks)
    g_theirs = core_swap(g_theirs)
    g_pairs = g_ours.astype(F32) + g_theirs.astype(F32)
    g_query = turn(g_query_rot, cosine, sine, -1.0).astype(BF16)
    ff_sum, _ = lax.optimization_barrier((ff_sum, g_theirs))
    ff_sum = pair_gather(pair_sum(deal(ff_sum, pair)), pair)
    g_kv = reduce_earlier([g_pairs[k] for k in range(8)])
    g_kv, down, ff_sum = lax.optimization_barrier((g_kv, down, ff_sum))
    output = (hidden + down.astype(F32)).astype(BF16)
    g_key = turn(g_kv[:KVWIDTH], cosine, sine, -1.0).astype(BF16)
    g_value = g_kv[KVWIDTH:].astype(BF16)
    g_qk = jnp.concatenate([g_query, g_key], axis=0)
    g_ov = jnp.pad(g_value, ((width, 0), (0, 0)))
    g_act_one = contract(g_qk, full_qk, 0, 1) + contract(g_ov, full_ov, 0, 1)
    g_inputs, gain_one_term = norm_back(
        unspread(g_act_one, part), normed_one, inverse_one, gain_one
    )
    input_grad = (g_hidden + g_inputs).astype(BF16)

    core = (ctx % 2).astype(jnp.int32).reshape(1)
    gain_terms = jnp.stack(
        [gain_one_term.reshape(8, part), gain_two_term.reshape(8, part)], axis=1
    )
    gain_terms = jnp.pad(gain_terms, ((0, 0), (0, 6), (0, 128 - part)))
    g_kv = jnp.concatenate([g_key, g_value], axis=0)
    mine, other = halves(core, act_one, g_query, attn, g_hid, g_kv, gain_terms)
    terms = add_terms(mine, core_swap(other), steps_from(me, 1))
    row_sum, one, last = reduce_terms(terms, "fsdp")
    row_sum = sum_parts(row_sum).astype(BF16)

    sums = ring_sum(deal(row_sum.reshape(4, 2, 16, columns), ring))
    sums = pair_gather(pair_sum(deal(sums, pair)), pair)
    sums = place(ring_gather(sums), ring).reshape(128, columns)
    sums_other = core_swap(sums)
    sums_zero = jnp.where(first, sums, sums_other).astype(F32)
    sums_one = jnp.where(first, sums_other, sums).astype(F32)

    ff_sum, _ = lax.optimization_barrier((ff_sum, one))
    ff_sum, _ = lax.optimization_barrier((ring_gather(ff_sum), last))
    ff_sum = place(ff_sum, ring).reshape(1024, -1)
    ff_sum, _ = lax.optimization_barrier((ff_sum, row_sum))
    gate_sum, down_sum = ff_sum[:, :ff_part], ff_sum[:, ff_part:]
    ff_rows = deal(gate_sum.reshape(8, 128, ff_part), steps_from(me, -1))
    ff_rows = place(exchange_parts(ff_rows, "fsdp"), where)
    ff_rows = ff_rows[:, :part].transpose(1, 0, 2).reshape(part, 8 * ff_part)
    ff_other = core_swap(ff_rows)
    grad_gate = jnp.where(first, ff_rows, ff_other).astype(F32)
    grad_up = jnp.where(first, ff_other, ff_rows).astype(F32)
    down_other = core_swap(down_sum)
    grad_down = jnp.concatenate(
        [jnp.where(first, down_sum, down_other), jnp.where(first, down_other, down_sum)], axis=1
    )
    grad_down = unspread_rows(grad_down, part).T.astype(F32)
    split = WIDE_SPLIT
    return (
        output[None],
        input_grad[None],
        sums_zero[part, width : width + part],
        jnp.concatenate([sums_zero[:part, :split], sums_one[:part, split:width]], axis=1),
        sums_zero[:part, width:],
        sums_one[:part, width:],
        jnp.concatenate([sums_one[:part, :split], sums_zero[:part, split:width]], axis=1),
        sums_zero[part + 1, width : width + part],
        grad_gate,
        grad_up,
        grad_down,
    )


def solution(mesh):
    rows = P("fsdp", None)
    tokens = P("fsdp", "ctx", None)
    in_specs = (
        tokens,
        P("fsdp"),
        rows,
        rows,
        rows,
        rows,
        P("fsdp"),
        rows,
        rows,
        rows,
        tokens,
    )
    out_specs = (
        tokens,
        tokens,
        P("fsdp"),
        rows,
        rows,
        rows,
        rows,
        P("fsdp"),
        rows,
        rows,
        rows,
    )
    return jax.shard_map(body, mesh=mesh, in_specs=in_specs, out_specs=out_specs, check_vma=False)
```
